512 devices in a mesh: lon: 128 (over x_lo, y, z), lat: 4 (over x_hi, core).
Axes of the slice: x: 4 (x_hi: 2, x_lo: 2; x = x_hi * 2 + x_lo), y: 4, z: 16, core: 2. Of those that a mesh axis runs over, the one named last changes fastest.
Arguments:
- y_block: bfloat16 [2, 24, 1536, 768], P(None, 'lat', 'lon'), may hold values from -6 to 6
- merge_gain: float32 [3072], replicated, may hold values from 0.25 to 1.75
- merge_weight: bfloat16 [3072, 1536], P('lon'), may hold values from -0.109375 to 0.109375
- d_merged: bfloat16 [2, 12, 768, 1536], P(None, 'lat', 'lon'), may hold values from -6 to 6
- q_proj: bfloat16 [2, 24, 1536, 768], P(None, 'lat', 'lon'), may hold values from -8 to 8
- k_proj: bfloat16 [2, 24, 1536, 768], P(None, 'lat', 'lon'), may hold values from -8 to 8
- v_proj: bfloat16 [2, 24, 1536, 768], P(None, 'lat', 'lon'), may hold values from -6 to 6
- bias_table: float32 [4, 24, 3312], P('lat'), may hold values from -5 to 5
Outputs:
- q_grad: bfloat16 [2, 24, 1536, 768], P(None, 'lat', 'lon')
- k_grad: bfloat16 [2, 24, 1536, 768], P(None, 'lat', 'lon')
- v_grad: bfloat16 [2, 24, 1536, 768], P(None, 'lat', 'lon')
- table_grad: float32 [4, 24, 3312], P('lat')
The draws below stay inside these ranges and needn't reach their ends.
All inputs are finite; a program needn't handle non-finite values.
Results may differ from the reference program's by a relative error of at most 0.011.
Values may be sent and summed in bfloat16 or wider, within the bound.
No kernel may reach another device: no remote copies, remote signals or barrier semaphores. Data moves between devices by JAX's collectives and lax.ppermute only.
A program may use at most 128 MiB of HBM per device.

```python
import jax
import jax.numpy as jnp
from jax import lax

H = 24
C = 768
Z = 2
POS = 3312
LAT = 24
LON = 1536
TYPES = 4


def draw_q_proj(key, part):
    key = jax.random.fold_in(key, 5)
    key_base = jax.random.fold_in(key, 0)
    values = jnp.clip(jax.random.normal(key_base, (Z, LAT, LON, C), jnp.float32), -6.0, 6.0)
    return values.astype(jnp.bfloat16)


def draw_k_proj(key, part):
    key = jax.random.fold_in(key, 9)
    key_base = jax.random.fold_in(key, 0)
    values = jnp.clip(jax.random.normal(key_base, (Z, LAT, LON, C), jnp.float32), -6.0, 6.0)
    return values.astype(jnp.bfloat16)


def block_levels(own_key, shape, cuts, smallest, top_value):
    factor_of = 1.0
    for dim, blocks in cuts:
        draws = jax.random.uniform(jax.random.fold_in(jax.random.fold_in(own_key, 6), dim), (blocks,), jnp.float32, smallest / len(cuts), top_value / len(cuts))
        factor_of = factor_of * jnp.repeat(jnp.exp(draws), shape[dim] // blocks).reshape((-1,) + (1,) * (len(shape) - 1 - dim))
    return factor_of


def scatter_about(rng, shape, deviation, most, cuts=(), kind=jnp.bfloat16):
    level = block_levels(rng, shape, cuts, -0.22, 0.18) if cuts else 1.0
    result = jax.random.normal(rng, shape, jnp.float32) * deviation * level
    return jnp.minimum(jnp.maximum(result, -most), most).astype(kind)


def setup_inputs(seed: int = 0) -> dict:
    seeds = jax.random.split(jax.random.key(seed), 9)
    return {
        "y_block": scatter_about(seeds[0], (Z, LAT, LON, C), 1.0, 6.0, ((1, 4), (2, 128))),
        "merge_gain": jnp.clip(1.0 + 0.15 * jax.random.normal(seeds[1], (4 * C,), jnp.float32), 0.25, 1.75),
        "merge_weight": scatter_about(seeds[2], (4 * C, 2 * C), (4 * C) ** -0.5, 0.109375, ((0, 128),)),
        "d_merged": scatter_about(seeds[3], (Z, LAT // 2, LON // 2, 2 * C), 1.0, 6.0, ((1, 4), (2, 128))),
        "q_proj": draw_q_proj(jax.random.fold_in(seeds[8], 71), 0),
        "k_proj": draw_k_proj(jax.random.fold_in(seeds[8], 71), 0),
        "v_proj": scatter_about(seeds[6], (Z, LAT, LON, C), 1.0, 6.0, ((1, 4), (2, 128))),
        "bias_table": scatter_about(seeds[7], (TYPES, H, POS), 1.0, 5.0, ((0, 4),), jnp.float32),
    }


score_factor = 32 ** (-0.5)

def window_positions():
    tokens = jnp.arange(144, dtype=jnp.int32)
    level = tokens // 72
    row_in = tokens // 12 % 6
    column = tokens % 12
    index = ((level[:, None] * 2 + level[None, :]) * 36 + row_in[:, None] * 6 + row_in[None, :]) * 23 + column[:, None] - column[None, :] + 11
    return (index.reshape(-1).astype(jnp.int32), row_in)

def window_grads(q_win, k_win, v_win, o_win, bias, allowed):
    batch, count, width = q_win.shape
    heads = width // 32
    shape_four = (batch, count, heads, 32)
    q_heads = q_win.reshape(shape_four).astype(jnp.float32)
    k_heads = k_win.reshape(shape_four).astype(jnp.float32)
    v_heads = v_win.reshape(shape_four).astype(jnp.float32)
    o_heads = o_win.reshape(shape_four).astype(jnp.float32)
    scores = jnp.einsum('bihd,bjhd->bhij', q_heads, k_heads) * score_factor + bias[None]
    scores = jnp.where(allowed[None, None], scores, -jnp.inf)
    row_max = lax.optimization_barrier(jnp.max(scores, axis=-1, keepdims=True))
    expon = jnp.exp(scores - row_max)
    probs = expon / lax.optimization_barrier(jnp.sum(expon, axis=-1, keepdims=True))
    probs_low = lax.optimization_barrier(probs.astype(jnp.bfloat16)).astype(jnp.float32)
    d_probs = jnp.einsum('bihd,bjhd->bhij', o_heads, v_heads)
    delta_sum = lax.optimization_barrier(jnp.sum(probs * d_probs, axis=-1, keepdims=True))
    d_scores = probs * (d_probs - delta_sum)
    d_low = lax.optimization_barrier(d_scores.astype(jnp.bfloat16)).astype(jnp.float32)
    v_grad = jnp.einsum('bhij,bihd->bjhd', probs_low, o_heads)
    q_grad = jnp.einsum('bhij,bjhd->bihd', d_low, k_heads) * score_factor
    k_grad = jnp.einsum('bhij,bihd->bjhd', d_low, q_heads) * score_factor
    final_shape = (batch, count, width)
    return (q_grad.reshape(final_shape).astype(jnp.bfloat16), k_grad.reshape(final_shape).astype(jnp.bfloat16), v_grad.reshape(final_shape).astype(jnp.bfloat16), lax.optimization_barrier(jnp.sum(d_scores, axis=0)))

def merge_backward(y_block, merge_gain, d_norm_flat):
    levels, rows, cols, width = y_block.shape
    stacked = y_block.reshape(levels, rows // 2, 2, cols // 2, 2, width).transpose(0, 1, 3, 4, 2, 5)
    stacked = stacked.reshape(levels, rows // 2, cols // 2, 4 * width).astype(jnp.float32)
    mean_value = lax.optimization_barrier(jnp.mean(stacked, axis=-1, keepdims=True))
    centred = stacked - mean_value
    variance = lax.optimization_barrier(jnp.mean(centred * centred, axis=-1, keepdims=True))
    inverse = lax.rsqrt(variance + 1e-05)
    normed = centred * inverse
    d_hat = d_norm_flat.reshape(normed.shape) * merge_gain
    d_stack = (d_hat - lax.optimization_barrier(jnp.mean(d_hat, axis=-1, keepdims=True)) - normed * lax.optimization_barrier(jnp.mean(d_hat * normed, axis=-1, keepdims=True))) * inverse
    back = d_stack.reshape(levels, rows // 2, cols // 2, 2, 2, width).transpose(0, 1, 4, 2, 3, 5)
    return back.reshape(levels, rows, cols, width).astype(jnp.bfloat16)

def reference(y_block, merge_gain, merge_weight, d_merged, q_proj, k_proj, v_proj, bias_table):
    flat_grad = d_merged.reshape(-1, d_merged.shape[-1])
    d_norm_flat = jnp.dot(flat_grad, merge_weight.T, preferred_element_type=jnp.float32)
    d_out = merge_backward(y_block, merge_gain, d_norm_flat)
    levels = q_proj.shape[0]

    def to_windows(field):
        rolled = jnp.roll(field, (-3, -6), axis=(1, 2))
        _, rows, cols, width = rolled.shape
        cut = rolled.reshape(levels, rows // 6, 6, cols // 12, 12, width).transpose(1, 3, 0, 2, 4, 5)
        return cut.reshape(rows // 6, cols // 12, 144, width)

    def from_windows(windows):
        kinds, count, _, width = windows.shape
        grid = windows.reshape(kinds, count, levels, 6, 12, width).transpose(2, 0, 3, 1, 4, 5)
        grid = grid.reshape(levels, kinds * 6, count * 12, width)
        return jnp.roll(grid, (3, 6), axis=(1, 2))
    positions, row_in = window_positions()
    upper = row_in >= 3
    same_group = upper[:, None] == upper[None, :]
    kinds = bias_table.shape[0]

    def per_type(inputs):
        q_win, k_win, v_win, o_win, table_row, type_id = inputs
        bias = table_row[:, positions].reshape(-1, 144, 144)
        allowed = jnp.logical_or(same_group, type_id != kinds - 1)
        return window_grads(q_win, k_win, v_win, o_win, bias, allowed)
    results = lax.map(per_type, (to_windows(q_proj), to_windows(k_proj), to_windows(v_proj), to_windows(d_out), bias_table, jnp.arange(kinds, dtype=jnp.int32)))
    table_grad = jnp.zeros(bias_table.shape, jnp.float32).at[:, :, positions].add(results[3].reshape(kinds, bias_table.shape[1], -1))
    return (from_windows(results[0]), from_windows(results[1]), from_windows(results[2]), table_grad)
```

```python
import jax
import jax.numpy as jnp
import numpy as np
from jax import lax
from jax.experimental import pallas as pl
from jax.experimental.pallas import tpu as pltpu
from jax.sharding import PartitionSpec as P

NX, NY, NZ = 2, 4, 16
LAT = 4
HEADS = 24
ROWS = 12
PAD = 16
TOK = ROWS * PAD
SEG = 32
WIDE = ROWS * SEG
GROUPS = 6
LOW = -1e30
VMEM = 56 * 1024 * 1024
score_factor = 32 ** (-0.5)

z_groups = [[a * NZ + z for z in range(NZ)] for a in range(NX * NY)]
y_groups = [[(x * NY + y) * NZ + z for y in range(NY)] for x in range(NX) for z in range(NZ)]
xy_groups = [[a * NZ + z for a in range(NX * NY)] for z in range(NZ)]
x_lat_groups = [
    [(x * NY * NZ + b) * LAT + l for x in range(NX) for l in range(LAT)] for b in range(NY * NZ)
]


def layout_constants():
    tokens = np.arange(TOK)
    row, col = tokens // PAD, tokens % PAD
    real = col < 12
    sums = np.zeros((TOK, WIDE), np.float32)
    sums[tokens[real], (row * SEG + 11 - col)[real]] = 1
    spread = np.zeros((WIDE, TOK), np.float32)
    spread[(row * SEG + 11 + col)[real], tokens[real]] = 1
    quarter = np.zeros((256, 256), np.float32)
    back = np.zeros((TOK, 256), np.float32)
    for level in range(2):
        for pr in range(4):
            for pc in range(6):
                for di in range(2):
                    for dj in range(2):
                        spot = (di + 2 * dj) * 64 + (level * 4 + pr) * 8 + pc
                        fine_row, fine_col = 2 * pr + di, 2 * pc + dj
                        quarter[spot, (level * 8 + fine_row) * PAD + fine_col] = 1
                        if 1 <= fine_row <= 6:
                            back[(level * 6 + fine_row - 1) * PAD + fine_col, spot] = 1
    order = np.zeros((384, 384), np.float32)
    for l in range(3):
        for z in range(NZ):
            for i in range(8):
                order[l * 128 + z * 8 + i, z * 24 + l * 8 + i] = 1
    return [jnp.asarray(a, jnp.bfloat16) for a in (sums, spread, quarter, back, order)]


def dot(a, b, dims=((1,), (0,))):
    return lax.dot_general(a, b, (dims, ((), ())), preferred_element_type=jnp.float32)


def head_mask(h):
    lanes = lax.broadcasted_iota(jnp.int32, (1, 128), 1)
    return (lanes // 32) == h


def by_head(block):
    return jnp.concatenate(
        [jnp.where(head_mask(h), block, jnp.zeros_like(block)) for h in range(4)], axis=0
    )


def probs_kernel(qkv_ref, table_ref, spread_ref, mask_ref, p_ref):
    table = table_ref[0]
    wide = jnp.broadcast_to(table[:, None, :], (4 * ROWS, PAD, WIDE))
    wide = jnp.concatenate(
        [
            pltpu.roll(wide[:, :, s * 128 : (s + 1) * 128], 0, 2, stride=1, stride_axis=1)
            for s in range(3)
        ],
        axis=2,
    ).reshape(4 * TOK, WIDE)
    high = wide.astype(jnp.bfloat16)
    low = (wide - high.astype(jnp.float32)).astype(jnp.bfloat16)
    bias = dot(high, spread_ref[...]) + dot(low, spread_ref[...])
    scores = dot(by_head(qkv_ref[0]), qkv_ref[1], ((1,), (1,))) * score_factor + bias
    scores = (scores.reshape(4, TOK, TOK) + mask_ref[...][None]).reshape(4 * TOK, TOK)
    expon = jnp.exp(scores - jnp.max(scores, axis=-1, keepdims=True))
    p_ref[0] = expon / jnp.sum(expon, axis=-1, keepdims=True)


def norm_kernel(y_ref, quarter_ref, normed_ref, inverse_ref):
    fields = dot(quarter_ref[...], y_ref[...])
    parts = [fields[q * 64 : (q + 1) * 64] for q in range(4)]
    mean = jnp.sum(parts[0] + parts[1] + parts[2] + parts[3], axis=-1, keepdims=True) / 3072
    parts = [part - mean for part in parts]
    squares = [part * part for part in parts]
    variance = (
        jnp.sum(squares[0] + squares[1] + squares[2] + squares[3], axis=-1, keepdims=True) / 3072
    )
    inverse = lax.rsqrt(variance + 1e-05)
    for q in range(4):
        normed_ref[q] = parts[q] * inverse
    inverse_ref[...] = jnp.broadcast_to(inverse, (64, 128))


def merge_kernel(x_ref, w_ref, out_ref, acc_ref):
    acc_ref[...] = dot(x_ref[...], w_ref[...], ((1,), (1,)))
    for x in range(NX):
        for l in range(LAT):
            for level in range(2):
                own = ((x * LAT + l) * 6 + level * 3) * 8
                below = ((x * LAT + (l + 1) % LAT) * 6 + level * 3) * 8
                out_ref[x * LAT + l, level * 32 : level * 32 + 16] = acc_ref[
                    own + 8 : own + 24
                ].astype(jnp.bfloat16)
                out_ref[x * LAT + l, level * 32 + 16 : level * 32 + 32] = acc_ref[
                    below : below + 16
                ].astype(jnp.bfloat16)


def grads_kernel(
    recv_ref,
    order_ref,
    normed_ref,
    inverse_ref,
    gain_ref,
    back_ref,
    sums_ref,
    qkv_ref,
    p_ref,
    grads_ref,
    table_ref,
    o_ref,
    sum_ref,
):
    g = pl.program_id(0)

    @pl.when(g == 0)
    def _():
        pieces = [
            jnp.concatenate(
                [recv_ref[x * LAT + l, :, y * 128 : (y + 1) * 128] for l in range(3)], axis=1
            )
            for x in range(NX)
            for y in range(NY)
        ]
        d_norm = dot(jnp.concatenate(pieces, axis=0), order_ref[...])
        hats = []
        for q in range(4):
            left = d_norm[(2 * q) * 64 : (2 * q + 1) * 64]
            right = d_norm[(2 * q + 1) * 64 : (2 * q + 2) * 64]
            hats.append(jnp.concatenate([left, right], axis=1) * gain_ref[q])
        mean = jnp.sum(hats[0] + hats[1] + hats[2] + hats[3], axis=-1, keepdims=True) / 3072
        cross = [hats[q] * normed_ref[q] for q in range(4)]
        along = jnp.sum(cross[0] + cross[1] + cross[2] + cross[3], axis=-1, keepdims=True) / 3072
        inverse = inverse_ref[:, 0:1]
        stack = [(hats[q] - mean - normed_ref[q] * along) * inverse for q in range(4)]
        d_out = dot(back_ref[...], jnp.concatenate(stack, axis=0).astype(jnp.bfloat16))
        d_out = d_out.astype(jnp.bfloat16)
        for s in range(GROUPS):
            o_ref[s] = d_out[:, s * 128 : (s + 1) * 128]

    o_win = o_ref[g]
    q_win, k_win, v_win = qkv_ref[0], qkv_ref[1], qkv_ref[2]
    probs = p_ref[0]
    d_probs = dot(by_head(o_win), v_win, ((1,), (1,)))
    delta = jnp.sum(probs * d_probs, axis=-1, keepdims=True)
    d_low = (probs * (d_probs - delta)).astype(jnp.bfloat16)
    p_low = probs.astype(jnp.bfloat16)

    spread = dot(d_low, sums_ref[...]).reshape(4 * ROWS, PAD, WIDE)
    sums = [
        jnp.sum(
            pltpu.roll(spread[:, :, s * 128 : (s + 1) * 128], 0, 2, stride=1, stride_axis=1), axis=1
        )
        for s in range(3)
    ]
    sum_ref[g] = jnp.concatenate(sums, axis=1)

    q_all = dot(d_low, k_win)
    q_grad = jnp.zeros((TOK, 128), jnp.float32)
    for h in range(4):
        q_grad = jnp.where(head_mask(h), q_all[h * TOK : (h + 1) * TOK], q_grad)
    grads_ref[0] = (q_grad * score_factor).astype(jnp.bfloat16)

    q_turn = q_win.astype(jnp.float32).T.astype(jnp.bfloat16)
    o_turn = o_win.astype(jnp.float32).T.astype(jnp.bfloat16)
    k_parts, v_parts = [], []
    for h in range(4):
        rows = slice(h * 32, (h + 1) * 32)
        k_parts.append(dot(q_turn[rows], d_low[h * TOK : (h + 1) * TOK]))
        v_parts.append(dot(o_turn[rows], p_low[h * TOK : (h + 1) * TOK]))
    k_grad = jnp.concatenate(k_parts, axis=0).T
    v_grad = jnp.concatenate(v_parts, axis=0).T
    grads_ref[1] = (k_grad * score_factor).astype(jnp.bfloat16)
    grads_ref[2] = v_grad.astype(jnp.bfloat16)

    @pl.when(g == GROUPS - 1)
    def _():
        whole = jnp.concatenate([sum_ref[s] for s in range(GROUPS)], axis=0)
        for part in range(8):
            table_ref[part, 0:36] = whole[part * 36 : (part + 1) * 36]
            table_ref[part, 36:40] = jnp.zeros((4, WIDE), jnp.float32)


def whole_spec(shape):
    return pl.BlockSpec(shape, lambda *_: (0,) * len(shape))


def window_probs(qkv, table, spread, mask):
    return pl.pallas_call(
        probs_kernel,
        grid=(GROUPS,),
        in_specs=[
            pl.BlockSpec((3, TOK, 128), lambda g: (0, 0, g)),
            pl.BlockSpec((1, 4 * ROWS, WIDE), lambda g: (g, 0, 0)),
            whole_spec((WIDE, TOK)),
            whole_spec((TOK, TOK)),
        ],
        out_specs=pl.BlockSpec((1, 4 * TOK, TOK), lambda g: (g, 0, 0)),
        out_shape=jax.ShapeDtypeStruct((GROUPS, 4 * TOK, TOK), jnp.float32),
        compiler_params=pltpu.CompilerParams(vmem_limit_bytes=VMEM),
        name="window_probs",
    )(qkv, table, spread, mask)


def normalise(y_rows, quarter):
    return pl.pallas_call(
        norm_kernel,
        out_shape=(
            jax.ShapeDtypeStruct((4, 64, 768), jnp.float32),
            jax.ShapeDtypeStruct((64, 128), jnp.float32),
        ),
        compiler_params=pltpu.CompilerParams(vmem_limit_bytes=VMEM),
        name="normalise",
    )(y_rows, quarter)


def merge_product(rows, weight):
    return pl.pallas_call(
        merge_kernel,
        out_shape=jax.ShapeDtypeStruct((8, 64, 512), jnp.bfloat16),
        scratch_shapes=[pltpu.VMEM((384, 512), jnp.float32)],
        compiler_params=pltpu.CompilerParams(vmem_limit_bytes=VMEM),
        name="merge_product",
    )(rows, weight)


def window_grads(recv, order, normed, inverse, gain, back, sums, qkv, probs):
    return pl.pallas_call(
        grads_kernel,
        grid=(GROUPS,),
        in_specs=[
            whole_spec((8, 64, 512)),
            whole_spec((384, 384)),
            whole_spec((4, 64, 768)),
            whole_spec((64, 128)),
            whole_spec((4, 1, 768)),
            whole_spec((TOK, 256)),
            whole_spec((TOK, WIDE)),
            pl.BlockSpec((3, TOK, 128), lambda g: (0, 0, g)),
            pl.BlockSpec((1, 4 * TOK, TOK), lambda g: (g, 0, 0)),
        ],
        out_specs=(
            pl.BlockSpec((3, TOK, 128), lambda g: (0, 0, g)),
            whole_spec((8, 40, WIDE)),
        ),
        out_shape=(
            jax.ShapeDtypeStruct((3, TOK, 768), jnp.bfloat16),
            jax.ShapeDtypeStruct((8, 40, WIDE), jnp.float32),
        ),
        scratch_shapes=[
            pltpu.VMEM((GROUPS, TOK, 128), jnp.bfloat16),
            pltpu.VMEM((GROUPS, 4 * ROWS, WIDE), jnp.float32),
        ],
        compiler_params=pltpu.CompilerParams(vmem_limit_bytes=VMEM),
        name="window_grads",
    )(recv, order, normed, inverse, gain, back, sums, qkv, probs)


def from_behind(shard, axis, by):
    size = lax.axis_size(axis)
    return lax.ppermute(shard, axis, [(i, (i + by) % size) for i in range(size)])


def swap(shard, axis, groups):
    return lax.all_to_all(shard, axis, 0, 0, tiled=True, axis_index_groups=groups)


def share(shard, count, axis, groups):
    return swap(jnp.broadcast_to(shard[None], (count,) + shard.shape), axis, groups)


def on_device(y_block, merge_gain, merge_weight, d_merged, q_proj, k_proj, v_proj, bias_table):
    sums, spread, quarter, back, order = layout_constants()
    lat = lax.axis_index("lat")

    mine = lax.dynamic_slice_in_dim(merge_weight, jnp.minimum(lat, 2) * 8, 8, axis=0)
    weight = share(mine, NZ, "lon", z_groups).reshape(NZ * 8, -1)
    weight = share(weight, NY, "lon", y_groups).reshape(NY * NZ * 8, -1)

    eastern_d = from_behind(d_merged[:, :, :3], "lon", -1)
    eastern = from_behind(
        jnp.stack([q_proj[:, :, :6], k_proj[:, :, :6], v_proj[:, :, :6], y_block[:, :, :6]]),
        "lon",
        -1,
    )
    d_rows = jnp.concatenate(
        [d_merged[:, :, 3:], eastern_d, jnp.zeros_like(d_merged[:, :, :2])], axis=2
    )
    d_rows = share(d_rows.reshape(48, -1), 8, ("lon", "lat"), x_lat_groups).reshape(384, -1)

    across = jnp.concatenate(
        [
            jnp.stack([q_proj[:, :, 6:], k_proj[:, :, 6:], v_proj[:, :, 6:], y_block[:, :, 6:]]),
            eastern,
            jnp.zeros_like(eastern[:, :, :, :4]),
        ],
        axis=3,
    )
    qkv_south = from_behind(across[:3, :, :3], "lat", -1)
    y_south = from_behind(across[3, :, :4], "lat", -1)
    qkv = jnp.concatenate([across[:3, :, 3:], qkv_south], axis=2).reshape(3, TOK, 768)
    y_rows = jnp.concatenate([across[3, :, 2:], y_south], axis=1).reshape(256, 768)

    table = bias_table.reshape(HEADS, 2, 2, 6, 6, 23).transpose(0, 1, 3, 2, 4, 5)[..., ::-1]
    table = jnp.pad(table, ((0, 0),) * 5 + ((0, SEG - 23),)).reshape(GROUPS, 4 * ROWS, WIDE)
    tokens = jnp.arange(TOK, dtype=jnp.int32)
    upper = tokens // PAD % 6 >= 3
    allowed = jnp.logical_or(upper[:, None] == upper[None, :], lat != LAT - 1)
    allowed = jnp.logical_and(allowed, (tokens % PAD < 12)[None, :])
    mask = jnp.where(allowed, 0.0, LOW)

    probs = window_probs(qkv, table, spread, mask)
    normed, inverse = normalise(y_rows, quarter)

    parts = merge_product(d_rows, weight)
    recv = swap(parts, ("lon", "lat"), x_lat_groups)
    grads, table_part = window_grads(
        recv, order, normed, inverse, merge_gain.reshape(4, 1, 768), back, sums, qkv, probs
    )

    table_part = jnp.sum(swap(table_part, "lon", xy_groups), axis=0).astype(jnp.bfloat16)
    table_part = share(table_part, NZ, "lon", z_groups).astype(jnp.float32)
    table_part = jnp.sum(table_part, axis=0).astype(jnp.bfloat16)
    table_sum = share(table_part, 8, "lon", xy_groups)[:, :36].astype(jnp.float32)
    table_sum = table_sum.reshape(HEADS, 2, 6, 2, 6, SEG)[..., :23].transpose(0, 1, 3, 2, 4, 5)
    table_grad = table_sum.reshape(bias_table.shape)

    grid = grads.reshape(3, 2, 6, PAD, 768)[:, :, :, :12]
    southern = from_behind(grid[:, :, 3:], "lat", 1)
    fixed = jnp.concatenate([southern, grid[:, :, :3]], axis=2)
    western = from_behind(fixed[:, :, :, 6:], "lon", 1)
    finished = jnp.concatenate([western, fixed[:, :, :, :6]], axis=3)
    return (finished[0], finished[1], finished[2], table_grad)


def solution(mesh):
    placed = (
        P(None, "lat", "lon", None),
        P(),
        P("lon", None),
        P(None, "lat", "lon", None),
        P(None, "lat", "lon", None),
        P(None, "lat", "lon", None),
        P(None, "lat", "lon", None),
        P("lat", None, None),
    )
    return jax.shard_map(
        on_device,
        mesh=mesh,
        in_specs=placed,
        out_specs=(
            P(None, "lat", "lon", None),
            P(None, "lat", "lon", None),
            P(None, "lat", "lon", None),
            P("lat", None, None),
        ),
        check_vma=False,
    )
```

```python
import jax
import jax.numpy as jnp
import numpy as np
from jax import lax
from jax.experimental import pallas as pl
from jax.experimental.pallas import tpu as pltpu
from jax.sharding import PartitionSpec as P

NX, NY, NZ = 2, 4, 16
LAT = 4
HEADS = 24
ROWS = 12
PAD = 16
TOK = ROWS * PAD
SEG = 32
WIDE = ROWS * SEG
GROUPS = 6
LOW = -1e30
VMEM = 56 * 1024 * 1024
score_factor = 32 ** (-0.5)

z_groups = [[a * NZ + z for z in range(NZ)] for a in range(NX * NY)]
y_groups = [[(x * NY + y) * NZ + z for y in range(NY)] for x in range(NX) for z in range(NZ)]
near_groups = [
    [a * NZ + 2 * pair + e for a in range(NX * NY) for e in range(2)] for pair in range(NZ // 2)
]
far_groups = [
    [a * NZ + 2 * pair + e for pair in range(NZ // 2)] for a in range(NX * NY) for e in range(2)
]
x_lat_groups = [
    [(x * NY * NZ + b) * LAT + l for x in range(NX) for l in range(LAT)] for b in range(NY * NZ)
]


def layout_constants():
    tokens = np.arange(TOK)
    row, col = tokens // PAD, tokens % PAD
    real = col < 12
    sums = np.zeros((TOK, WIDE), np.float32)
    sums[tokens[real], (row * SEG + 11 - col)[real]] = 1
    spread = np.zeros((WIDE, TOK), np.float32)
    spread[(row * SEG + 11 + col)[real], tokens[real]] = 1
    quarter = np.zeros((256, 256), np.float32)
    back = np.zeros((TOK, 256), np.float32)
    for level in range(2):
        for pr in range(4):
            for pc in range(6):
                for di in range(2):
                    for dj in range(2):
                        spot = (di + 2 * dj) * 64 + (level * 4 + pr) * 8 + pc
                        fine_row, fine_col = 2 * pr + di, 2 * pc + dj
                        quarter[spot, (level * 8 + fine_row) * PAD + fine_col] = 1
                        if 1 <= fine_row <= 6:
                            back[(level * 6 + fine_row - 1) * PAD + fine_col, spot] = 1
    shuffle = np.zeros((512, 384), np.float32)
    order = np.zeros((512, 384), np.float32)
    for l in range(4):
        for z in range(NZ):
            for i in range(6):
                shuffle[l * 128 + z * 6 + i, z * 24 + l * 6 + i] = 1
                order[l * 128 + z * 6 + i, z * 24 + l * 6 + i] = 1
    open_up = np.zeros((2, 138, WIDE), np.float32)
    for half in range(2):
        for r in range(6):
            for d in range(23):
                open_up[half, r * 23 + d, half * 192 + r * SEG + 22 - d] = 1
    all_of = (sums, spread, quarter, back, order, shuffle, open_up)
    return [jnp.asarray(a, jnp.bfloat16) for a in all_of]


def dot(a, b, dims=((1,), (0,))):
    return lax.dot_general(a, b, (dims, ((), ())), preferred_element_type=jnp.float32)


def head_mask(h):
    lanes = lax.broadcasted_iota(jnp.int32, (1, 128), 1)
    return (lanes // 32) == h


def by_head(block):
    return jnp.concatenate(
        [jnp.where(head_mask(h), block, jnp.zeros_like(block)) for h in range(4)], axis=0
    )


def split_dot(values, matrix):
    high = values.astype(jnp.bfloat16)
    low = (values - high.astype(jnp.float32)).astype(jnp.bfloat16)
    return dot(high, matrix) + dot(low, matrix)


def window(north_ref, south_ref, which):
    pieces = []
    for level in range(2):
        pieces.append(north_ref[which, level].reshape(48, 128))
        pieces.append(south_ref[which, level, 0:3].reshape(48, 128))
    return jnp.concatenate(pieces, axis=0)


def pack_kernel(lat_ref, w_ref, out_ref):
    first = lat_ref[0] * 6
    to = lax.broadcasted_iota(jnp.int32, (24, 24), 0)
    source = lax.broadcasted_iota(jnp.int32, (24, 24), 1)
    total = jnp.zeros((24, 384), jnp.float32)
    for part in range(4):
        pick = jnp.logical_and(to // 6 == part, source == first + to - part * 6)
        pick = jnp.where(pick, 1.0, 0.0).astype(jnp.bfloat16)
        total += dot(pick, w_ref[:, part * 384 : (part + 1) * 384])
    packed = total.astype(jnp.bfloat16)
    for z in range(NZ):
        out_ref[z] = packed


def bias_kernel(table_ref, open_ref, spread_ref, mask_ref, bias_ref, wide_ref):
    @pl.when(pl.program_id(0) == 0)
    def _():
        halves = []
        for half in range(2):
            pieces = []
            for a in range(ROWS):
                first = (a // 6 * 2 + half) * 828 + a % 6 * 138
                pieces.append(table_ref[0, :, first : first + 138])
            halves.append(split_dot(jnp.concatenate(pieces, axis=0), open_ref[half]))
        for s in range(3):
            wide_ref[s] = (halves[0] + halves[1])[:, s * 128 : (s + 1) * 128]

    first = pl.program_id(0) * 4
    pieces = []
    for s in range(3):
        table = jnp.concatenate(
            [wide_ref[s, pl.ds(first + h, ROWS, stride=HEADS), :] for h in range(4)], axis=0
        )
        table = jnp.broadcast_to(table[:, None, :], (4 * ROWS, PAD, 128))
        pieces.append(pltpu.roll(table, 0, 2, stride=1, stride_axis=1))
    wide = jnp.concatenate(pieces, axis=2).reshape(4 * TOK, WIDE)
    bias = split_dot(wide, spread_ref[...]).reshape(4, TOK, TOK) + mask_ref[...][None]
    bias_ref[0] = bias.reshape(4 * TOK, TOK)


def probs_kernel(north_ref, south_ref, bias_ref, p_ref):
    q_win, k_win = window(north_ref, south_ref, 0), window(north_ref, south_ref, 1)
    scores = dot(by_head(q_win), k_win, ((1,), (1,))) * score_factor + bias_ref[0]
    expon = jnp.exp(scores - jnp.max(scores, axis=-1, keepdims=True))
    p_ref[0] = expon * (1.0 / jnp.sum(expon, axis=-1, keepdims=True))


def norm_kernel(a_ref, b_ref, south_ref, quarter_ref, normed_ref, inverse_ref):
    pieces = []
    for level in range(2):
        pieces.append(a_ref[0, level].reshape(32, 768))
        pieces.append(b_ref[0, level].reshape(32, 768))
        pieces.append(south_ref[0, level].reshape(64, 768))
    fields = dot(quarter_ref[...], jnp.concatenate(pieces, axis=0))
    parts = [fields[q * 64 : (q + 1) * 64] for q in range(4)]
    mean = jnp.sum(parts[0] + parts[1] + parts[2] + parts[3], axis=-1, keepdims=True) / 3072
    parts = [part - mean for part in parts]
    squares = [part * part for part in parts]
    variance = (
        jnp.sum(squares[0] + squares[1] + squares[2] + squares[3], axis=-1, keepdims=True) / 3072
    )
    inverse = lax.rsqrt(variance + 1e-05)
    for q in range(4):
        normed_ref[q] = parts[q] * inverse
    inverse_ref[...] = jnp.broadcast_to(inverse, (64, 128))


def merge_kernel(spot_ref, near_ref, far_ref, w_ref, shuffle_ref, out_ref, acc_ref):
    weights = [dot(shuffle_ref[...], w_ref[y]).astype(jnp.bfloat16) for y in range(NY)]
    near, far = None, None
    for part in range(4):
        rows, columns = slice(part * 128, part * 128 + 128), slice(part * 384, part * 384 + 384)
        weight = jnp.concatenate([weights[y][rows] for y in range(NY)], axis=0)
        near_part = dot(near_ref[:, columns], weight, ((1,), (1,)))
        far_part = dot(far_ref[:, columns], weight, ((1,), (1,)))
        near = near_part if part == 0 else near + near_part
        far = far_part if part == 0 else far + far_part
    acc_ref[:192] = near
    acc_ref[192:] = far
    for x in range(NX):
        for l in range(LAT):
            for level in range(2):
                own = pl.multiple_of(spot_ref[x * LAT + l] + level * 24 + 8, 8)
                below = pl.multiple_of(spot_ref[x * LAT + (l + 1) % LAT] + level * 24, 8)
                out_ref[x * LAT + l, level * 32 : level * 32 + 16] = acc_ref[
                    pl.ds(own, 16)
                ].astype(jnp.bfloat16)
                out_ref[x * LAT + l, level * 32 + 16 : level * 32 + 32] = acc_ref[
                    pl.ds(below, 16)
                ].astype(jnp.bfloat16)


def scores_kernel(
    recv_ref,
    order_ref,
    normed_ref,
    inverse_ref,
    gain_ref,
    back_ref,
    sums_ref,
    north_ref,
    south_ref,
    p_ref,
    o_out_ref,
    d_ref,
    table_ref,
    o_ref,
    sum_ref,
):
    g = pl.program_id(0)

    @pl.when(g == 0)
    def _():
        pieces = [
            jnp.concatenate(
                [recv_ref[x * LAT + l, :, y * 128 : (y + 1) * 128] for l in range(LAT)], axis=1
            )
            for x in range(NX)
            for y in range(NY)
        ]
        d_norm = dot(jnp.concatenate(pieces, axis=0), order_ref[...])
        hats = []
        for q in range(4):
            left = d_norm[(2 * q) * 64 : (2 * q + 1) * 64]
            right = d_norm[(2 * q + 1) * 64 : (2 * q + 2) * 64]
            hats.append(jnp.concatenate([left, right], axis=1) * gain_ref[q])
        mean = jnp.sum(hats[0] + hats[1] + hats[2] + hats[3], axis=-1, keepdims=True) / 3072
        cross = [hats[q] * normed_ref[q] for q in range(4)]
        along = jnp.sum(cross[0] + cross[1] + cross[2] + cross[3], axis=-1, keepdims=True) / 3072
        inverse = inverse_ref[:, 0:1]
        stack = [(hats[q] - mean - normed_ref[q] * along) * inverse for q in range(4)]
        d_out = dot(back_ref[...], jnp.concatenate(stack, axis=0).astype(jnp.bfloat16))
        d_out = d_out.astype(jnp.bfloat16)
        for s in range(GROUPS):
            o_ref[s] = d_out[:, s * 128 : (s + 1) * 128]

    o_win = o_ref[g]
    o_out_ref[0] = o_win
    probs = p_ref[0]
    d_probs = dot(by_head(o_win), window(north_ref, south_ref, 0), ((1,), (1,)))
    delta = jnp.sum(probs * d_probs, axis=-1, keepdims=True)
    d_low = (probs * (d_probs - delta)).astype(jnp.bfloat16)
    d_ref[0] = d_low

    spread = dot(d_low, sums_ref[...]).reshape(4 * ROWS, PAD, WIDE)
    sums = [
        jnp.sum(
            pltpu.roll(spread[:, :, s * 128 : (s + 1) * 128], 0, 2, stride=1, stride_axis=1), axis=1
        )
        for s in range(3)
    ]
    sum_ref[g] = jnp.concatenate(sums, axis=1)

    @pl.when(g == GROUPS - 1)
    def _():
        whole = jnp.concatenate([sum_ref[s] for s in range(GROUPS)], axis=0)
        for part in range(16):
            table_ref[part, 0:18] = whole[part * 18 : (part + 1) * 18]
            table_ref[part, 18:24] = jnp.zeros((6, WIDE), jnp.float32)


def grads_kernel(north_ref, south_ref, o_ref, d_ref, p_ref, grads_ref):
    q_win, k_win = window(north_ref, south_ref, 0), window(north_ref, south_ref, 1)
    o_win = o_ref[0]
    d_low = d_ref[0]
    p_low = p_ref[0].astype(jnp.bfloat16)
    q_all = dot(d_low, k_win)
    q_grad = jnp.zeros((TOK, 128), jnp.float32)
    for h in range(4):
        q_grad = jnp.where(head_mask(h), q_all[h * TOK : (h + 1) * TOK], q_grad)
    grads_ref[0] = (q_grad * score_factor).astype(jnp.bfloat16)

    q_turn = q_win.astype(jnp.float32).T.astype(jnp.bfloat16)
    o_turn = o_win.astype(jnp.float32).T.astype(jnp.bfloat16)
    k_parts, v_parts = [], []
    for h in range(4):
        rows = slice(h * 32, (h + 1) * 32)
        k_parts.append(dot(q_turn[rows], d_low[h * TOK : (h + 1) * TOK]))
        v_parts.append(dot(o_turn[rows], p_low[h * TOK : (h + 1) * TOK]))
    k_grad = jnp.concatenate(k_parts, axis=0).T
    v_grad = jnp.concatenate(v_parts, axis=0).T
    grads_ref[1] = (k_grad * score_factor).astype(jnp.bfloat16)
    grads_ref[2] = v_grad.astype(jnp.bfloat16)


def whole_spec(shape):
    return pl.BlockSpec(shape, lambda *_: (0,) * len(shape))


def north_spec(first, count):
    return pl.BlockSpec((count, 2, 3, PAD, 128), lambda g: (first // count, 0, 1, 0, g))


def south_spec(first, count):
    return pl.BlockSpec((count, 2, 4, PAD, 128), lambda g: (first // count, 0, 0, 0, g))


def group_spec(rows, columns):
    return pl.BlockSpec((1, rows, columns), lambda g: (g, 0, 0))


params = pltpu.CompilerParams(vmem_limit_bytes=VMEM)
smem = pl.BlockSpec(memory_space=pltpu.SMEM)
vmem = pl.BlockSpec(memory_space=pltpu.VMEM)


def pack_weight(lat, weight):
    return pl.pallas_call(
        pack_kernel,
        in_specs=[smem, vmem],
        out_specs=vmem,
        out_shape=jax.ShapeDtypeStruct((NZ, 24, 384), jnp.bfloat16),
        compiler_params=params,
        name="pack_weight",
    )(lat, weight)


def window_bias(table, open_up, spread, mask):
    return pl.pallas_call(
        bias_kernel,
        grid=(GROUPS,),
        in_specs=[
            whole_spec((1, HEADS, 3312)),
            whole_spec((2, 138, WIDE)),
            whole_spec((WIDE, TOK)),
            whole_spec((TOK, TOK)),
        ],
        out_specs=group_spec(4 * TOK, TOK),
        out_shape=jax.ShapeDtypeStruct((GROUPS, 4 * TOK, TOK), jnp.float32),
        scratch_shapes=[pltpu.VMEM((3, ROWS * HEADS, 128), jnp.float32)],
        compiler_params=params,
        name="window_bias",
    )(table, open_up, spread, mask)


def window_probs(across, south, bias):
    return pl.pallas_call(
        probs_kernel,
        grid=(GROUPS,),
        in_specs=[north_spec(0, 2), south_spec(0, 2), group_spec(4 * TOK, TOK)],
        out_specs=group_spec(4 * TOK, TOK),
        out_shape=jax.ShapeDtypeStruct((GROUPS, 4 * TOK, TOK), jnp.float32),
        compiler_params=params,
        name="window_probs",
    )(across, south, bias)


def normalise(across, south, quarter):
    return pl.pallas_call(
        norm_kernel,
        grid=(1,),
        in_specs=[
            pl.BlockSpec((1, 2, 2, PAD, 768), lambda g: (3, 0, 1, 0, 0)),
            pl.BlockSpec((1, 2, 2, PAD, 768), lambda g: (3, 0, 2, 0, 0)),
            pl.BlockSpec((1, 2, 4, PAD, 768), lambda g: (3, 0, 0, 0, 0)),
            whole_spec((256, 256)),
        ],
        out_specs=(whole_spec((4, 64, 768)), whole_spec((64, 128))),
        out_shape=(
            jax.ShapeDtypeStruct((4, 64, 768), jnp.float32),
            jax.ShapeDtypeStruct((64, 128), jnp.float32),
        ),
        compiler_params=params,
        name="normalise",
    )(across, across, south, quarter)


def merge_product(spots, near, far, weight, shuffle):
    return pl.pallas_call(
        merge_kernel,
        in_specs=[smem, vmem, vmem, vmem, vmem],
        out_specs=vmem,
        out_shape=jax.ShapeDtypeStruct((8, 64, 512), jnp.bfloat16),
        scratch_shapes=[pltpu.VMEM((384, 512), jnp.float32)],
        compiler_params=params,
        name="merge_product",
    )(spots, near, far, weight, shuffle)


def score_grads(recv, order, normed, inverse, gain, back, sums, across, south, probs):
    return pl.pallas_call(
        scores_kernel,
        grid=(GROUPS,),
        in_specs=[
            whole_spec((8, 64, 512)),
            whole_spec((512, 384)),
            whole_spec((4, 64, 768)),
            whole_spec((64, 128)),
            whole_spec((4, 1, 768)),
            whole_spec((TOK, 256)),
            whole_spec((TOK, WIDE)),
            north_spec(2, 1),
            south_spec(2, 1),
            group_spec(4 * TOK, TOK),
        ],
        out_specs=(
            group_spec(TOK, 128),
            group_spec(4 * TOK, TOK),
            whole_spec((16, 24, WIDE)),
        ),
        out_shape=(
            jax.ShapeDtypeStruct((GROUPS, TOK, 128), jnp.bfloat16),
            jax.ShapeDtypeStruct((GROUPS, 4 * TOK, TOK), jnp.bfloat16),
            jax.ShapeDtypeStruct((16, 24, WIDE), jnp.float32),
        ),
        scratch_shapes=[
            pltpu.VMEM((GROUPS, TOK, 128), jnp.bfloat16),
            pltpu.VMEM((GROUPS, 4 * ROWS, WIDE), jnp.float32),
        ],
        compiler_params=params,
        name="score_grads",
    )(recv, order, normed, inverse, gain, back, sums, across, south, probs)


def window_grads(across, south, o_win, d_low, probs):
    return pl.pallas_call(
        grads_kernel,
        grid=(GROUPS,),
        in_specs=[
            north_spec(0, 2),
            south_spec(0, 2),
            group_spec(TOK, 128),
            group_spec(4 * TOK, TOK),
            group_spec(4 * TOK, TOK),
        ],
        out_specs=pl.BlockSpec((3, TOK, 128), lambda g: (0, 0, g)),
        out_shape=jax.ShapeDtypeStruct((3, TOK, 768), jnp.bfloat16),
        compiler_params=params,
        name="window_grads",
    )(across, south, o_win, d_low, probs)


def from_behind(shard, axis, by):
    size = lax.axis_size(axis)
    return lax.ppermute(shard, axis, [(i, (i + by) % size) for i in range(size)])


def partner(shard, axis, bit):
    return lax.ppermute(shard, axis, [(i, i ^ bit) for i in range(lax.axis_size(axis))])


def swap(shard, axis, groups):
    return lax.all_to_all(shard, axis, 0, 0, tiled=True, axis_index_groups=groups)


def share(shard, count, axis, groups):
    return swap(jnp.broadcast_to(shard[None], (count,) + shard.shape), axis, groups)


def on_device(y_block, merge_gain, merge_weight, d_merged, q_proj, k_proj, v_proj, bias_table):
    sums, spread, quarter, back, order, shuffle, open_up = layout_constants()
    lat = lax.axis_index("lat")

    packed = pack_weight(lat.reshape(1), merge_weight)
    weight_z = swap(packed, "lon", z_groups).reshape(NZ * 24, 384)

    tokens = jnp.arange(TOK, dtype=jnp.int32)
    upper = tokens // PAD % 6 >= 3
    allowed = jnp.logical_or(upper[:, None] == upper[None, :], lat != LAT - 1)
    allowed = jnp.logical_and(allowed, (tokens % PAD < 12)[None, :])
    bias = window_bias(bias_table, open_up, spread, jnp.where(allowed, 0.0, LOW))

    eastern_d = from_behind(d_merged[:, :, :3], "lon", -1)
    d_rows = jnp.concatenate(
        [d_merged[:, :, 3:], eastern_d, jnp.zeros_like(d_merged[:, :, :2])], axis=2
    ).reshape(48, -1)
    d_rows = jnp.concatenate([d_rows, partner(d_rows, "lat", 2)], axis=0)
    near = jnp.concatenate([d_rows, partner(d_rows, "lon", NY * NZ)], axis=0)
    far = partner(near, "lat", 1)
    me = (lax.axis_index("lon") // (NY * NZ)) * LAT + lat
    rel = jnp.bitwise_xor(jnp.arange(8, dtype=jnp.int32), me)
    spots = (rel % 2 * 4 + rel // 4 * 2 + rel // 2 % 2) * 48

    weight_z, bias, q_proj, k_proj, v_proj, y_block = lax.optimization_barrier(
        (weight_z, bias, q_proj, k_proj, v_proj, y_block)
    )
    weight = share(weight_z, NY, "lon", y_groups)
    eastern = from_behind(
        jnp.stack([q_proj[:, :, :6], k_proj[:, :, :6], v_proj[:, :, :6], y_block[:, :, :6]]),
        "lon",
        -1,
    )
    across = jnp.concatenate(
        [
            jnp.stack([q_proj[:, :, 6:], k_proj[:, :, 6:], v_proj[:, :, 6:], y_block[:, :, 6:]]),
            eastern,
            jnp.zeros_like(eastern[:, :, :, :4]),
        ],
        axis=3,
    )
    south = from_behind(across[:, :, :4], "lat", -1)

    parts = merge_product(spots, near, far, weight, shuffle)
    recv = swap(parts, ("lon", "lat"), x_lat_groups)

    south, _ = lax.optimization_barrier((south, parts))
    probs = window_probs(across, south, bias)
    normed, inverse = normalise(across, south, quarter)

    o_win, d_low, table_part = score_grads(
        recv, order, normed, inverse, merge_gain.reshape(4, 1, 768), back, sums, across, south, probs
    )

    table_part = jnp.sum(swap(table_part, "lon", near_groups), axis=0).astype(jnp.bfloat16)
    grads = window_grads(across, south, o_win, d_low, probs)
    grid = grads.reshape(3, 2, 6, PAD, 768)[:, :, :, :12]
    southern = from_behind(grid[:, :, 3:], "lat", 1)
    fixed = jnp.concatenate([southern, grid[:, :, :3]], axis=2)

    table_part = share(table_part, NZ // 2, "lon", far_groups)
    table_part, fixed = lax.optimization_barrier((table_part, fixed))
    western = from_behind(fixed[:, :, :, 6:], "lon", 1)
    finished = jnp.concatenate([western, fixed[:, :, :, :6]], axis=3)

    table_part = jnp.sum(table_part.astype(jnp.float32), axis=0).astype(jnp.bfloat16)
    table_sum = share(table_part, 16, "lon", near_groups)[:, :18].astype(jnp.float32)
    table_sum = table_sum.reshape(HEADS, 2, 6, 2, 6, SEG)[..., :23].transpose(0, 1, 3, 2, 4, 5)
    table_grad = table_sum.reshape(bias_table.shape)
    return (finished[0], finished[1], finished[2], table_grad)


def solution(mesh):
    placed = (
        P(None, "lat", "lon", None),
        P(),
        P("lon", None),
        P(None, "lat", "lon", None),
        P(None, "lat", "lon", None),
        P(None, "lat", "lon", None),
        P(None, "lat", "lon", None),
        P("lat", None, None),
    )
    return jax.shard_map(
        on_device,
        mesh=mesh,
        in_specs=placed,
        out_specs=(
            P(None, "lat", "lon", None),
            P(None, "lat", "lon", None),
            P(None, "lat", "lon", None),
            P("lat", None, None),
        ),
        check_vma=False,
    )
```

```python
import jax
import jax.numpy as jnp
import numpy as np
from jax import lax
from jax.experimental import pallas as pl
from jax.experimental.pallas import tpu as pltpu
from jax.sharding import PartitionSpec as P

NX, NY, NZ = 2, 4, 16
LAT = 4
HEADS = 24
ROWS = 12
PAD = 16
TOK = ROWS * PAD
SEG = 32
WIDE = ROWS * SEG
GROUPS = 6
LOW = -1e30
VMEM = 56 * 1024 * 1024
score_factor = 32 ** (-0.5)

z_groups = [[a * NZ + z for z in range(NZ)] for a in range(NX * NY)]
y_groups = [[(x * NY + y) * NZ + z for y in range(NY)] for x in range(NX) for z in range(NZ)]
near_groups = [
    [a * NZ + 2 * pair + e for a in range(NX * NY) for e in range(2)] for pair in range(NZ // 2)
]
far_groups = [
    [a * NZ + 2 * pair + e for pair in range(NZ // 2)] for a in range(NX * NY) for e in range(2)
]
x_lat_groups = [
    [(x * NY * NZ + b) * LAT + l for x in range(NX) for l in range(LAT)] for b in range(NY * NZ)
]


def layout_constants():
    tokens = np.arange(TOK)
    row, col = tokens // PAD, tokens % PAD
    real = col < 12
    sums = np.zeros((TOK, WIDE), np.float32)
    sums[tokens[real], (row * SEG + 11 - col)[real]] = 1
    spread = np.zeros((WIDE, TOK), np.float32)
    spread[(row * SEG + 11 + col)[real], tokens[real]] = 1
    quarter = np.zeros((256, 256), np.float32)
    back = np.zeros((TOK, 256), np.float32)
    for level in range(2):
        for pr in range(4):
            for pc in range(6):
                for di in range(2):
                    for dj in range(2):
                        spot = (di + 2 * dj) * 64 + (level * 4 + pr) * 8 + pc
                        fine_row, fine_col = 2 * pr + di, 2 * pc + dj
                        quarter[spot, (level * 8 + fine_row) * PAD + fine_col] = 1
                        if 1 <= fine_row <= 6:
                            back[(level * 6 + fine_row - 1) * PAD + fine_col, spot] = 1
    shuffle = np.zeros((512, 384), np.float32)
    order = np.zeros((512, 384), np.float32)
    for l in range(4):
        for z in range(NZ):
            for i in range(6):
                shuffle[l * 128 + z * 6 + i, z * 24 + l * 6 + i] = 1
                order[l * 128 + z * 6 + i, z * 24 + l * 6 + i] = 1
    open_up = np.zeros((2, 138, WIDE), np.float32)
    for half in range(2):
        for r in range(6):
            for d in range(23):
                open_up[half, r * 23 + d, half * 192 + r * SEG + 22 - d] = 1
    all_of = (sums, spread, quarter, back, order, shuffle, open_up)
    return [jnp.asarray(a, jnp.bfloat16) for a in all_of]


def dot(a, b, dims=((1,), (0,))):
    return lax.dot_general(a, b, (dims, ((), ())), preferred_element_type=jnp.float32)


def head_mask(h):
    lanes = lax.broadcasted_iota(jnp.int32, (1, 128), 1)
    return (lanes // 32) == h


def by_head(block):
    return jnp.concatenate(
        [jnp.where(head_mask(h), block, jnp.zeros_like(block)) for h in range(4)], axis=0
    )


def split_dot(values, matrix):
    high = values.astype(jnp.bfloat16)
    low = (values - high.astype(jnp.float32)).astype(jnp.bfloat16)
    return dot(high, matrix) + dot(low, matrix)


def window(north_ref, south_ref, which):
    pieces = []
    for level in range(2):
        pieces.append(north_ref[which, level].reshape(48, 128))
        pieces.append(south_ref[which, level, 0:3].reshape(48, 128))
    return jnp.concatenate(pieces, axis=0)


def pack_kernel(lat_ref, w_ref, out_ref):
    first = lat_ref[0] * 6
    to = lax.broadcasted_iota(jnp.int32, (24, 24), 0)
    source = lax.broadcasted_iota(jnp.int32, (24, 24), 1)
    total = jnp.zeros((24, 384), jnp.float32)
    for part in range(4):
        pick = jnp.logical_and(to // 6 == part, source == first + to - part * 6)
        pick = jnp.where(pick, 1.0, 0.0).astype(jnp.bfloat16)
        total += dot(pick, w_ref[:, part * 384 : (part + 1) * 384])
    packed = total.astype(jnp.bfloat16)
    for z in range(NZ):
        out_ref[z] = packed


def bias_kernel(table_ref, open_ref, spread_ref, mask_ref, bias_ref, wide_ref):
    @pl.when(pl.program_id(0) == 0)
    def _():
        halves = []
        for half in range(2):
            pieces = []
            for a in range(ROWS):
                first = (a // 6 * 2 + half) * 828 + a % 6 * 138
                pieces.append(table_ref[0, :, first : first + 138])
            halves.append(split_dot(jnp.concatenate(pieces, axis=0), open_ref[half]))
        for s in range(3):
            wide_ref[s] = (halves[0] + halves[1])[:, s * 128 : (s + 1) * 128]

    first = pl.program_id(0) * 4
    pieces = []
    for s in range(3):
        table = jnp.concatenate(
            [wide_ref[s, pl.ds(first + h, ROWS, stride=HEADS), :] for h in range(4)], axis=0
        )
        table = jnp.broadcast_to(table[:, None, :], (4 * ROWS, PAD, 128))
        pieces.append(pltpu.roll(table, 0, 2, stride=1, stride_axis=1))
    wide = jnp.concatenate(pieces, axis=2).reshape(4 * TOK, WIDE)
    bias = split_dot(wide, spread_ref[...]).reshape(4, TOK, TOK) + mask_ref[...][None]
    bias_ref[0] = bias.reshape(4 * TOK, TOK)


def probs_kernel(north_ref, south_ref, bias_ref, p_ref):
    q_win, k_win = window(north_ref, south_ref, 0), window(north_ref, south_ref, 1)
    scores = dot(by_head(q_win), k_win, ((1,), (1,))) * score_factor + bias_ref[0]
    expon = jnp.exp(scores - jnp.max(scores, axis=-1, keepdims=True))
    p_ref[0] = expon * (1.0 / jnp.sum(expon, axis=-1, keepdims=True))


def norm_kernel(a_ref, b_ref, south_ref, quarter_ref, normed_ref, inverse_ref):
    pieces = []
    for level in range(2):
        pieces.append(a_ref[0, level].reshape(32, 768))
        pieces.append(b_ref[0, level].reshape(32, 768))
        pieces.append(south_ref[0, level].reshape(64, 768))
    fields = dot(quarter_ref[...], jnp.concatenate(pieces, axis=0))
    parts = [fields[q * 64 : (q + 1) * 64] for q in range(4)]
    mean = jnp.sum(parts[0] + parts[1] + parts[2] + parts[3], axis=-1, keepdims=True) / 3072
    parts = [part - mean for part in parts]
    squares = [part * part for part in parts]
    variance = (
        jnp.sum(squares[0] + squares[1] + squares[2] + squares[3], axis=-1, keepdims=True) / 3072
    )
    inverse = lax.rsqrt(variance + 1e-05)
    for q in range(4):
        normed_ref[q] = parts[q] * inverse
    inverse_ref[...] = jnp.broadcast_to(inverse, (64, 128))


def merge_kernel(spot_ref, near_ref, far_ref, w_ref, shuffle_ref, out_ref, acc_ref):
    weights = [dot(shuffle_ref[...], w_ref[y]).astype(jnp.bfloat16) for y in range(NY)]
    near, far = None, None
    for part in range(4):
        rows, columns = slice(part * 128, part * 128 + 128), slice(part * 384, part * 384 + 384)
        weight = jnp.concatenate([weights[y][rows] for y in range(NY)], axis=0)
        near_part = dot(near_ref[:, columns], weight, ((1,), (1,)))
        far_part = dot(far_ref[:, columns], weight, ((1,), (1,)))
        near = near_part if part == 0 else near + near_part
        far = far_part if part == 0 else far + far_part
    acc_ref[:192] = near
    acc_ref[192:] = far
    for x in range(NX):
        for l in range(LAT):
            for level in range(2):
                own = pl.multiple_of(spot_ref[x * LAT + l] + level * 24 + 8, 8)
                below = pl.multiple_of(spot_ref[x * LAT + (l + 1) % LAT] + level * 24, 8)
                out_ref[x * LAT + l, level * 32 : level * 32 + 16] = acc_ref[
                    pl.ds(own, 16)
                ].astype(jnp.bfloat16)
                out_ref[x * LAT + l, level * 32 + 16 : level * 32 + 32] = acc_ref[
                    pl.ds(below, 16)
                ].astype(jnp.bfloat16)


def scores_kernel(
    recv_ref,
    order_ref,
    normed_ref,
    inverse_ref,
    gain_ref,
    back_ref,
    sums_ref,
    north_ref,
    south_ref,
    p_ref,
    o_out_ref,
    d_ref,
    table_ref,
    o_ref,
    sum_ref,
):
    g = pl.program_id(0)

    @pl.when(g == 0)
    def _():
        pieces = [
            jnp.concatenate(
                [recv_ref[x * LAT + l, :, y * 128 : (y + 1) * 128] for l in range(LAT)], axis=1
            )
            for x in range(NX)
            for y in range(NY)
        ]
        d_norm = dot(jnp.concatenate(pieces, axis=0), order_ref[...])
        hats = []
        for q in range(4):
            left = d_norm[(2 * q) * 64 : (2 * q + 1) * 64]
            right = d_norm[(2 * q + 1) * 64 : (2 * q + 2) * 64]
            hats.append(jnp.concatenate([left, right], axis=1) * gain_ref[q])
        mean = jnp.sum(hats[0] + hats[1] + hats[2] + hats[3], axis=-1, keepdims=True) / 3072
        cross = [hats[q] * normed_ref[q] for q in range(4)]
        along = jnp.sum(cross[0] + cross[1] + cross[2] + cross[3], axis=-1, keepdims=True) / 3072
        inverse = inverse_ref[:, 0:1]
        stack = [(hats[q] - mean - normed_ref[q] * along) * inverse for q in range(4)]
        d_out = dot(back_ref[...], jnp.concatenate(stack, axis=0).astype(jnp.bfloat16))
        d_out = d_out.astype(jnp.bfloat16)
        for s in range(GROUPS):
            o_ref[s] = d_out[:, s * 128 : (s + 1) * 128]

    o_win = o_ref[g]
    o_out_ref[0] = o_win
    probs = p_ref[0]
    d_probs = dot(by_head(o_win), window(north_ref, south_ref, 0), ((1,), (1,)))
    delta = jnp.sum(probs * d_probs, axis=-1, keepdims=True)
    d_low = (probs * (d_probs - delta)).astype(jnp.bfloat16)
    d_ref[0] = d_low

    spread = dot(d_low, sums_ref[...]).reshape(4 * ROWS, PAD, WIDE)
    sums = [
        jnp.sum(
            pltpu.roll(spread[:, :, s * 128 : (s + 1) * 128], 0, 2, stride=1, stride_axis=1), axis=1
        )
        for s in range(3)
    ]
    sum_ref[g] = jnp.concatenate(sums, axis=1)

    @pl.when(g == GROUPS - 1)
    def _():
        whole = jnp.concatenate([sum_ref[s] for s in range(GROUPS)], axis=0)
        for part in range(16):
            table_ref[part, 0:18] = whole[part * 18 : (part + 1) * 18]
            table_ref[part, 18:24] = jnp.zeros((6, WIDE), jnp.float32)


def grads_kernel(north_ref, south_ref, o_ref, d_ref, p_ref, grads_ref):
    q_win, k_win = window(north_ref, south_ref, 0), window(north_ref, south_ref, 1)
    o_win = o_ref[0]
    d_low = d_ref[0]
    p_low = p_ref[0].astype(jnp.bfloat16)
    q_all = dot(d_low, k_win)
    q_grad = jnp.zeros((TOK, 128), jnp.float32)
    for h in range(4):
        q_grad = jnp.where(head_mask(h), q_all[h * TOK : (h + 1) * TOK], q_grad)
    grads_ref[0] = (q_grad * score_factor).astype(jnp.bfloat16)

    q_turn = q_win.astype(jnp.float32).T.astype(jnp.bfloat16)
    o_turn = o_win.astype(jnp.float32).T.astype(jnp.bfloat16)
    k_parts, v_parts = [], []
    for h in range(4):
        rows = slice(h * 32, (h + 1) * 32)
        k_parts.append(dot(q_turn[rows], d_low[h * TOK : (h + 1) * TOK]))
        v_parts.append(dot(o_turn[rows], p_low[h * TOK : (h + 1) * TOK]))
    k_grad = jnp.concatenate(k_parts, axis=0).T
    v_grad = jnp.concatenate(v_parts, axis=0).T
    grads_ref[1] = (k_grad * score_factor).astype(jnp.bfloat16)
    grads_ref[2] = v_grad.astype(jnp.bfloat16)


def whole_spec(shape):
    return pl.BlockSpec(shape, lambda *_: (0,) * len(shape))


def north_spec(first, count):
    return pl.BlockSpec((count, 2, 3, PAD, 128), lambda g: (first // count, 0, 1, 0, g))


def south_spec(first, count):
    return pl.BlockSpec((count, 2, 4, PAD, 128), lambda g: (first // count, 0, 0, 0, g))


def group_spec(rows, columns):
    return pl.BlockSpec((1, rows, columns), lambda g: (g, 0, 0))


params = pltpu.CompilerParams(vmem_limit_bytes=VMEM)
smem = pl.BlockSpec(memory_space=pltpu.SMEM)
vmem = pl.BlockSpec(memory_space=pltpu.VMEM)


def pack_weight(lat, weight):
    return pl.pallas_call(
        pack_kernel,
        in_specs=[smem, vmem],
        out_specs=vmem,
        out_shape=jax.ShapeDtypeStruct((NZ, 24, 384), jnp.bfloat16),
        compiler_params=params,
        name="pack_weight",
    )(lat, weight)


def window_bias(table, open_up, spread, mask):
    return pl.pallas_call(
        bias_kernel,
        grid=(GROUPS,),
        in_specs=[
            whole_spec((1, HEADS, 3312)),
            whole_spec((2, 138, WIDE)),
            whole_spec((WIDE, TOK)),
            whole_spec((TOK, TOK)),
        ],
        out_specs=group_spec(4 * TOK, TOK),
        out_shape=jax.ShapeDtypeStruct((GROUPS, 4 * TOK, TOK), jnp.float32),
        scratch_shapes=[pltpu.VMEM((3, ROWS * HEADS, 128), jnp.float32)],
        compiler_params=params,
        name="window_bias",
    )(table, open_up, spread, mask)


def window_probs(across, south, bias):
    return pl.pallas_call(
        probs_kernel,
        grid=(GROUPS,),
        in_specs=[north_spec(0, 2), south_spec(0, 2), group_spec(4 * TOK, TOK)],
        out_specs=group_spec(4 * TOK, TOK),
        out_shape=jax.ShapeDtypeStruct((GROUPS, 4 * TOK, TOK), jnp.float32),
        compiler_params=params,
        name="window_probs",
    )(across, south, bias)


def normalise(across, south, quarter):
    return pl.pallas_call(
        norm_kernel,
        grid=(1,),
        in_specs=[
            pl.BlockSpec((1, 2, 2, PAD, 768), lambda g: (3, 0, 1, 0, 0)),
            pl.BlockSpec((1, 2, 2, PAD, 768), lambda g: (3, 0, 2, 0, 0)),
            pl.BlockSpec((1, 2, 4, PAD, 768), lambda g: (3, 0, 0, 0, 0)),
            whole_spec((256, 256)),
        ],
        out_specs=(whole_spec((4, 64, 768)), whole_spec((64, 128))),
        out_shape=(
            jax.ShapeDtypeStruct((4, 64, 768), jnp.float32),
            jax.ShapeDtypeStruct((64, 128), jnp.float32),
        ),
        compiler_params=params,
        name="normalise",
    )(across, across, south, quarter)


def merge_product(spots, near, far, weight, shuffle):
    return pl.pallas_call(
        merge_kernel,
        in_specs=[smem, vmem, vmem, vmem, vmem],
        out_specs=vmem,
        out_shape=jax.ShapeDtypeStruct((8, 64, 512), jnp.bfloat16),
        scratch_shapes=[pltpu.VMEM((384, 512), jnp.float32)],
        compiler_params=params,
        name="merge_product",
    )(spots, near, far, weight, shuffle)


def score_grads(recv, order, normed, inverse, gain, back, sums, across, south, probs):
    return pl.pallas_call(
        scores_kernel,
        grid=(GROUPS,),
        in_specs=[
            whole_spec((8, 64, 512)),
            whole_spec((512, 384)),
            whole_spec((4, 64, 768)),
            whole_spec((64, 128)),
            whole_spec((4, 1, 768)),
            whole_spec((TOK, 256)),
            whole_spec((TOK, WIDE)),
            north_spec(2, 1),
            south_spec(2, 1),
            group_spec(4 * TOK, TOK),
        ],
        out_specs=(
            group_spec(TOK, 128),
            group_spec(4 * TOK, TOK),
            whole_spec((16, 24, WIDE)),
        ),
        out_shape=(
            jax.ShapeDtypeStruct((GROUPS, TOK, 128), jnp.bfloat16),
            jax.ShapeDtypeStruct((GROUPS, 4 * TOK, TOK), jnp.bfloat16),
            jax.ShapeDtypeStruct((16, 24, WIDE), jnp.float32),
        ),
        scratch_shapes=[
            pltpu.VMEM((GROUPS, TOK, 128), jnp.bfloat16),
            pltpu.VMEM((GROUPS, 4 * ROWS, WIDE), jnp.float32),
        ],
        compiler_params=params,
        name="score_grads",
    )(recv, order, normed, inverse, gain, back, sums, across, south, probs)


def window_grads(across, south, o_win, d_low, probs):
    return pl.pallas_call(
        grads_kernel,
        grid=(GROUPS,),
        in_specs=[
            north_spec(0, 2),
            south_spec(0, 2),
            group_spec(TOK, 128),
            group_spec(4 * TOK, TOK),
            group_spec(4 * TOK, TOK),
        ],
        out_specs=pl.BlockSpec((3, TOK, 128), lambda g: (0, 0, g)),
        out_shape=jax.ShapeDtypeStruct((3, TOK, 768), jnp.bfloat16),
        compiler_params=params,
        name="window_grads",
    )(across, south, o_win, d_low, probs)


def from_behind(shard, axis, by):
    size = lax.axis_size(axis)
    return lax.ppermute(shard, axis, [(i, (i + by) % size) for i in range(size)])


def partner(shard, axis, bit):
    return lax.ppermute(shard, axis, [(i, i ^ bit) for i in range(lax.axis_size(axis))])


def swap(shard, axis, groups):
    return lax.all_to_all(shard, axis, 0, 0, tiled=True, axis_index_groups=groups)


def share(shard, count, axis, groups):
    return swap(jnp.broadcast_to(shard[None], (count,) + shard.shape), axis, groups)


def on_device(y_block, merge_gain, merge_weight, d_merged, q_proj, k_proj, v_proj, bias_table):
    sums, spread, quarter, back, order, shuffle, open_up = layout_constants()
    lat = lax.axis_index("lat")

    packed = pack_weight(lat.reshape(1), merge_weight)

    tokens = jnp.arange(TOK, dtype=jnp.int32)
    upper = tokens // PAD % 6 >= 3
    allowed = jnp.logical_or(upper[:, None] == upper[None, :], lat != LAT - 1)
    allowed = jnp.logical_and(allowed, (tokens % PAD < 12)[None, :])
    mask = jnp.where(allowed, 0.0, LOW)

    packed, d_merged = lax.optimization_barrier((packed, d_merged))
    weight_z = swap(packed, "lon", z_groups).reshape(NZ * 24, 384)
    eastern_d = from_behind(d_merged[:, :, :3], "lon", -1)
    d_rows = jnp.concatenate(
        [d_merged[:, :, 3:], eastern_d, jnp.zeros_like(d_merged[:, :, :2])], axis=2
    ).reshape(48, -1)
    d_rows = jnp.concatenate([d_rows, partner(d_rows, "lat", 2)], axis=0)
    near = jnp.concatenate([d_rows, partner(d_rows, "lon", NY * NZ)], axis=0)
    far = partner(near, "lat", 1)
    me = (lax.axis_index("lon") // (NY * NZ)) * LAT + lat
    rel = jnp.bitwise_xor(jnp.arange(8, dtype=jnp.int32), me)
    spots = (rel % 2 * 4 + rel // 4 * 2 + rel // 2 % 2) * 48

    weight_z = jnp.broadcast_to(weight_z[None], (NY,) + weight_z.shape)
    weight_z, bias_table = lax.optimization_barrier((weight_z, bias_table))
    weight = swap(weight_z, "lon", y_groups)
    bias = window_bias(bias_table, open_up, spread, mask)

    eastern = from_behind(
        jnp.stack([q_proj[:, :, :6], k_proj[:, :, :6], v_proj[:, :, :6], y_block[:, :, :6]]),
        "lon",
        -1,
    )
    across = jnp.concatenate(
        [
            jnp.stack([q_proj[:, :, 6:], k_proj[:, :, 6:], v_proj[:, :, 6:], y_block[:, :, 6:]]),
            eastern,
            jnp.zeros_like(eastern[:, :, :, :4]),
        ],
        axis=3,
    )
    south = from_behind(across[:, :, :4], "lat", -1)

    normed, inverse = normalise(across, south, quarter)
    weight, bias, normed = lax.optimization_barrier((weight, bias, normed))
    parts = merge_product(spots, near, far, weight, shuffle)
    recv = swap(parts, ("lon", "lat"), x_lat_groups)

    bias, _ = lax.optimization_barrier((bias, parts))
    probs = window_probs(across, south, bias)

    o_win, d_low, table_part = score_grads(
        recv, order, normed, inverse, merge_gain.reshape(4, 1, 768), back, sums, across, south, probs
    )

    table_part = jnp.sum(swap(table_part, "lon", near_groups), axis=0).astype(jnp.bfloat16)
    grads = window_grads(across, south, o_win, d_low, probs)
    grid = grads.reshape(3, 2, 6, PAD, 768)[:, :, :, :12]
    southern = from_behind(grid[:, :, 3:], "lat", 1)
    fixed = jnp.concatenate([southern, grid[:, :, :3]], axis=2)

    table_part = share(table_part, NZ // 2, "lon", far_groups)
    table_part, fixed = lax.optimization_barrier((table_part, fixed))
    western = from_behind(fixed[:, :, :, 6:], "lon", 1)
    finished = jnp.concatenate([western, fixed[:, :, :, :6]], axis=3)

    table_part = jnp.sum(table_part.astype(jnp.float32), axis=0).astype(jnp.bfloat16)
    table_sum = share(table_part, 16, "lon", near_groups)[:, :18].astype(jnp.float32)
    table_sum = table_sum.reshape(HEADS, 2, 6, 2, 6, SEG)[..., :23].transpose(0, 1, 3, 2, 4, 5)
    table_grad = table_sum.reshape(bias_table.shape)
    return (finished[0], finished[1], finished[2], table_grad)


def solution(mesh):
    placed = (
        P(None, "lat", "lon", None),
        P(),
        P("lon", None),
        P(None, "lat", "lon", None),
        P(None, "lat", "lon", None),
        P(None, "lat", "lon", None),
        P(None, "lat", "lon", None),
        P("lat", None, None),
    )
    return jax.shard_map(
        on_device,
        mesh=mesh,
        in_specs=placed,
        out_specs=(
            P(None, "lat", "lon", None),
            P(None, "lat", "lon", None),
            P(None, "lat", "lon", None),
            P("lat", None, None),
        ),
        check_vma=False,
    )
```

```python
import jax
import jax.numpy as jnp
import numpy as np
from jax import lax
from jax.experimental import pallas as pl
from jax.experimental.pallas import tpu as pltpu
from jax.sharding import PartitionSpec as P

NX, NY, NZ = 2, 4, 16
LAT = 4
HEADS = 24
ROWS = 12
PAD = 16
TOK = ROWS * PAD
SEG = 32
WIDE = ROWS * SEG
GROUPS = 6
LOW = -1e30
VMEM = 56 * 1024 * 1024
score_factor = 32 ** (-0.5)

z_groups = [[a * NZ + z for z in range(NZ)] for a in range(NX * NY)]
y_groups = [[(x * NY + y) * NZ + z for y in range(NY)] for x in range(NX) for z in range(NZ)]
near_groups = [
    [a * NZ + 2 * pair + e for a in range(NX * NY) for e in range(2)] for pair in range(NZ // 2)
]
far_groups = [
    [a * NZ + 2 * pair + e for pair in range(NZ // 2)] for a in range(NX * NY) for e in range(2)
]
x_lat_groups = [
    [(x * NY * NZ + b) * LAT + l for x in range(NX) for l in range(LAT)] for b in range(NY * NZ)
]


def layout_constants():
    tokens = np.arange(TOK)
    row, col = tokens // PAD, tokens % PAD
    real = col < 12
    sums = np.zeros((TOK, WIDE), np.float32)
    sums[tokens[real], (row * SEG + 11 - col)[real]] = 1
    spread = np.zeros((WIDE, TOK), np.float32)
    spread[(row * SEG + 11 + col)[real], tokens[real]] = 1
    quarter = np.zeros((256, 256), np.float32)
    back = np.zeros((TOK, 256), np.float32)
    for level in range(2):
        for pr in range(4):
            for pc in range(6):
                for di in range(2):
                    for dj in range(2):
                        spot = (di + 2 * dj) * 64 + (level * 4 + pr) * 8 + pc
                        fine_row, fine_col = 2 * pr + di, 2 * pc + dj
                        quarter[spot, (level * 8 + fine_row) * PAD + fine_col] = 1
                        if 1 <= fine_row <= 6:
                            back[(level * 6 + fine_row - 1) * PAD + fine_col, spot] = 1
    shuffle = np.zeros((512, 384), np.float32)
    order = np.zeros((512, 384), np.float32)
    for l in range(4):
        for z in range(NZ):
            for i in range(6):
                shuffle[l * 128 + z * 6 + i, z * 24 + l * 6 + i] = 1
                order[l * 128 + z * 6 + i, z * 24 + l * 6 + i] = 1
    open_up = np.zeros((2, 138, WIDE), np.float32)
    for half in range(2):
        for r in range(6):
            for d in range(23):
                open_up[half, r * 23 + d, half * 192 + r * SEG + 22 - d] = 1
    all_of = (sums, spread, quarter, back, order, shuffle, open_up)
    return [jnp.asarray(a, jnp.bfloat16) for a in all_of]


def dot(a, b, dims=((1,), (0,))):
    return lax.dot_general(a, b, (dims, ((), ())), preferred_element_type=jnp.float32)


def head_mask(h):
    lanes = lax.broadcasted_iota(jnp.int32, (1, 128), 1)
    return (lanes // 32) == h


def by_head(block):
    return jnp.concatenate(
        [jnp.where(head_mask(h), block, jnp.zeros_like(block)) for h in range(4)], axis=0
    )


def split_dot(values, matrix):
    high = values.astype(jnp.bfloat16)
    low = (values - high.astype(jnp.float32)).astype(jnp.bfloat16)
    return dot(high, matrix) + dot(low, matrix)


def window(north_ref, south_ref, which):
    pieces = []
    for level in range(2):
        pieces.append(north_ref[which, level].reshape(48, 128))
        pieces.append(south_ref[which, level, 0:3].reshape(48, 128))
    return jnp.concatenate(pieces, axis=0)


def pack_kernel(lat_ref, w_ref, out_ref):
    first = lat_ref[0] * 6
    to = lax.broadcasted_iota(jnp.int32, (24, 24), 0)
    source = lax.broadcasted_iota(jnp.int32, (24, 24), 1)
    total = jnp.zeros((24, 384), jnp.float32)
    for part in range(4):
        pick = jnp.logical_and(to // 6 == part, source == first + to - part * 6)
        pick = jnp.where(pick, 1.0, 0.0).astype(jnp.bfloat16)
        total += dot(pick, w_ref[:, part * 384 : (part + 1) * 384])
    packed = total.astype(jnp.bfloat16)
    for z in range(NZ):
        out_ref[z] = packed


def open_kernel(table_ref, open_ref, out_ref, wide_ref):
    halves = []
    for half in range(2):
        pieces = []
        for a in range(ROWS):
            first = (a // 6 * 2 + half) * 828 + a % 6 * 138
            pieces.append(table_ref[0, :, first : first + 138])
        halves.append(split_dot(jnp.concatenate(pieces, axis=0), open_ref[half]))
    whole = halves[0] + halves[1]
    for s in range(3):
        wide_ref[s] = whole[:, s * 128 : (s + 1) * 128]
    for head in range(HEADS):
        row = head % 4 * ROWS
        for s in range(3):
            out_ref[head // 4, row : row + ROWS, s * 128 : (s + 1) * 128] = wide_ref[
                s, pl.ds(head, ROWS, stride=HEADS), :
            ]


def probs_kernel(north_ref, south_ref, table_ref, spread_ref, mask_ref, p_ref):
    pieces = []
    for s in range(3):
        table = table_ref[0, :, s * 128 : (s + 1) * 128]
        table = jnp.broadcast_to(table[:, None, :], (4 * ROWS, PAD, 128))
        pieces.append(pltpu.roll(table, 0, 2, stride=1, stride_axis=1))
    wide = jnp.concatenate(pieces, axis=2).reshape(4 * TOK, WIDE)
    q_win, k_win = window(north_ref, south_ref, 0), window(north_ref, south_ref, 1)
    scores = dot(by_head(q_win), k_win, ((1,), (1,))) * score_factor
    scores = scores + split_dot(wide, spread_ref[...])
    scores = (scores.reshape(4, TOK, TOK) + mask_ref[...][None]).reshape(4 * TOK, TOK)
    expon = jnp.exp(scores - jnp.max(scores, axis=-1, keepdims=True))
    p_ref[0] = expon * (1.0 / jnp.sum(expon, axis=-1, keepdims=True))


def norm_kernel(a_ref, b_ref, south_ref, quarter_ref, normed_ref, inverse_ref):
    pieces = []
    for level in range(2):
        pieces.append(a_ref[0, level].reshape(32, 768))
        pieces.append(b_ref[0, level].reshape(32, 768))
        pieces.append(south_ref[0, level].reshape(64, 768))
    fields = dot(quarter_ref[...], jnp.concatenate(pieces, axis=0))
    parts = [fields[q * 64 : (q + 1) * 64] for q in range(4)]
    mean = jnp.sum(parts[0] + parts[1] + parts[2] + parts[3], axis=-1, keepdims=True) / 3072
    parts = [part - mean for part in parts]
    squares = [part * part for part in parts]
    variance = (
        jnp.sum(squares[0] + squares[1] + squares[2] + squares[3], axis=-1, keepdims=True) / 3072
    )
    inverse = lax.rsqrt(variance + 1e-05)
    for q in range(4):
        normed_ref[q] = parts[q] * inverse
    inverse_ref[...] = jnp.broadcast_to(inverse, (64, 128))


def merge_kernel(spot_ref, near_ref, far_ref, w_ref, shuffle_ref, out_ref, acc_ref):
    weights = [dot(shuffle_ref[...], w_ref[y]).astype(jnp.bfloat16) for y in range(NY)]
    near, far = None, None
    for part in range(4):
        rows, columns = slice(part * 128, part * 128 + 128), slice(part * 384, part * 384 + 384)
        weight = jnp.concatenate([weights[y][rows] for y in range(NY)], axis=0)
        near_part = dot(near_ref[:, columns], weight, ((1,), (1,)))
        far_part = dot(far_ref[:, columns], weight, ((1,), (1,)))
        near = near_part if part == 0 else near + near_part
        far = far_part if part == 0 else far + far_part
    acc_ref[:192] = near
    acc_ref[192:] = far
    for x in range(NX):
        for l in range(LAT):
            for level in range(2):
                own = pl.multiple_of(spot_ref[x * LAT + l] + level * 24 + 8, 8)
                below = pl.multiple_of(spot_ref[x * LAT + (l + 1) % LAT] + level * 24, 8)
                out_ref[x * LAT + l, level * 32 : level * 32 + 16] = acc_ref[
                    pl.ds(own, 16)
                ].astype(jnp.bfloat16)
                out_ref[x * LAT + l, level * 32 + 16 : level * 32 + 32] = acc_ref[
                    pl.ds(below, 16)
                ].astype(jnp.bfloat16)


def scores_kernel(
    recv_ref,
    order_ref,
    normed_ref,
    inverse_ref,
    gain_ref,
    back_ref,
    sums_ref,
    north_ref,
    south_ref,
    p_ref,
    o_out_ref,
    d_ref,
    table_ref,
    o_ref,
    sum_ref,
):
    g = pl.program_id(0)

    @pl.when(g == 0)
    def _():
        pieces = [
            jnp.concatenate(
                [recv_ref[x * LAT + l, :, y * 128 : (y + 1) * 128] for l in range(LAT)], axis=1
            )
            for x in range(NX)
            for y in range(NY)
        ]
        d_norm = dot(jnp.concatenate(pieces, axis=0), order_ref[...])
        hats = []
        for q in range(4):
            left = d_norm[(2 * q) * 64 : (2 * q + 1) * 64]
            right = d_norm[(2 * q + 1) * 64 : (2 * q + 2) * 64]
            hats.append(jnp.concatenate([left, right], axis=1) * gain_ref[q])
        mean = jnp.sum(hats[0] + hats[1] + hats[2] + hats[3], axis=-1, keepdims=True) / 3072
        cross = [hats[q] * normed_ref[q] for q in range(4)]
        along = jnp.sum(cross[0] + cross[1] + cross[2] + cross[3], axis=-1, keepdims=True) / 3072
        inverse = inverse_ref[:, 0:1]
        stack = [(hats[q] - mean - normed_ref[q] * along) * inverse for q in range(4)]
        d_out = dot(back_ref[...], jnp.concatenate(stack, axis=0).astype(jnp.bfloat16))
        d_out = d_out.astype(jnp.bfloat16)
        for s in range(GROUPS):
            o_ref[s] = d_out[:, s * 128 : (s + 1) * 128]

    o_win = o_ref[g]
    o_out_ref[0] = o_win
    probs = p_ref[0]
    d_probs = dot(by_head(o_win), window(north_ref, south_ref, 0), ((1,), (1,)))
    delta = jnp.sum(probs * d_probs, axis=-1, keepdims=True)
    d_low = (probs * (d_probs - delta)).astype(jnp.bfloat16)
    d_ref[0] = d_low

    spread = dot(d_low, sums_ref[...]).reshape(4 * ROWS, PAD, WIDE)
    sums = [
        jnp.sum(
            pltpu.roll(spread[:, :, s * 128 : (s + 1) * 128], 0, 2, stride=1, stride_axis=1), axis=1
        )
        for s in range(3)
    ]
    sum_ref[g] = jnp.concatenate(sums, axis=1)

    @pl.when(g == GROUPS - 1)
    def _():
        whole = jnp.concatenate([sum_ref[s] for s in range(GROUPS)], axis=0)
        for part in range(16):
            table_ref[part, 0:18] = whole[part * 18 : (part + 1) * 18]
            table_ref[part, 18:24] = jnp.zeros((6, WIDE), jnp.float32)


def grads_kernel(north_ref, south_ref, o_ref, d_ref, p_ref, grads_ref):
    q_win, k_win = window(north_ref, south_ref, 0), window(north_ref, south_ref, 1)
    o_win = o_ref[0]
    d_low = d_ref[0]
    p_low = p_ref[0].astype(jnp.bfloat16)
    q_all = dot(d_low, k_win)
    q_grad = jnp.zeros((TOK, 128), jnp.float32)
    for h in range(4):
        q_grad = jnp.where(head_mask(h), q_all[h * TOK : (h + 1) * TOK], q_grad)
    grads_ref[0] = (q_grad * score_factor).astype(jnp.bfloat16)

    q_turn = q_win.astype(jnp.float32).T.astype(jnp.bfloat16)
    o_turn = o_win.astype(jnp.float32).T.astype(jnp.bfloat16)
    k_parts, v_parts = [], []
    for h in range(4):
        rows = slice(h * 32, (h + 1) * 32)
        k_parts.append(dot(q_turn[rows], d_low[h * TOK : (h + 1) * TOK]))
        v_parts.append(dot(o_turn[rows], p_low[h * TOK : (h + 1) * TOK]))
    k_grad = jnp.concatenate(k_parts, axis=0).T
    v_grad = jnp.concatenate(v_parts, axis=0).T
    grads_ref[1] = (k_grad * score_factor).astype(jnp.bfloat16)
    grads_ref[2] = v_grad.astype(jnp.bfloat16)


def whole_spec(shape):
    return pl.BlockSpec(shape, lambda *_: (0,) * len(shape))


def north_spec(first, count):
    return pl.BlockSpec((count, 2, 3, PAD, 128), lambda g: (first // count, 0, 1, 0, g))


def south_spec(first, count):
    return pl.BlockSpec((count, 2, 4, PAD, 128), lambda g: (first // count, 0, 0, 0, g))


def group_spec(rows, columns):
    return pl.BlockSpec((1, rows, columns), lambda g: (g, 0, 0))


params = pltpu.CompilerParams(vmem_limit_bytes=VMEM)
smem = pl.BlockSpec(memory_space=pltpu.SMEM)
vmem = pl.BlockSpec(memory_space=pltpu.VMEM)


def pack_weight(lat, weight):
    return pl.pallas_call(
        pack_kernel,
        in_specs=[smem, vmem],
        out_specs=vmem,
        out_shape=jax.ShapeDtypeStruct((NZ, 24, 384), jnp.bfloat16),
        compiler_params=params,
        name="pack_weight",
    )(lat, weight)


def open_table(table, open_up):
    return pl.pallas_call(
        open_kernel,
        in_specs=[vmem, vmem],
        out_specs=vmem,
        out_shape=jax.ShapeDtypeStruct((GROUPS, 4 * ROWS, WIDE), jnp.float32),
        scratch_shapes=[pltpu.VMEM((3, ROWS * HEADS, 128), jnp.float32)],
        compiler_params=params,
        name="open_table",
    )(table, open_up)


def window_probs(across, south, table, spread, mask):
    return pl.pallas_call(
        probs_kernel,
        grid=(GROUPS,),
        in_specs=[
            north_spec(0, 2),
            south_spec(0, 2),
            group_spec(4 * ROWS, WIDE),
            whole_spec((WIDE, TOK)),
            whole_spec((TOK, TOK)),
        ],
        out_specs=group_spec(4 * TOK, TOK),
        out_shape=jax.ShapeDtypeStruct((GROUPS, 4 * TOK, TOK), jnp.float32),
        compiler_params=params,
        name="window_probs",
    )(across, south, table, spread, mask)


def normalise(across, south, quarter):
    return pl.pallas_call(
        norm_kernel,
        grid=(1,),
        in_specs=[
            pl.BlockSpec((1, 2, 2, PAD, 768), lambda g: (3, 0, 1, 0, 0)),
            pl.BlockSpec((1, 2, 2, PAD, 768), lambda g: (3, 0, 2, 0, 0)),
            pl.BlockSpec((1, 2, 4, PAD, 768), lambda g: (3, 0, 0, 0, 0)),
            whole_spec((256, 256)),
        ],
        out_specs=(whole_spec((4, 64, 768)), whole_spec((64, 128))),
        out_shape=(
            jax.ShapeDtypeStruct((4, 64, 768), jnp.float32),
            jax.ShapeDtypeStruct((64, 128), jnp.float32),
        ),
        compiler_params=params,
        name="normalise",
    )(across, across, south, quarter)


def merge_product(spots, near, far, weight, shuffle):
    return pl.pallas_call(
        merge_kernel,
        in_specs=[smem, vmem, vmem, vmem, vmem],
        out_specs=vmem,
        out_shape=jax.ShapeDtypeStruct((8, 64, 512), jnp.bfloat16),
        scratch_shapes=[pltpu.VMEM((384, 512), jnp.float32)],
        compiler_params=params,
        name="merge_product",
    )(spots, near, far, weight, shuffle)


def score_grads(recv, order, normed, inverse, gain, back, sums, across, south, probs):
    return pl.pallas_call(
        scores_kernel,
        grid=(GROUPS,),
        in_specs=[
            whole_spec((8, 64, 512)),
            whole_spec((512, 384)),
            whole_spec((4, 64, 768)),
            whole_spec((64, 128)),
            whole_spec((4, 1, 768)),
            whole_spec((TOK, 256)),
            whole_spec((TOK, WIDE)),
            north_spec(2, 1),
            south_spec(2, 1),
            group_spec(4 * TOK, TOK),
        ],
        out_specs=(
            group_spec(TOK, 128),
            group_spec(4 * TOK, TOK),
            whole_spec((16, 24, WIDE)),
        ),
        out_shape=(
            jax.ShapeDtypeStruct((GROUPS, TOK, 128), jnp.bfloat16),
            jax.ShapeDtypeStruct((GROUPS, 4 * TOK, TOK), jnp.bfloat16),
            jax.ShapeDtypeStruct((16, 24, WIDE), jnp.float32),
        ),
        scratch_shapes=[
            pltpu.VMEM((GROUPS, TOK, 128), jnp.bfloat16),
            pltpu.VMEM((GROUPS, 4 * ROWS, WIDE), jnp.float32),
        ],
        compiler_params=params,
        name="score_grads",
    )(recv, order, normed, inverse, gain, back, sums, across, south, probs)


def window_grads(across, south, o_win, d_low, probs):
    return pl.pallas_call(
        grads_kernel,
        grid=(GROUPS,),
        in_specs=[
            north_spec(0, 2),
            south_spec(0, 2),
            group_spec(TOK, 128),
            group_spec(4 * TOK, TOK),
            group_spec(4 * TOK, TOK),
        ],
        out_specs=pl.BlockSpec((3, TOK, 128), lambda g: (0, 0, g)),
        out_shape=jax.ShapeDtypeStruct((3, TOK, 768), jnp.bfloat16),
        compiler_params=params,
        name="window_grads",
    )(across, south, o_win, d_low, probs)


def from_behind(shard, axis, by):
    size = lax.axis_size(axis)
    return lax.ppermute(shard, axis, [(i, (i + by) % size) for i in range(size)])


def partner(shard, axis, bit):
    return lax.ppermute(shard, axis, [(i, i ^ bit) for i in range(lax.axis_size(axis))])


def swap(shard, axis, groups):
    return lax.all_to_all(shard, axis, 0, 0, tiled=True, axis_index_groups=groups)


def share(shard, count, axis, groups):
    return swap(jnp.broadcast_to(shard[None], (count,) + shard.shape), axis, groups)


def on_device(y_block, merge_gain, merge_weight, d_merged, q_proj, k_proj, v_proj, bias_table):
    sums, spread, quarter, back, order, shuffle, open_up = layout_constants()
    lat = lax.axis_index("lat")

    packed = pack_weight(lat.reshape(1), merge_weight)

    tokens = jnp.arange(TOK, dtype=jnp.int32)
    upper = tokens // PAD % 6 >= 3
    allowed = jnp.logical_or(upper[:, None] == upper[None, :], lat != LAT - 1)
    allowed = jnp.logical_and(allowed, (tokens % PAD < 12)[None, :])
    mask = jnp.where(allowed, 0.0, LOW)

    packed, d_merged = lax.optimization_barrier((packed, d_merged))
    weight_z = swap(packed, "lon", z_groups).reshape(NZ * 24, 384)
    eastern_d = from_behind(d_merged[:, :, :3], "lon", -1)
    d_rows = jnp.concatenate(
        [d_merged[:, :, 3:], eastern_d, jnp.zeros_like(d_merged[:, :, :2])], axis=2
    ).reshape(48, -1)
    d_rows = jnp.concatenate([d_rows, partner(d_rows, "lat", 2)], axis=0)
    near = jnp.concatenate([d_rows, partner(d_rows, "lon", NY * NZ)], axis=0)
    far = partner(near, "lat", 1)
    me = (lax.axis_index("lon") // (NY * NZ)) * LAT + lat
    rel = jnp.bitwise_xor(jnp.arange(8, dtype=jnp.int32), me)
    spots = (rel % 2 * 4 + rel // 4 * 2 + rel // 2 % 2) * 48

    weight = share(weight_z, NY, "lon", y_groups)
    table = open_table(bias_table, open_up)

    eastern = from_behind(
        jnp.stack([q_proj[:, :, :6], k_proj[:, :, :6], v_proj[:, :, :6], y_block[:, :, :6]]),
        "lon",
        -1,
    )
    across = jnp.concatenate(
        [
            jnp.stack([q_proj[:, :, 6:], k_proj[:, :, 6:], v_proj[:, :, 6:], y_block[:, :, 6:]]),
            eastern,
            jnp.zeros_like(eastern[:, :, :, :4]),
        ],
        axis=3,
    )
    south = from_behind(across[:, :, :4], "lat", -1)

    normed, inverse = normalise(across, south, quarter)
    weight, table, mask, normed = lax.optimization_barrier((weight, table, mask, normed))
    parts = merge_product(spots, near, far, weight, shuffle)
    recv = swap(parts, ("lon", "lat"), x_lat_groups)

    table, _ = lax.optimization_barrier((table, parts))
    probs = window_probs(across, south, table, spread, mask)

    o_win, d_low, table_part = score_grads(
        recv, order, normed, inverse, merge_gain.reshape(4, 1, 768), back, sums, across, south, probs
    )

    table_part = jnp.sum(swap(table_part, "lon", near_groups), axis=0).astype(jnp.bfloat16)
    grads = window_grads(across, south, o_win, d_low, probs)
    grid = grads.reshape(3, 2, 6, PAD, 768)[:, :, :, :12]
    southern = from_behind(grid[:, :, 3:], "lat", 1)
    fixed = jnp.concatenate([southern, grid[:, :, :3]], axis=2)

    table_part = share(table_part, NZ // 2, "lon", far_groups)
    table_part, fixed = lax.optimization_barrier((table_part, fixed))
    western = from_behind(fixed[:, :, :, 6:], "lon", 1)
    finished = jnp.concatenate([western, fixed[:, :, :, :6]], axis=3)

    table_part = jnp.sum(table_part.astype(jnp.float32), axis=0).astype(jnp.bfloat16)
    table_sum = share(table_part, 16, "lon", near_groups)[:, :18].astype(jnp.float32)
    table_sum = table_sum.reshape(HEADS, 2, 6, 2, 6, SEG)[..., :23].transpose(0, 1, 3, 2, 4, 5)
    table_grad = table_sum.reshape(bias_table.shape)
    return (finished[0], finished[1], finished[2], table_grad)


def solution(mesh):
    placed = (
        P(None, "lat", "lon", None),
        P(),
        P("lon", None),
        P(None, "lat", "lon", None),
        P(None, "lat", "lon", None),
        P(None, "lat", "lon", None),
        P(None, "lat", "lon", None),
        P("lat", None, None),
    )
    return jax.shard_map(
        on_device,
        mesh=mesh,
        in_specs=placed,
        out_specs=(
            P(None, "lat", "lon", None),
            P(None, "lat", "lon", None),
            P(None, "lat", "lon", None),
            P("lat", None, None),
        ),
        check_vma=False,
    )
```

```python
import jax
import jax.numpy as jnp
import numpy as np
from jax import lax
from jax.experimental import pallas as pl
from jax.experimental.pallas import tpu as pltpu
from jax.sharding import PartitionSpec as P

NX, NY, NZ = 2, 4, 16
LAT = 4
HEADS = 24
ROWS = 12
PAD = 16
TOK = ROWS * PAD
SEG = 32
WIDE = ROWS * SEG
GROUPS = 6
LOW = -1e30
VMEM = 12 * 1024 * 1024
score_factor = 32 ** (-0.5)

z_groups = [[a * NZ + z for z in range(NZ)] for a in range(NX * NY)]
y_groups = [[(x * NY + y) * NZ + z for y in range(NY)] for x in range(NX) for z in range(NZ)]
near_groups = [
    [a * NZ + 2 * pair + e for a in range(NX * NY) for e in range(2)] for pair in range(NZ // 2)
]
far_groups = [
    [a * NZ + 2 * pair + e for pair in range(NZ // 2)] for a in range(NX * NY) for e in range(2)
]
x_lat_groups = [
    [(x * NY * NZ + b) * LAT + l for x in range(NX) for l in range(LAT)] for b in range(NY * NZ)
]


def layout_constants():
    tokens = np.arange(TOK)
    row, col = tokens // PAD, tokens % PAD
    real = col < 12
    sums = np.zeros((TOK, WIDE), np.float32)
    sums[tokens[real], (row * SEG + 11 - col)[real]] = 1
    spread = np.zeros((WIDE, TOK), np.float32)
    spread[(row * SEG + 11 + col)[real], tokens[real]] = 1
    quarter = np.zeros((256, 256), np.float32)
    back = np.zeros((TOK, 256), np.float32)
    for level in range(2):
        for pr in range(4):
            for pc in range(6):
                for di in range(2):
                    for dj in range(2):
                        spot = (di + 2 * dj) * 64 + (level * 4 + pr) * 8 + pc
                        fine_row, fine_col = 2 * pr + di, 2 * pc + dj
                        quarter[spot, (level * 8 + fine_row) * PAD + fine_col] = 1
                        if 1 <= fine_row <= 6:
                            back[(level * 6 + fine_row - 1) * PAD + fine_col, spot] = 1
    shuffle = np.zeros((512, 384), np.float32)
    order = np.zeros((512, 384), np.float32)
    for l in range(4):
        for z in range(NZ):
            for i in range(6):
                shuffle[l * 128 + z * 6 + i, z * 24 + l * 6 + i] = 1
                order[l * 128 + z * 6 + i, z * 24 + l * 6 + i] = 1
    open_up = np.zeros((2, 138, WIDE), np.float32)
    for half in range(2):
        for r in range(6):
            for d in range(23):
                open_up[half, r * 23 + d, half * 192 + r * SEG + 22 - d] = 1
    all_of = (sums, spread, quarter, back, order, shuffle, open_up)
    return [jnp.asarray(a, jnp.bfloat16) for a in all_of]


def dot(a, b, dims=((1,), (0,))):
    return lax.dot_general(a, b, (dims, ((), ())), preferred_element_type=jnp.float32)


def head_mask(h):
    lanes = lax.broadcasted_iota(jnp.int32, (1, 128), 1)
    return (lanes // 32) == h


def by_head(block):
    return jnp.concatenate(
        [jnp.where(head_mask(h), block, jnp.zeros_like(block)) for h in range(4)], axis=0
    )


def split_dot(values, matrix):
    high = values.astype(jnp.bfloat16)
    low = (values - high.astype(jnp.float32)).astype(jnp.bfloat16)
    return dot(high, matrix) + dot(low, matrix)


def window(north_ref, south_ref, which):
    pieces = []
    for level in range(2):
        pieces.append(north_ref[which, level].reshape(48, 128))
        pieces.append(south_ref[which, level, 0:3].reshape(48, 128))
    return jnp.concatenate(pieces, axis=0)


def pack_kernel(lat_ref, w_ref, out_ref):
    first = lat_ref[0] * 6
    to = lax.broadcasted_iota(jnp.int32, (24, 24), 0)
    source = lax.broadcasted_iota(jnp.int32, (24, 24), 1)
    total = jnp.zeros((24, 384), jnp.float32)
    for part in range(4):
        pick = jnp.logical_and(to // 6 == part, source == first + to - part * 6)
        pick = jnp.where(pick, 1.0, 0.0).astype(jnp.bfloat16)
        total += dot(pick, w_ref[:, part * 384 : (part + 1) * 384])
    packed = total.astype(jnp.bfloat16)
    for z in range(NZ):
        out_ref[z] = packed


def open_kernel(table_ref, open_ref, out_ref, wide_ref):
    halves = []
    for half in range(2):
        pieces = []
        for a in range(ROWS):
            first = (a // 6 * 2 + half) * 828 + a % 6 * 138
            pieces.append(table_ref[0, :, first : first + 138])
        halves.append(split_dot(jnp.concatenate(pieces, axis=0), open_ref[half]))
    whole = halves[0] + halves[1]
    for s in range(3):
        wide_ref[s] = whole[:, s * 128 : (s + 1) * 128]
    for head in range(HEADS):
        row = head % 4 * ROWS
        for s in range(3):
            out_ref[head // 4, row : row + ROWS, s * 128 : (s + 1) * 128] = wide_ref[
                s, pl.ds(head, ROWS, stride=HEADS), :
            ]


def probs_kernel(north_ref, south_ref, table_ref, spread_ref, mask_ref, p_ref):
    pieces = []
    for s in range(3):
        table = table_ref[0, :, s * 128 : (s + 1) * 128]
        table = jnp.broadcast_to(table[:, None, :], (4 * ROWS, PAD, 128))
        pieces.append(pltpu.roll(table, 0, 2, stride=1, stride_axis=1))
    wide = jnp.concatenate(pieces, axis=2).reshape(4 * TOK, WIDE)
    q_win, k_win = window(north_ref, south_ref, 0), window(north_ref, south_ref, 1)
    scores = dot(by_head(q_win), k_win, ((1,), (1,))) * score_factor
    scores = scores + split_dot(wide, spread_ref[...])
    scores = (scores.reshape(4, TOK, TOK) + mask_ref[...][None]).reshape(4 * TOK, TOK)
    expon = jnp.exp(scores - jnp.max(scores, axis=-1, keepdims=True))
    p_ref[0] = expon * (1.0 / jnp.sum(expon, axis=-1, keepdims=True))


def norm_kernel(a_ref, b_ref, south_ref, quarter_ref, normed_ref, inverse_ref):
    pieces = []
    for level in range(2):
        pieces.append(a_ref[0, level].reshape(32, 768))
        pieces.append(b_ref[0, level].reshape(32, 768))
        pieces.append(south_ref[0, level].reshape(64, 768))
    fields = dot(quarter_ref[...], jnp.concatenate(pieces, axis=0))
    parts = [fields[q * 64 : (q + 1) * 64] for q in range(4)]
    mean = jnp.sum(parts[0] + parts[1] + parts[2] + parts[3], axis=-1, keepdims=True) / 3072
    parts = [part - mean for part in parts]
    squares = [part * part for part in parts]
    variance = (
        jnp.sum(squares[0] + squares[1] + squares[2] + squares[3], axis=-1, keepdims=True) / 3072
    )
    inverse = lax.rsqrt(variance + 1e-05)
    for q in range(4):
        normed_ref[q] = parts[q] * inverse
    inverse_ref[...] = jnp.broadcast_to(inverse, (64, 128))


def merge_kernel(spot_ref, near_ref, far_ref, w_ref, shuffle_ref, out_ref, acc_ref):
    weights = [dot(shuffle_ref[...], w_ref[y]).astype(jnp.bfloat16) for y in range(NY)]
    near, far = None, None
    for part in range(4):
        rows, columns = slice(part * 128, part * 128 + 128), slice(part * 384, part * 384 + 384)
        weight = jnp.concatenate([weights[y][rows] for y in range(NY)], axis=0)
        near_part = dot(near_ref[:, columns], weight, ((1,), (1,)))
        far_part = dot(far_ref[:, columns], weight, ((1,), (1,)))
        near = near_part if part == 0 else near + near_part
        far = far_part if part == 0 else far + far_part
    acc_ref[:192] = near
    acc_ref[192:] = far
    for x in range(NX):
        for l in range(LAT):
            for level in range(2):
                own = pl.multiple_of(spot_ref[x * LAT + l] + level * 24 + 8, 8)
                below = pl.multiple_of(spot_ref[x * LAT + (l + 1) % LAT] + level * 24, 8)
                out_ref[x * LAT + l, level * 32 : level * 32 + 16] = acc_ref[
                    pl.ds(own, 16)
                ].astype(jnp.bfloat16)
                out_ref[x * LAT + l, level * 32 + 16 : level * 32 + 32] = acc_ref[
                    pl.ds(below, 16)
                ].astype(jnp.bfloat16)


def scores_kernel(
    recv_ref,
    order_ref,
    normed_ref,
    inverse_ref,
    gain_ref,
    back_ref,
    sums_ref,
    north_ref,
    south_ref,
    p_ref,
    o_out_ref,
    d_ref,
    table_ref,
    o_ref,
    sum_ref,
):
    g = pl.program_id(0)

    @pl.when(g == 0)
    def _():
        pieces = [
            jnp.concatenate(
                [recv_ref[x * LAT + l, :, y * 128 : (y + 1) * 128] for l in range(LAT)], axis=1
            )
            for x in range(NX)
            for y in range(NY)
        ]
        d_norm = dot(jnp.concatenate(pieces, axis=0), order_ref[...])
        hats = []
        for q in range(4):
            left = d_norm[(2 * q) * 64 : (2 * q + 1) * 64]
            right = d_norm[(2 * q + 1) * 64 : (2 * q + 2) * 64]
            hats.append(jnp.concatenate([left, right], axis=1) * gain_ref[q])
        mean = jnp.sum(hats[0] + hats[1] + hats[2] + hats[3], axis=-1, keepdims=True) / 3072
        cross = [hats[q] * normed_ref[q] for q in range(4)]
        along = jnp.sum(cross[0] + cross[1] + cross[2] + cross[3], axis=-1, keepdims=True) / 3072
        inverse = inverse_ref[:, 0:1]
        stack = [(hats[q] - mean - normed_ref[q] * along) * inverse for q in range(4)]
        d_out = dot(back_ref[...], jnp.concatenate(stack, axis=0).astype(jnp.bfloat16))
        d_out = d_out.astype(jnp.bfloat16)
        for s in range(GROUPS):
            o_ref[s] = d_out[:, s * 128 : (s + 1) * 128]

    o_win = o_ref[g]
    o_out_ref[0] = o_win
    probs = p_ref[0]
    d_probs = dot(by_head(o_win), window(north_ref, south_ref, 0), ((1,), (1,)))
    delta = jnp.sum(probs * d_probs, axis=-1, keepdims=True)
    d_low = (probs * (d_probs - delta)).astype(jnp.bfloat16)
    d_ref[0] = d_low

    spread = dot(d_low, sums_ref[...]).reshape(4 * ROWS, PAD, WIDE)
    sums = [
        jnp.sum(
            pltpu.roll(spread[:, :, s * 128 : (s + 1) * 128], 0, 2, stride=1, stride_axis=1), axis=1
        )
        for s in range(3)
    ]
    sum_ref[g] = jnp.concatenate(sums, axis=1)

    @pl.when(g == GROUPS - 1)
    def _():
        whole = jnp.concatenate([sum_ref[s] for s in range(GROUPS)], axis=0)
        for part in range(16):
            table_ref[part, 0:18] = whole[part * 18 : (part + 1) * 18]
            table_ref[part, 18:24] = jnp.zeros((6, WIDE), jnp.float32)


def grads_kernel(north_ref, south_ref, o_ref, d_ref, p_ref, grads_ref):
    q_win, k_win = window(north_ref, south_ref, 0), window(north_ref, south_ref, 1)
    o_win = o_ref[0]
    d_low = d_ref[0]
    p_low = p_ref[0].astype(jnp.bfloat16)
    q_all = dot(d_low, k_win)
    q_grad = jnp.zeros((TOK, 128), jnp.float32)
    for h in range(4):
        q_grad = jnp.where(head_mask(h), q_all[h * TOK : (h + 1) * TOK], q_grad)
    grads_ref[0] = (q_grad * score_factor).astype(jnp.bfloat16)

    q_turn = q_win.astype(jnp.float32).T.astype(jnp.bfloat16)
    o_turn = o_win.astype(jnp.float32).T.astype(jnp.bfloat16)
    k_parts, v_parts = [], []
    for h in range(4):
        rows = slice(h * 32, (h + 1) * 32)
        k_parts.append(dot(q_turn[rows], d_low[h * TOK : (h + 1) * TOK]))
        v_parts.append(dot(o_turn[rows], p_low[h * TOK : (h + 1) * TOK]))
    k_grad = jnp.concatenate(k_parts, axis=0).T
    v_grad = jnp.concatenate(v_parts, axis=0).T
    grads_ref[1] = (k_grad * score_factor).astype(jnp.bfloat16)
    grads_ref[2] = v_grad.astype(jnp.bfloat16)


def whole_spec(shape):
    return pl.BlockSpec(shape, lambda *_: (0,) * len(shape))


def north_spec(first, count):
    return pl.BlockSpec((count, 2, 3, PAD, 128), lambda g: (first // count, 0, 1, 0, g))


def south_spec(first, count):
    return pl.BlockSpec((count, 2, 4, PAD, 128), lambda g: (first // count, 0, 0, 0, g))


def group_spec(rows, columns):
    return pl.BlockSpec((1, rows, columns), lambda g: (g, 0, 0))


params = pltpu.CompilerParams(vmem_limit_bytes=VMEM)
smem = pl.BlockSpec(memory_space=pltpu.SMEM)
vmem = pl.BlockSpec(memory_space=pltpu.VMEM)


def pack_weight(lat, weight):
    return pl.pallas_call(
        pack_kernel,
        in_specs=[smem, vmem],
        out_specs=vmem,
        out_shape=jax.ShapeDtypeStruct((NZ, 24, 384), jnp.bfloat16),
        compiler_params=params,
        name="pack_weight",
    )(lat, weight)


def open_table(table, open_up):
    return pl.pallas_call(
        open_kernel,
        in_specs=[vmem, vmem],
        out_specs=vmem,
        out_shape=jax.ShapeDtypeStruct((GROUPS, 4 * ROWS, WIDE), jnp.float32),
        scratch_shapes=[pltpu.VMEM((3, ROWS * HEADS, 128), jnp.float32)],
        compiler_params=params,
        name="open_table",
    )(table, open_up)


def window_probs(across, south, table, spread, mask):
    return pl.pallas_call(
        probs_kernel,
        grid=(GROUPS,),
        in_specs=[
            north_spec(0, 2),
            south_spec(0, 2),
            group_spec(4 * ROWS, WIDE),
            whole_spec((WIDE, TOK)),
            whole_spec((TOK, TOK)),
        ],
        out_specs=group_spec(4 * TOK, TOK),
        out_shape=jax.ShapeDtypeStruct((GROUPS, 4 * TOK, TOK), jnp.float32),
        compiler_params=params,
        name="window_probs",
    )(across, south, table, spread, mask)


def normalise(across, south, quarter):
    return pl.pallas_call(
        norm_kernel,
        grid=(1,),
        in_specs=[
            pl.BlockSpec((1, 2, 2, PAD, 768), lambda g: (3, 0, 1, 0, 0)),
            pl.BlockSpec((1, 2, 2, PAD, 768), lambda g: (3, 0, 2, 0, 0)),
            pl.BlockSpec((1, 2, 4, PAD, 768), lambda g: (3, 0, 0, 0, 0)),
            whole_spec((256, 256)),
        ],
        out_specs=(whole_spec((4, 64, 768)), whole_spec((64, 128))),
        out_shape=(
            jax.ShapeDtypeStruct((4, 64, 768), jnp.float32),
            jax.ShapeDtypeStruct((64, 128), jnp.float32),
        ),
        compiler_params=params,
        name="normalise",
    )(across, across, south, quarter)


def merge_product(spots, near, far, weight, shuffle):
    return pl.pallas_call(
        merge_kernel,
        in_specs=[smem, vmem, vmem, vmem, vmem],
        out_specs=vmem,
        out_shape=jax.ShapeDtypeStruct((8, 64, 512), jnp.bfloat16),
        scratch_shapes=[pltpu.VMEM((384, 512), jnp.float32)],
        compiler_params=params,
        name="merge_product",
    )(spots, near, far, weight, shuffle)


def score_grads(recv, order, normed, inverse, gain, back, sums, across, south, probs):
    return pl.pallas_call(
        scores_kernel,
        grid=(GROUPS,),
        in_specs=[
            whole_spec((8, 64, 512)),
            whole_spec((512, 384)),
            whole_spec((4, 64, 768)),
            whole_spec((64, 128)),
            whole_spec((4, 1, 768)),
            whole_spec((TOK, 256)),
            whole_spec((TOK, WIDE)),
            north_spec(2, 1),
            south_spec(2, 1),
            group_spec(4 * TOK, TOK),
        ],
        out_specs=(
            group_spec(TOK, 128),
            group_spec(4 * TOK, TOK),
            whole_spec((16, 24, WIDE)),
        ),
        out_shape=(
            jax.ShapeDtypeStruct((GROUPS, TOK, 128), jnp.bfloat16),
            jax.ShapeDtypeStruct((GROUPS, 4 * TOK, TOK), jnp.bfloat16),
            jax.ShapeDtypeStruct((16, 24, WIDE), jnp.float32),
        ),
        scratch_shapes=[
            pltpu.VMEM((GROUPS, TOK, 128), jnp.bfloat16),
            pltpu.VMEM((GROUPS, 4 * ROWS, WIDE), jnp.float32),
        ],
        compiler_params=params,
        name="score_grads",
    )(recv, order, normed, inverse, gain, back, sums, across, south, probs)


def window_grads(across, south, o_win, d_low, probs):
    return pl.pallas_call(
        grads_kernel,
        grid=(GROUPS,),
        in_specs=[
            north_spec(0, 2),
            south_spec(0, 2),
            group_spec(TOK, 128),
            group_spec(4 * TOK, TOK),
            group_spec(4 * TOK, TOK),
        ],
        out_specs=pl.BlockSpec((3, TOK, 128), lambda g: (0, 0, g)),
        out_shape=jax.ShapeDtypeStruct((3, TOK, 768), jnp.bfloat16),
        compiler_params=params,
        name="window_grads",
    )(across, south, o_win, d_low, probs)


def from_behind(shard, axis, by):
    size = lax.axis_size(axis)
    return lax.ppermute(shard, axis, [(i, (i + by) % size) for i in range(size)])


def partner(shard, axis, bit):
    return lax.ppermute(shard, axis, [(i, i ^ bit) for i in range(lax.axis_size(axis))])


def swap(shard, axis, groups):
    return lax.all_to_all(shard, axis, 0, 0, tiled=True, axis_index_groups=groups)


def share(shard, count, axis, groups):
    return swap(jnp.broadcast_to(shard[None], (count,) + shard.shape), axis, groups)


def on_device(y_block, merge_gain, merge_weight, d_merged, q_proj, k_proj, v_proj, bias_table):
    sums, spread, quarter, back, order, shuffle, open_up = layout_constants()
    lat = lax.axis_index("lat")

    packed = pack_weight(lat.reshape(1), merge_weight)

    tokens = jnp.arange(TOK, dtype=jnp.int32)
    upper = tokens // PAD % 6 >= 3
    allowed = jnp.logical_or(upper[:, None] == upper[None, :], lat != LAT - 1)
    allowed = jnp.logical_and(allowed, (tokens % PAD < 12)[None, :])
    mask = jnp.where(allowed, 0.0, LOW)

    packed, d_merged = lax.optimization_barrier((packed, d_merged))
    weight_z = swap(packed, "lon", z_groups).reshape(NZ * 24, 384)
    eastern_d = from_behind(d_merged[:, :, :3], "lon", -1)
    d_rows = jnp.concatenate(
        [d_merged[:, :, 3:], eastern_d, jnp.zeros_like(d_merged[:, :, :2])], axis=2
    ).reshape(48, -1)
    d_rows = jnp.concatenate([d_rows, partner(d_rows, "lat", 2)], axis=0)
    near = jnp.concatenate([d_rows, partner(d_rows, "lon", NY * NZ)], axis=0)
    far = partner(near, "lat", 1)
    me = (lax.axis_index("lon") // (NY * NZ)) * LAT + lat
    rel = jnp.bitwise_xor(jnp.arange(8, dtype=jnp.int32), me)
    spots = (rel % 2 * 4 + rel // 4 * 2 + rel // 2 % 2) * 48

    weight = share(weight_z, NY, "lon", y_groups)
    table = open_table(bias_table, open_up)

    eastern = from_behind(
        jnp.stack([q_proj[:, :, :6], k_proj[:, :, :6], v_proj[:, :, :6], y_block[:, :, :6]]),
        "lon",
        -1,
    )
    across = jnp.concatenate(
        [
            jnp.stack([q_proj[:, :, 6:], k_proj[:, :, 6:], v_proj[:, :, 6:], y_block[:, :, 6:]]),
            eastern,
            jnp.zeros_like(eastern[:, :, :, :4]),
        ],
        axis=3,
    )
    south = from_behind(across[:, :, :4, :12], "lat", -1)
    south = jnp.pad(south, ((0, 0), (0, 0), (0, 0), (0, 4), (0, 0)))

    weight, table, mask = lax.optimization_barrier((weight, table, mask))
    parts = merge_product(spots, near, far, weight, shuffle)
    recv = swap(parts, ("lon", "lat"), x_lat_groups)

    south, _ = lax.optimization_barrier((south, parts))
    probs = window_probs(across, south, table, spread, mask)
    normed, inverse = normalise(across, south, quarter)

    o_win, d_low, table_part = score_grads(
        recv, order, normed, inverse, merge_gain.reshape(4, 1, 768), back, sums, across, south, probs
    )

    table_part = jnp.sum(swap(table_part, "lon", near_groups), axis=0).astype(jnp.bfloat16)
    grads = window_grads(across, south, o_win, d_low, probs)
    grid = grads.reshape(3, 2, 6, PAD, 768)[:, :, :, :12]
    southern = from_behind(grid[:, :, 3:], "lat", 1)
    fixed = jnp.concatenate([southern, grid[:, :, :3]], axis=2)

    table_part = share(table_part, NZ // 2, "lon", far_groups)
    table_part, fixed = lax.optimization_barrier((table_part, fixed))
    western = from_behind(fixed[:, :, :, 6:], "lon", 1)
    finished = jnp.concatenate([western, fixed[:, :, :, :6]], axis=3)

    table_part = jnp.sum(table_part.astype(jnp.float32), axis=0).astype(jnp.bfloat16)
    table_sum = share(table_part, 16, "lon", near_groups)[:, :18].astype(jnp.float32)
    table_sum = table_sum.reshape(HEADS, 2, 6, 2, 6, SEG)[..., :23].transpose(0, 1, 3, 2, 4, 5)
    table_grad = table_sum.reshape(bias_table.shape)
    return (finished[0], finished[1], finished[2], table_grad)


def solution(mesh):
    placed = (
        P(None, "lat", "lon", None),
        P(),
        P("lon", None),
        P(None, "lat", "lon", None),
        P(None, "lat", "lon", None),
        P(None, "lat", "lon", None),
        P(None, "lat", "lon", None),
        P("lat", None, None),
    )
    return jax.shard_map(
        on_device,
        mesh=mesh,
        in_specs=placed,
        out_specs=(
            P(None, "lat", "lon", None),
            P(None, "lat", "lon", None),
            P(None, "lat", "lon", None),
            P("lat", None, None),
        ),
        check_vma=False,
    )
```

```python
import jax
import jax.numpy as jnp
import numpy as np
from jax import lax
from jax.experimental import pallas as pl
from jax.experimental.pallas import tpu as pltpu
from jax.sharding import PartitionSpec as P

NX, NY, NZ = 2, 4, 16
LAT = 4
HEADS = 24
ROWS = 12
PAD = 16
TOK = ROWS * PAD
SEG = 32
WIDE = ROWS * SEG
GROUPS = 6
PER = 3
STEPS = GROUPS // PER
LOW = -1e30
SMALL = 12 * 1024 * 1024
LARGE = 56 * 1024 * 1024
score_factor = 32 ** (-0.5)

z_groups = [[a * NZ + z for z in range(NZ)] for a in range(NX * NY)]
y_groups = [[(x * NY + y) * NZ + z for y in range(NY)] for x in range(NX) for z in range(NZ)]
near_groups = [
    [a * NZ + 2 * pair + e for a in range(NX * NY) for e in range(2)] for pair in range(NZ // 2)
]
far_groups = [
    [a * NZ + 2 * pair + e for pair in range(NZ // 2)] for a in range(NX * NY) for e in range(2)
]
x_lat_groups = [
    [(x * NY * NZ + b) * LAT + l for x in range(NX) for l in range(LAT)] for b in range(NY * NZ)
]


def layout_constants():
    tokens = np.arange(TOK)
    row, col = tokens // PAD, tokens % PAD
    real = col < 12
    sums = np.zeros((TOK, WIDE), np.float32)
    sums[tokens[real], (row * SEG + 11 - col)[real]] = 1
    spread = np.zeros((WIDE, TOK), np.float32)
    spread[(row * SEG + 11 + col)[real], tokens[real]] = 1
    quarter = np.zeros((256, 256), np.float32)
    back = np.zeros((TOK, 256), np.float32)
    for level in range(2):
        for pr in range(4):
            for pc in range(6):
                for di in range(2):
                    for dj in range(2):
                        spot = (di + 2 * dj) * 64 + (level * 4 + pr) * 8 + pc
                        fine_row, fine_col = 2 * pr + di, 2 * pc + dj
                        quarter[spot, (level * 8 + fine_row) * PAD + fine_col] = 1
                        if 1 <= fine_row <= 6:
                            back[(level * 6 + fine_row - 1) * PAD + fine_col, spot] = 1
    shuffle = np.zeros((512, 384), np.float32)
    order = np.zeros((512, 384), np.float32)
    for l in range(4):
        for z in range(NZ):
            for i in range(6):
                shuffle[l * 128 + z * 6 + i, z * 24 + l * 6 + i] = 1
                order[l * 128 + z * 6 + i, z * 24 + l * 6 + i] = 1
    open_up = np.zeros((2, 138, WIDE), np.float32)
    for half in range(2):
        for r in range(6):
            for d in range(23):
                open_up[half, r * 23 + d, half * 192 + r * SEG + 22 - d] = 1
    all_of = (sums, spread, quarter, back, order, shuffle, open_up)
    return [jnp.asarray(a, jnp.bfloat16) for a in all_of]


def dot(a, b, dims=((1,), (0,))):
    return lax.dot_general(a, b, (dims, ((), ())), preferred_element_type=jnp.float32)


def head_mask(h):
    lanes = lax.broadcasted_iota(jnp.int32, (1, 128), 1)
    return (lanes // 32) == h


def by_head(block):
    return jnp.concatenate(
        [jnp.where(head_mask(h), block, jnp.zeros_like(block)) for h in range(4)], axis=0
    )


def split_dot(values, matrix):
    high = values.astype(jnp.bfloat16)
    low = (values - high.astype(jnp.float32)).astype(jnp.bfloat16)
    return dot(high, matrix) + dot(low, matrix)


def window(north_ref, south_ref, which, group):
    lanes = slice(group * 128, (group + 1) * 128)
    pieces = []
    for level in range(2):
        pieces.append(north_ref[which, level, :, :, lanes].reshape(48, 128))
        pieces.append(south_ref[which, level, 0:3, :, lanes].reshape(48, 128))
    return jnp.concatenate(pieces, axis=0)


def pack_kernel(lat_ref, w_ref, out_ref):
    first = lat_ref[0] * 6
    to = lax.broadcasted_iota(jnp.int32, (24, 24), 0)
    source = lax.broadcasted_iota(jnp.int32, (24, 24), 1)
    total = jnp.zeros((24, 384), jnp.float32)
    for part in range(4):
        pick = jnp.logical_and(to // 6 == part, source == first + to - part * 6)
        pick = jnp.where(pick, 1.0, 0.0).astype(jnp.bfloat16)
        total += dot(pick, w_ref[:, part * 384 : (part + 1) * 384])
    packed = total.astype(jnp.bfloat16)
    for z in range(NZ):
        out_ref[z] = packed


def open_kernel(table_ref, open_ref, out_ref, wide_ref):
    halves = []
    for half in range(2):
        pieces = []
        for a in range(ROWS):
            first = (a // 6 * 2 + half) * 828 + a % 6 * 138
            pieces.append(table_ref[0, :, first : first + 138])
        halves.append(split_dot(jnp.concatenate(pieces, axis=0), open_ref[half]))
    whole = halves[0] + halves[1]
    for s in range(3):
        wide_ref[s] = whole[:, s * 128 : (s + 1) * 128]
    for head in range(HEADS):
        row = head % 4 * ROWS
        for s in range(3):
            out_ref[head // 4, row : row + ROWS, s * 128 : (s + 1) * 128] = wide_ref[
                s, pl.ds(head, ROWS, stride=HEADS), :
            ]


def probs_kernel(north_ref, south_ref, table_ref, spread_ref, mask_ref, p_ref):
    for group in range(PER):
        pieces = []
        for s in range(3):
            table = table_ref[group, :, s * 128 : (s + 1) * 128]
            table = jnp.broadcast_to(table[:, None, :], (4 * ROWS, PAD, 128))
            pieces.append(pltpu.roll(table, 0, 2, stride=1, stride_axis=1))
        wide = jnp.concatenate(pieces, axis=2).reshape(4 * TOK, WIDE)
        q_win = window(north_ref, south_ref, 0, group)
        k_win = window(north_ref, south_ref, 1, group)
        scores = dot(by_head(q_win), k_win, ((1,), (1,))) * score_factor
        scores = scores + split_dot(wide, spread_ref[...])
        scores = (scores.reshape(4, TOK, TOK) + mask_ref[...][None]).reshape(4 * TOK, TOK)
        expon = jnp.exp(scores - jnp.max(scores, axis=-1, keepdims=True))
        probs = expon * (1.0 / jnp.sum(expon, axis=-1, keepdims=True))
        p_ref[group] = probs.astype(jnp.bfloat16)


def norm_kernel(a_ref, b_ref, south_ref, quarter_ref, normed_ref, inverse_ref):
    pieces = []
    for level in range(2):
        pieces.append(a_ref[0, level].reshape(32, 768))
        pieces.append(b_ref[0, level].reshape(32, 768))
        pieces.append(south_ref[0, level].reshape(64, 768))
    fields = dot(quarter_ref[...], jnp.concatenate(pieces, axis=0))
    parts = [fields[q * 64 : (q + 1) * 64] for q in range(4)]
    mean = jnp.sum(parts[0] + parts[1] + parts[2] + parts[3], axis=-1, keepdims=True) / 3072
    parts = [part - mean for part in parts]
    squares = [part * part for part in parts]
    variance = (
        jnp.sum(squares[0] + squares[1] + squares[2] + squares[3], axis=-1, keepdims=True) / 3072
    )
    inverse = lax.rsqrt(variance + 1e-05)
    for q in range(4):
        normed_ref[q] = parts[q] * inverse
    inverse_ref[...] = jnp.broadcast_to(inverse, (64, 128))


def merge_kernel(spot_ref, near_ref, far_ref, w_ref, shuffle_ref, out_ref, acc_ref):
    weights = [dot(shuffle_ref[...], w_ref[y]).astype(jnp.bfloat16) for y in range(NY)]
    near, far = None, None
    for part in range(4):
        rows, columns = slice(part * 128, part * 128 + 128), slice(part * 384, part * 384 + 384)
        weight = jnp.concatenate([weights[y][rows] for y in range(NY)], axis=0)
        near_part = dot(near_ref[:, columns], weight, ((1,), (1,)))
        far_part = dot(far_ref[:, columns], weight, ((1,), (1,)))
        near = near_part if part == 0 else near + near_part
        far = far_part if part == 0 else far + far_part
    acc_ref[:192] = near
    acc_ref[192:] = far
    for x in range(NX):
        for l in range(LAT):
            for level in range(2):
                own = pl.multiple_of(spot_ref[x * LAT + l] + level * 24 + 8, 8)
                below = pl.multiple_of(spot_ref[x * LAT + (l + 1) % LAT] + level * 24, 8)
                out_ref[x * LAT + l, level * 32 : level * 32 + 16] = acc_ref[
                    pl.ds(own, 16)
                ].astype(jnp.bfloat16)
                out_ref[x * LAT + l, level * 32 + 16 : level * 32 + 32] = acc_ref[
                    pl.ds(below, 16)
                ].astype(jnp.bfloat16)


def scores_kernel(
    recv_ref,
    order_ref,
    normed_ref,
    inverse_ref,
    gain_ref,
    back_ref,
    sums_ref,
    north_ref,
    south_ref,
    p_ref,
    o_out_ref,
    d_ref,
    table_ref,
    o_ref,
    sum_ref,
):
    g = pl.program_id(0)

    @pl.when(g == 0)
    def _():
        pieces = [
            jnp.concatenate(
                [recv_ref[x * LAT + l, :, y * 128 : (y + 1) * 128] for l in range(LAT)], axis=1
            )
            for x in range(NX)
            for y in range(NY)
        ]
        d_norm = dot(jnp.concatenate(pieces, axis=0), order_ref[...])
        hats = []
        for q in range(4):
            left = d_norm[(2 * q) * 64 : (2 * q + 1) * 64]
            right = d_norm[(2 * q + 1) * 64 : (2 * q + 2) * 64]
            hats.append(jnp.concatenate([left, right], axis=1) * gain_ref[q])
        mean = jnp.sum(hats[0] + hats[1] + hats[2] + hats[3], axis=-1, keepdims=True) / 3072
        cross = [hats[q] * normed_ref[q] for q in range(4)]
        along = jnp.sum(cross[0] + cross[1] + cross[2] + cross[3], axis=-1, keepdims=True) / 3072
        inverse = inverse_ref[:, 0:1]
        stack = [(hats[q] - mean - normed_ref[q] * along) * inverse for q in range(4)]
        d_out = dot(back_ref[...], jnp.concatenate(stack, axis=0).astype(jnp.bfloat16))
        d_out = d_out.astype(jnp.bfloat16)
        for s in range(GROUPS):
            o_ref[s] = d_out[:, s * 128 : (s + 1) * 128]

    for group in range(PER):
        o_win = o_ref[g * PER + group]
        o_out_ref[group] = o_win
        probs = p_ref[group].astype(jnp.float32)
        v_win = window(north_ref, south_ref, 0, group)
        d_probs = dot(by_head(o_win), v_win, ((1,), (1,)))
        delta = jnp.sum(probs * d_probs, axis=-1, keepdims=True)
        d_low = (probs * (d_probs - delta)).astype(jnp.bfloat16)
        d_ref[group] = d_low

        spread = dot(d_low, sums_ref[...]).reshape(4 * ROWS, PAD, WIDE)
        for s in range(3):
            lanes = slice(s * 128, (s + 1) * 128)
            turned = pltpu.roll(spread[:, :, lanes], 0, 2, stride=1, stride_axis=1)
            sum_ref[g * PER + group, :, lanes] = jnp.sum(turned, axis=1)

    @pl.when(g == STEPS - 1)
    def _():
        whole = jnp.concatenate([sum_ref[s] for s in range(GROUPS)], axis=0)
        for part in range(16):
            table_ref[part, 0:18] = whole[part * 18 : (part + 1) * 18]
            table_ref[part, 18:24] = jnp.zeros((6, WIDE), jnp.float32)


def grads_kernel(north_ref, south_ref, o_ref, d_ref, p_ref, grads_ref):
    for group in range(PER):
        lanes = slice(group * 128, (group + 1) * 128)
        q_win = window(north_ref, south_ref, 0, group)
        k_win = window(north_ref, south_ref, 1, group)
        o_win, d_low, p_low = o_ref[group], d_ref[group], p_ref[group]
        q_all = dot(d_low, k_win)
        q_grad = jnp.zeros((TOK, 128), jnp.float32)
        for h in range(4):
            q_grad = jnp.where(head_mask(h), q_all[h * TOK : (h + 1) * TOK], q_grad)
        grads_ref[0, :, lanes] = (q_grad * score_factor).astype(jnp.bfloat16)

        q_turn = q_win.astype(jnp.float32).T.astype(jnp.bfloat16)
        o_turn = o_win.astype(jnp.float32).T.astype(jnp.bfloat16)
        k_parts, v_parts = [], []
        for h in range(4):
            rows = slice(h * 32, (h + 1) * 32)
            k_parts.append(dot(q_turn[rows], d_low[h * TOK : (h + 1) * TOK]))
            v_parts.append(dot(o_turn[rows], p_low[h * TOK : (h + 1) * TOK]))
        k_grad = jnp.concatenate(k_parts, axis=0).T
        v_grad = jnp.concatenate(v_parts, axis=0).T
        grads_ref[1, :, lanes] = (k_grad * score_factor).astype(jnp.bfloat16)
        grads_ref[2, :, lanes] = v_grad.astype(jnp.bfloat16)


def whole_spec(shape):
    return pl.BlockSpec(shape, lambda *_: (0,) * len(shape))


def north_spec(first, count):
    return pl.BlockSpec((count, 2, 3, PAD, PER * 128), lambda g: (first // count, 0, 1, 0, g))


def south_spec(first, count):
    return pl.BlockSpec((count, 2, 4, PAD, PER * 128), lambda g: (first // count, 0, 0, 0, g))


def group_spec(rows, columns):
    return pl.BlockSpec((PER, rows, columns), lambda g: (g, 0, 0))


params = pltpu.CompilerParams(vmem_limit_bytes=SMALL)
large = pltpu.CompilerParams(vmem_limit_bytes=LARGE)
smem = pl.BlockSpec(memory_space=pltpu.SMEM)
vmem = pl.BlockSpec(memory_space=pltpu.VMEM)


def pack_weight(lat, weight):
    return pl.pallas_call(
        pack_kernel,
        in_specs=[smem, vmem],
        out_specs=vmem,
        out_shape=jax.ShapeDtypeStruct((NZ, 24, 384), jnp.bfloat16),
        compiler_params=params,
        name="pack_weight",
    )(lat, weight)


def open_table(table, open_up):
    return pl.pallas_call(
        open_kernel,
        in_specs=[vmem, vmem],
        out_specs=vmem,
        out_shape=jax.ShapeDtypeStruct((GROUPS, 4 * ROWS, WIDE), jnp.float32),
        scratch_shapes=[pltpu.VMEM((3, ROWS * HEADS, 128), jnp.float32)],
        compiler_params=params,
        name="open_table",
    )(table, open_up)


def window_probs(across, south, table, spread, mask):
    return pl.pallas_call(
        probs_kernel,
        grid=(STEPS,),
        in_specs=[
            north_spec(0, 2),
            south_spec(0, 2),
            group_spec(4 * ROWS, WIDE),
            whole_spec((WIDE, TOK)),
            whole_spec((TOK, TOK)),
        ],
        out_specs=group_spec(4 * TOK, TOK),
        out_shape=jax.ShapeDtypeStruct((GROUPS, 4 * TOK, TOK), jnp.bfloat16),
        compiler_params=large,
        name="window_probs",
    )(across, south, table, spread, mask)


def normalise(across, south, quarter):
    return pl.pallas_call(
        norm_kernel,
        grid=(1,),
        in_specs=[
            pl.BlockSpec((1, 2, 2, PAD, 768), lambda g: (3, 0, 1, 0, 0)),
            pl.BlockSpec((1, 2, 2, PAD, 768), lambda g: (3, 0, 2, 0, 0)),
            pl.BlockSpec((1, 2, 4, PAD, 768), lambda g: (3, 0, 0, 0, 0)),
            whole_spec((256, 256)),
        ],
        out_specs=(whole_spec((4, 64, 768)), whole_spec((64, 128))),
        out_shape=(
            jax.ShapeDtypeStruct((4, 64, 768), jnp.float32),
            jax.ShapeDtypeStruct((64, 128), jnp.float32),
        ),
        compiler_params=params,
        name="normalise",
    )(across, across, south, quarter)


def merge_product(spots, near, far, weight, shuffle):
    return pl.pallas_call(
        merge_kernel,
        in_specs=[smem, vmem, vmem, vmem, vmem],
        out_specs=vmem,
        out_shape=jax.ShapeDtypeStruct((8, 64, 512), jnp.bfloat16),
        scratch_shapes=[pltpu.VMEM((384, 512), jnp.float32)],
        compiler_params=params,
        name="merge_product",
    )(spots, near, far, weight, shuffle)


def score_grads(recv, order, normed, inverse, gain, back, sums, across, south, probs):
    return pl.pallas_call(
        scores_kernel,
        grid=(STEPS,),
        in_specs=[
            whole_spec((8, 64, 512)),
            whole_spec((512, 384)),
            whole_spec((4, 64, 768)),
            whole_spec((64, 128)),
            whole_spec((4, 1, 768)),
            whole_spec((TOK, 256)),
            whole_spec((TOK, WIDE)),
            north_spec(2, 1),
            south_spec(2, 1),
            group_spec(4 * TOK, TOK),
        ],
        out_specs=(
            group_spec(TOK, 128),
            group_spec(4 * TOK, TOK),
            whole_spec((16, 24, WIDE)),
        ),
        out_shape=(
            jax.ShapeDtypeStruct((GROUPS, TOK, 128), jnp.bfloat16),
            jax.ShapeDtypeStruct((GROUPS, 4 * TOK, TOK), jnp.bfloat16),
            jax.ShapeDtypeStruct((16, 24, WIDE), jnp.float32),
        ),
        scratch_shapes=[
            pltpu.VMEM((GROUPS, TOK, 128), jnp.bfloat16),
            pltpu.VMEM((GROUPS, 4 * ROWS, WIDE), jnp.float32),
        ],
        compiler_params=large,
        name="score_grads",
    )(recv, order, normed, inverse, gain, back, sums, across, south, probs)


def window_grads(across, south, o_win, d_low, probs):
    return pl.pallas_call(
        grads_kernel,
        grid=(STEPS,),
        in_specs=[
            north_spec(0, 2),
            south_spec(0, 2),
            group_spec(TOK, 128),
            group_spec(4 * TOK, TOK),
            group_spec(4 * TOK, TOK),
        ],
        out_specs=pl.BlockSpec((3, TOK, PER * 128), lambda g: (0, 0, g)),
        out_shape=jax.ShapeDtypeStruct((3, TOK, 768), jnp.bfloat16),
        compiler_params=large,
        name="window_grads",
    )(across, south, o_win, d_low, probs)


def from_behind(shard, axis, by):
    size = lax.axis_size(axis)
    return lax.ppermute(shard, axis, [(i, (i + by) % size) for i in range(size)])


def partner(shard, axis, bit):
    return lax.ppermute(shard, axis, [(i, i ^ bit) for i in range(lax.axis_size(axis))])


def swap(shard, axis, groups):
    return lax.all_to_all(shard, axis, 0, 0, tiled=True, axis_index_groups=groups)


def share(shard, count, axis, groups):
    return swap(jnp.broadcast_to(shard[None], (count,) + shard.shape), axis, groups)


def on_device(y_block, merge_gain, merge_weight, d_merged, q_proj, k_proj, v_proj, bias_table):
    sums, spread, quarter, back, order, shuffle, open_up = layout_constants()
    lat = lax.axis_index("lat")

    packed = pack_weight(lat.reshape(1), merge_weight)

    tokens = jnp.arange(TOK, dtype=jnp.int32)
    upper = tokens // PAD % 6 >= 3
    allowed = jnp.logical_or(upper[:, None] == upper[None, :], lat != LAT - 1)
    allowed = jnp.logical_and(allowed, (tokens % PAD < 12)[None, :])
    mask = jnp.where(allowed, 0.0, LOW)

    packed, d_merged = lax.optimization_barrier((packed, d_merged))
    weight_z = swap(packed, "lon", z_groups).reshape(NZ * 24, 384)
    eastern_d = from_behind(d_merged[:, :, :3], "lon", -1)
    d_rows = jnp.concatenate(
        [d_merged[:, :, 3:], eastern_d, jnp.zeros_like(d_merged[:, :, :2])], axis=2
    ).reshape(48, -1)
    d_rows = jnp.concatenate([d_rows, partner(d_rows, "lat", 2)], axis=0)
    near = jnp.concatenate([d_rows, partner(d_rows, "lon", NY * NZ)], axis=0)
    far = partner(near, "lat", 1)
    me = (lax.axis_index("lon") // (NY * NZ)) * LAT + lat
    rel = jnp.bitwise_xor(jnp.arange(8, dtype=jnp.int32), me)
    spots = (rel % 2 * 4 + rel // 4 * 2 + rel // 2 % 2) * 48

    weight = share(weight_z, NY, "lon", y_groups)
    table = open_table(bias_table, open_up)

    eastern = from_behind(
        jnp.stack([q_proj[:, :, :6], k_proj[:, :, :6], v_proj[:, :, :6], y_block[:, :, :6]]),
        "lon",
        -1,
    )
    across = jnp.concatenate(
        [
            jnp.stack([q_proj[:, :, 6:], k_proj[:, :, 6:], v_proj[:, :, 6:], y_block[:, :, 6:]]),
            eastern,
            jnp.zeros_like(eastern[:, :, :, :4]),
        ],
        axis=3,
    )
    south = from_behind(across[:, :, :4, :12], "lat", -1)
    south = jnp.pad(south, ((0, 0), (0, 0), (0, 0), (0, 4), (0, 0)))

    weight, table, mask = lax.optimization_barrier((weight, table, mask))
    parts = merge_product(spots, near, far, weight, shuffle)
    recv = swap(parts, ("lon", "lat"), x_lat_groups)

    south, _ = lax.optimization_barrier((south, parts))
    probs = window_probs(across, south, table, spread, mask)
    normed, inverse = normalise(across, south, quarter)

    o_win, d_low, table_part = score_grads(
        recv, order, normed, inverse, merge_gain.reshape(4, 1, 768), back, sums, across, south, probs
    )

    table_part = jnp.sum(swap(table_part, "lon", near_groups), axis=0).astype(jnp.bfloat16)
    grads = window_grads(across, south, o_win, d_low, probs)
    grid = grads.reshape(3, 2, 6, PAD, 768)[:, :, :, :12]
    southern = from_behind(grid[:, :, 3:], "lat", 1)
    fixed = jnp.concatenate([southern, grid[:, :, :3]], axis=2)

    table_part = share(table_part, NZ // 2, "lon", far_groups)
    table_part, fixed = lax.optimization_barrier((table_part, fixed))
    western = from_behind(fixed[:, :, :, 6:], "lon", 1)
    finished = jnp.concatenate([western, fixed[:, :, :, :6]], axis=3)

    table_part = jnp.sum(table_part.astype(jnp.float32), axis=0).astype(jnp.bfloat16)
    table_sum = share(table_part, 16, "lon", near_groups)[:, :18].astype(jnp.float32)
    table_sum = table_sum.reshape(HEADS, 2, 6, 2, 6, SEG)[..., :23].transpose(0, 1, 3, 2, 4, 5)
    table_grad = table_sum.reshape(bias_table.shape)
    return (finished[0], finished[1], finished[2], table_grad)


def solution(mesh):
    placed = (
        P(None, "lat", "lon", None),
        P(),
        P("lon", None),
        P(None, "lat", "lon", None),
        P(None, "lat", "lon", None),
        P(None, "lat", "lon", None),
        P(None, "lat", "lon", None),
        P("lat", None, None),
    )
    return jax.shard_map(
        on_device,
        mesh=mesh,
        in_specs=placed,
        out_specs=(
            P(None, "lat", "lon", None),
            P(None, "lat", "lon", None),
            P(None, "lat", "lon", None),
            P("lat", None, None),
        ),
        check_vma=False,
    )
```

```python
import jax
import jax.numpy as jnp
import numpy as np
from jax import lax
from jax.experimental import pallas as pl
from jax.experimental.pallas import tpu as pltpu
from jax.sharding import PartitionSpec as P

NX, NY, NZ = 2, 4, 16
LAT = 4
HEADS = 24
ROWS = 12
PAD = 16
TOK = ROWS * PAD
SEG = 32
WIDE = ROWS * SEG
GROUPS = 6
PER = 3
STEPS = GROUPS // PER
SHARE = 7
LOW = -1e30
SMALL = 12 * 1024 * 1024
LARGE = 56 * 1024 * 1024
score_factor = 32 ** (-0.5)

z_groups = [[a * NZ + z for z in range(NZ)] for a in range(NX * NY)]
y_groups = [[(x * NY + y) * NZ + z for y in range(NY)] for x in range(NX) for z in range(NZ)]
near_groups = [
    [a * NZ + 2 * pair + e for a in range(NX * NY) for e in range(2)] for pair in range(NZ // 2)
]
far_groups = [
    [a * NZ + 2 * pair + e for pair in range(NZ // 2)] for a in range(NX * NY) for e in range(2)
]
x_lat_groups = [
    [(x * NY * NZ + b) * LAT + l for x in range(NX) for l in range(LAT)] for b in range(NY * NZ)
]


def layout_constants():
    tokens = np.arange(TOK)
    row, col = tokens // PAD, tokens % PAD
    real = col < 12
    sums = np.zeros((TOK, WIDE), np.float32)
    sums[tokens[real], (row * SEG + 11 - col)[real]] = 1
    spread = np.zeros((WIDE, TOK), np.float32)
    spread[(row * SEG + 11 + col)[real], tokens[real]] = 1
    quarter = np.zeros((256, 256), np.float32)
    back = np.zeros((TOK, 256), np.float32)
    for level in range(2):
        for pr in range(4):
            for pc in range(6):
                for di in range(2):
                    for dj in range(2):
                        spot = (di + 2 * dj) * 64 + (level * 4 + pr) * 8 + pc
                        fine_row, fine_col = 2 * pr + di, 2 * pc + dj
                        quarter[spot, (level * 8 + fine_row) * PAD + fine_col] = 1
                        if 1 <= fine_row <= 6:
                            back[(level * 6 + fine_row - 1) * PAD + fine_col, spot] = 1
    shuffle = np.zeros((512, 384), np.float32)
    order = np.zeros((512, 384), np.float32)
    for l in range(4):
        for z in range(NZ):
            for i in range(6):
                shuffle[l * 128 + z * 6 + i, z * 24 + l * 6 + i] = 1
                order[l * 128 + z * 6 + i, z * 24 + l * 6 + i] = 1
    open_up = np.zeros((2, 138, WIDE), np.float32)
    for half in range(2):
        for r in range(6):
            for d in range(23):
                open_up[half, r * 23 + d, half * 192 + r * SEG + 22 - d] = 1
    close = np.zeros((WIDE, 512), np.float32)
    for b in range(ROWS):
        for d in range(23):
            close[b * SEG + d, b // 6 * 256 + b % 6 * 23 + d] = 1
    all_of = (sums, spread, quarter, back, order, shuffle, open_up, close)
    return [jnp.asarray(a, jnp.bfloat16) for a in all_of]


def dot(a, b, dims=((1,), (0,))):
    return lax.dot_general(a, b, (dims, ((), ())), preferred_element_type=jnp.float32)


def head_mask(h):
    lanes = lax.broadcasted_iota(jnp.int32, (1, 128), 1)
    return (lanes // 32) == h


def by_head(block):
    return jnp.concatenate(
        [jnp.where(head_mask(h), block, jnp.zeros_like(block)) for h in range(4)], axis=0
    )


def split_dot(values, matrix):
    high = values.astype(jnp.bfloat16)
    low = (values - high.astype(jnp.float32)).astype(jnp.bfloat16)
    return dot(high, matrix) + dot(low, matrix)


def window(north_ref, south_ref, which, group):
    lanes = slice(group * 128, (group + 1) * 128)
    pieces = []
    for level in range(2):
        pieces.append(north_ref[which, level, :, :, lanes].reshape(48, 128))
        pieces.append(south_ref[which, level, 0:3, :, lanes].reshape(48, 128))
    return jnp.concatenate(pieces, axis=0)


def pack_kernel(lat_ref, w_ref, out_ref):
    first = lat_ref[0] * 6
    to = lax.broadcasted_iota(jnp.int32, (24, 24), 0)
    source = lax.broadcasted_iota(jnp.int32, (24, 24), 1)
    total = jnp.zeros((24, 384), jnp.float32)
    for part in range(4):
        pick = jnp.logical_and(to // 6 == part, source == first + to - part * 6)
        pick = jnp.where(pick, 1.0, 0.0).astype(jnp.bfloat16)
        total += dot(pick, w_ref[:, part * 384 : (part + 1) * 384])
    packed = total.astype(jnp.bfloat16)
    for z in range(NZ):
        out_ref[z] = packed


def open_kernel(table_ref, open_ref, out_ref, wide_ref):
    halves = []
    for half in range(2):
        pieces = []
        for a in range(ROWS):
            first = (a // 6 * 2 + half) * 828 + a % 6 * 138
            pieces.append(table_ref[0, :, first : first + 138])
        halves.append(split_dot(jnp.concatenate(pieces, axis=0), open_ref[half]))
    whole = halves[0] + halves[1]
    for s in range(3):
        wide_ref[s] = whole[:, s * 128 : (s + 1) * 128]
    for head in range(HEADS):
        row = head % 4 * ROWS
        for s in range(3):
            out_ref[head // 4, row : row + ROWS, s * 128 : (s + 1) * 128] = wide_ref[
                s, pl.ds(head, ROWS, stride=HEADS), :
            ]


def probs_kernel(north_ref, south_ref, table_ref, spread_ref, mask_ref, p_ref):
    for group in range(PER):
        pieces = []
        for s in range(3):
            table = table_ref[group, :, s * 128 : (s + 1) * 128]
            table = jnp.broadcast_to(table[:, None, :], (4 * ROWS, PAD, 128))
            pieces.append(pltpu.roll(table, 0, 2, stride=1, stride_axis=1))
        wide = jnp.concatenate(pieces, axis=2).reshape(4 * TOK, WIDE)
        q_win = window(north_ref, south_ref, 0, group)
        k_win = window(north_ref, south_ref, 1, group)
        scores = dot(by_head(q_win), k_win, ((1,), (1,))) * score_factor
        scores = scores + split_dot(wide, spread_ref[...])
        scores = (scores.reshape(4, TOK, TOK) + mask_ref[...][None]).reshape(4 * TOK, TOK)
        expon = jnp.exp(scores - jnp.max(scores, axis=-1, keepdims=True))
        probs = expon * (1.0 / jnp.sum(expon, axis=-1, keepdims=True))
        p_ref[group] = probs.astype(jnp.bfloat16)


def norm_kernel(a_ref, b_ref, south_ref, quarter_ref, normed_ref, inverse_ref):
    pieces = []
    for level in range(2):
        pieces.append(a_ref[0, level].reshape(32, 768))
        pieces.append(b_ref[0, level].reshape(32, 768))
        pieces.append(south_ref[0, level].reshape(64, 768))
    fields = dot(quarter_ref[...], jnp.concatenate(pieces, axis=0))
    parts = [fields[q * 64 : (q + 1) * 64] for q in range(4)]
    mean = jnp.sum(parts[0] + parts[1] + parts[2] + parts[3], axis=-1, keepdims=True) / 3072
    parts = [part - mean for part in parts]
    squares = [part * part for part in parts]
    variance = (
        jnp.sum(squares[0] + squares[1] + squares[2] + squares[3], axis=-1, keepdims=True) / 3072
    )
    inverse = lax.rsqrt(variance + 1e-05)
    for q in range(4):
        normed_ref[q] = parts[q] * inverse
    inverse_ref[...] = jnp.broadcast_to(inverse, (64, 128))


def merge_kernel(spot_ref, near_ref, far_ref, w_ref, shuffle_ref, out_ref, acc_ref):
    weights = [dot(shuffle_ref[...], w_ref[y]).astype(jnp.bfloat16) for y in range(NY)]
    near, far = None, None
    for part in range(4):
        rows, columns = slice(part * 128, part * 128 + 128), slice(part * 384, part * 384 + 384)
        weight = jnp.concatenate([weights[y][rows] for y in range(NY)], axis=0)
        near_part = dot(near_ref[:, columns], weight, ((1,), (1,)))
        far_part = dot(far_ref[:, columns], weight, ((1,), (1,)))
        near = near_part if part == 0 else near + near_part
        far = far_part if part == 0 else far + far_part
    acc_ref[:192] = near
    acc_ref[192:] = far
    for x in range(NX):
        for l in range(LAT):
            for level in range(2):
                own = pl.multiple_of(spot_ref[x * LAT + l] + level * 24 + 8, 8)
                below = pl.multiple_of(spot_ref[x * LAT + (l + 1) % LAT] + level * 24, 8)
                out_ref[x * LAT + l, level * 32 : level * 32 + 16] = acc_ref[
                    pl.ds(own, 16)
                ].astype(jnp.bfloat16)
                out_ref[x * LAT + l, level * 32 + 16 : level * 32 + 32] = acc_ref[
                    pl.ds(below, 16)
                ].astype(jnp.bfloat16)


def score_grad(probs, o_win, v_win):
    d_probs = dot(by_head(o_win), v_win, ((1,), (1,)))
    probs = probs.astype(jnp.float32)
    delta = jnp.sum(probs * d_probs, axis=-1, keepdims=True)
    return (probs * (d_probs - delta)).astype(jnp.bfloat16)


def scores_kernel(
    recv_ref,
    order_ref,
    normed_ref,
    inverse_ref,
    gain_ref,
    back_ref,
    sums_ref,
    north_ref,
    south_ref,
    p_ref,
    o_out_ref,
    table_ref,
    o_ref,
    sum_ref,
):
    g = pl.program_id(0)

    @pl.when(g == 0)
    def _():
        pieces = [
            jnp.concatenate(
                [recv_ref[x * LAT + l, :, y * 128 : (y + 1) * 128] for l in range(LAT)], axis=1
            )
            for x in range(NX)
            for y in range(NY)
        ]
        d_norm = dot(jnp.concatenate(pieces, axis=0), order_ref[...])
        hats = []
        for q in range(4):
            left = d_norm[(2 * q) * 64 : (2 * q + 1) * 64]
            right = d_norm[(2 * q + 1) * 64 : (2 * q + 2) * 64]
            hats.append(jnp.concatenate([left, right], axis=1) * gain_ref[q])
        mean = jnp.sum(hats[0] + hats[1] + hats[2] + hats[3], axis=-1, keepdims=True) / 3072
        cross = [hats[q] * normed_ref[q] for q in range(4)]
        along = jnp.sum(cross[0] + cross[1] + cross[2] + cross[3], axis=-1, keepdims=True) / 3072
        inverse = inverse_ref[:, 0:1]
        stack = [(hats[q] - mean - normed_ref[q] * along) * inverse for q in range(4)]
        d_out = dot(back_ref[...], jnp.concatenate(stack, axis=0).astype(jnp.bfloat16))
        d_out = d_out.astype(jnp.bfloat16)
        for s in range(GROUPS):
            o_ref[s] = d_out[:, s * 128 : (s + 1) * 128]

    for group in range(PER):
        o_win = o_ref[g * PER + group]
        o_out_ref[group] = o_win
        d_low = score_grad(p_ref[group], o_win, window(north_ref, south_ref, 0, group))
        spread = dot(d_low, sums_ref[...]).reshape(4 * ROWS, PAD, WIDE)
        for s in range(3):
            lanes = slice(s * 128, (s + 1) * 128)
            turned = pltpu.roll(spread[:, :, lanes], 0, 2, stride=1, stride_axis=1)
            sum_ref[g * PER + group, :, lanes] = jnp.sum(turned, axis=1)

    @pl.when(g == STEPS - 1)
    def _():
        whole = jnp.concatenate([sum_ref[s] for s in range(GROUPS)], axis=0)
        tiles = [
            whole[r * 8 : (r + 1) * 8, s * 128 : (s + 1) * 128] for s in range(3) for r in range(36)
        ]
        tiles += [jnp.zeros((8, 128), jnp.float32)] * (16 * SHARE - len(tiles))
        for part in range(16):
            chunk = jnp.concatenate(tiles[part * SHARE : (part + 1) * SHARE], axis=0)
            table_ref[part] = chunk.astype(jnp.bfloat16)


def close_kernel(parts_ref, close_ref, out_ref, wide_ref):
    for part in range(16):
        chunk = parts_ref[part].astype(jnp.float32)
        for k in range(SHARE):
            s, r = divmod(part * SHARE + k, 36)
            if s < 3:
                wide_ref[s, r * 8 : (r + 1) * 8] = chunk[k * 8 : (k + 1) * 8]
    rows = []
    for a in range(ROWS):
        lanes = [wide_ref[s, pl.ds(a, HEADS, stride=ROWS), :] for s in range(3)]
        rows.append(jnp.concatenate(lanes, axis=1))
    dense = dot(jnp.concatenate(rows, axis=0).astype(jnp.bfloat16), close_ref[...])
    for a in range(ROWS):
        for half in range(2):
            first = (a // 6 * 2 + half) * 828 + a % 6 * 138
            out_ref[0, :, first : first + 138] = dense[
                a * HEADS : (a + 1) * HEADS, half * 256 : half * 256 + 138
            ]


def grads_kernel(north_ref, south_ref, o_ref, p_ref, grads_ref):
    for group in range(PER):
        lanes = slice(group * 128, (group + 1) * 128)
        q_win = window(north_ref, south_ref, 0, group)
        k_win = window(north_ref, south_ref, 1, group)
        o_win, p_low = o_ref[group], p_ref[group]
        d_low = score_grad(p_low, o_win, window(north_ref, south_ref, 2, group))
        q_all = dot(d_low, k_win)
        q_grad = jnp.zeros((TOK, 128), jnp.float32)
        for h in range(4):
            q_grad = jnp.where(head_mask(h), q_all[h * TOK : (h + 1) * TOK], q_grad)
        grads_ref[0, :, lanes] = (q_grad * score_factor).astype(jnp.bfloat16)

        q_turn = q_win.astype(jnp.float32).T.astype(jnp.bfloat16)
        o_turn = o_win.astype(jnp.float32).T.astype(jnp.bfloat16)
        k_parts, v_parts = [], []
        for h in range(4):
            rows = slice(h * 32, (h + 1) * 32)
            k_parts.append(dot(q_turn[rows], d_low[h * TOK : (h + 1) * TOK]))
            v_parts.append(dot(o_turn[rows], p_low[h * TOK : (h + 1) * TOK]))
        k_grad = jnp.concatenate(k_parts, axis=0).T
        v_grad = jnp.concatenate(v_parts, axis=0).T
        grads_ref[1, :, lanes] = (k_grad * score_factor).astype(jnp.bfloat16)
        grads_ref[2, :, lanes] = v_grad.astype(jnp.bfloat16)


def whole_spec(shape):
    return pl.BlockSpec(shape, lambda *_: (0,) * len(shape))


def north_spec(first, count):
    return pl.BlockSpec((count, 2, 3, PAD, PER * 128), lambda g: (first // count, 0, 1, 0, g))


def south_spec(first, count):
    return pl.BlockSpec((count, 2, 4, PAD, PER * 128), lambda g: (first // count, 0, 0, 0, g))


def group_spec(rows, columns):
    return pl.BlockSpec((PER, rows, columns), lambda g: (g, 0, 0))


params = pltpu.CompilerParams(vmem_limit_bytes=SMALL)
large = pltpu.CompilerParams(vmem_limit_bytes=LARGE)
smem = pl.BlockSpec(memory_space=pltpu.SMEM)
vmem = pl.BlockSpec(memory_space=pltpu.VMEM)


def pack_weight(lat, weight):
    return pl.pallas_call(
        pack_kernel,
        in_specs=[smem, vmem],
        out_specs=vmem,
        out_shape=jax.ShapeDtypeStruct((NZ, 24, 384), jnp.bfloat16),
        compiler_params=params,
        name="pack_weight",
    )(lat, weight)


def open_table(table, open_up):
    return pl.pallas_call(
        open_kernel,
        in_specs=[vmem, vmem],
        out_specs=vmem,
        out_shape=jax.ShapeDtypeStruct((GROUPS, 4 * ROWS, WIDE), jnp.float32),
        scratch_shapes=[pltpu.VMEM((3, ROWS * HEADS, 128), jnp.float32)],
        compiler_params=params,
        name="open_table",
    )(table, open_up)


def window_probs(across, south, table, spread, mask):
    return pl.pallas_call(
        probs_kernel,
        grid=(STEPS,),
        in_specs=[
            north_spec(0, 2),
            south_spec(0, 2),
            group_spec(4 * ROWS, WIDE),
            whole_spec((WIDE, TOK)),
            whole_spec((TOK, TOK)),
        ],
        out_specs=group_spec(4 * TOK, TOK),
        out_shape=jax.ShapeDtypeStruct((GROUPS, 4 * TOK, TOK), jnp.bfloat16),
        compiler_params=large,
        name="window_probs",
    )(across, south, table, spread, mask)


def normalise(across, south, quarter):
    return pl.pallas_call(
        norm_kernel,
        grid=(1,),
        in_specs=[
            pl.BlockSpec((1, 2, 2, PAD, 768), lambda g: (3, 0, 1, 0, 0)),
            pl.BlockSpec((1, 2, 2, PAD, 768), lambda g: (3, 0, 2, 0, 0)),
            pl.BlockSpec((1, 2, 4, PAD, 768), lambda g: (3, 0, 0, 0, 0)),
            whole_spec((256, 256)),
        ],
        out_specs=(whole_spec((4, 64, 768)), whole_spec((64, 128))),
        out_shape=(
            jax.ShapeDtypeStruct((4, 64, 768), jnp.float32),
            jax.ShapeDtypeStruct((64, 128), jnp.float32),
        ),
        compiler_params=params,
        name="normalise",
    )(across, across, south, quarter)


def merge_product(spots, near, far, weight, shuffle):
    return pl.pallas_call(
        merge_kernel,
        in_specs=[smem, vmem, vmem, vmem, vmem],
        out_specs=vmem,
        out_shape=jax.ShapeDtypeStruct((8, 64, 512), jnp.bfloat16),
        scratch_shapes=[pltpu.VMEM((384, 512), jnp.float32)],
        compiler_params=params,
        name="merge_product",
    )(spots, near, far, weight, shuffle)


def score_grads(recv, order, normed, inverse, gain, back, sums, across, south, probs):
    return pl.pallas_call(
        scores_kernel,
        grid=(STEPS,),
        in_specs=[
            whole_spec((8, 64, 512)),
            whole_spec((512, 384)),
            whole_spec((4, 64, 768)),
            whole_spec((64, 128)),
            whole_spec((4, 1, 768)),
            whole_spec((TOK, 256)),
            whole_spec((TOK, WIDE)),
            north_spec(2, 1),
            south_spec(2, 1),
            group_spec(4 * TOK, TOK),
        ],
        out_specs=(
            group_spec(TOK, 128),
            whole_spec((16, 8 * SHARE, 128)),
        ),
        out_shape=(
            jax.ShapeDtypeStruct((GROUPS, TOK, 128), jnp.bfloat16),
            jax.ShapeDtypeStruct((16, 8 * SHARE, 128), jnp.bfloat16),
        ),
        scratch_shapes=[
            pltpu.VMEM((GROUPS, TOK, 128), jnp.bfloat16),
            pltpu.VMEM((GROUPS, 4 * ROWS, WIDE), jnp.float32),
        ],
        compiler_params=large,
        name="score_grads",
    )(recv, order, normed, inverse, gain, back, sums, across, south, probs)


def close_table(parts, close):
    return pl.pallas_call(
        close_kernel,
        in_specs=[vmem, vmem],
        out_specs=vmem,
        out_shape=jax.ShapeDtypeStruct((1, HEADS, 3312), jnp.float32),
        scratch_shapes=[pltpu.VMEM((3, ROWS * HEADS, 128), jnp.float32)],
        compiler_params=params,
        name="close_table",
    )(parts, close)


def window_grads(across, south, o_win, probs):
    return pl.pallas_call(
        grads_kernel,
        grid=(STEPS,),
        in_specs=[
            north_spec(0, 3),
            south_spec(0, 3),
            group_spec(TOK, 128),
            group_spec(4 * TOK, TOK),
        ],
        out_specs=pl.BlockSpec((3, TOK, PER * 128), lambda g: (0, 0, g)),
        out_shape=jax.ShapeDtypeStruct((3, TOK, 768), jnp.bfloat16),
        compiler_params=large,
        name="window_grads",
    )(across, south, o_win, probs)


def from_behind(shard, axis, by):
    size = lax.axis_size(axis)
    return lax.ppermute(shard, axis, [(i, (i + by) % size) for i in range(size)])


def partner(shard, axis, bit):
    return lax.ppermute(shard, axis, [(i, i ^ bit) for i in range(lax.axis_size(axis))])


def swap(shard, axis, groups):
    return lax.all_to_all(shard, axis, 0, 0, tiled=True, axis_index_groups=groups)


def share(shard, count, axis, groups):
    return swap(jnp.broadcast_to(shard[None], (count,) + shard.shape), axis, groups)


def on_device(y_block, merge_gain, merge_weight, d_merged, q_proj, k_proj, v_proj, bias_table):
    sums, spread, quarter, back, order, shuffle, open_up, close = layout_constants()
    lat = lax.axis_index("lat")

    packed = pack_weight(lat.reshape(1), merge_weight)

    tokens = jnp.arange(TOK, dtype=jnp.int32)
    upper = tokens // PAD % 6 >= 3
    allowed = jnp.logical_or(upper[:, None] == upper[None, :], lat != LAT - 1)
    allowed = jnp.logical_and(allowed, (tokens % PAD < 12)[None, :])
    mask = jnp.where(allowed, 0.0, LOW)

    packed, d_merged = lax.optimization_barrier((packed, d_merged))
    weight_z = swap(packed, "lon", z_groups).reshape(NZ * 24, 384)
    eastern_d = from_behind(d_merged[:, :, :3], "lon", -1)
    d_rows = jnp.concatenate(
        [d_merged[:, :, 3:], eastern_d, jnp.zeros_like(d_merged[:, :, :2])], axis=2
    ).reshape(48, -1)
    d_rows = jnp.concatenate([d_rows, partner(d_rows, "lat", 2)], axis=0)
    near = jnp.concatenate([d_rows, partner(d_rows, "lon", NY * NZ)], axis=0)
    far = partner(near, "lat", 1)
    me = (lax.axis_index("lon") // (NY * NZ)) * LAT + lat
    rel = jnp.bitwise_xor(jnp.arange(8, dtype=jnp.int32), me)
    spots = (rel % 2 * 4 + rel // 4 * 2 + rel // 2 % 2) * 48

    weight = share(weight_z, NY, "lon", y_groups)
    table = open_table(bias_table, open_up)

    eastern = from_behind(
        jnp.stack([q_proj[:, :, :6], k_proj[:, :, :6], v_proj[:, :, :6], y_block[:, :, :6]]),
        "lon",
        -1,
    )
    across = jnp.concatenate(
        [
            jnp.stack([q_proj[:, :, 6:], k_proj[:, :, 6:], v_proj[:, :, 6:], y_block[:, :, 6:]]),
            eastern,
            jnp.zeros_like(eastern[:, :, :, :4]),
        ],
        axis=3,
    )
    south = from_behind(across[:, :, :4], "lat", -1)

    weight, table, mask = lax.optimization_barrier((weight, table, mask))
    parts = merge_product(spots, near, far, weight, shuffle)
    recv = swap(parts, ("lon", "lat"), x_lat_groups)

    table, quarter, _ = lax.optimization_barrier((table, quarter, parts))
    probs = window_probs(across, south, table, spread, mask)
    normed, inverse = normalise(across, south, quarter)

    o_win, table_part = score_grads(
        recv, order, normed, inverse, merge_gain.reshape(4, 1, 768), back, sums, across, south, probs
    )

    table_part = swap(table_part, "lon", near_groups).astype(jnp.float32)
    table_part = jnp.sum(table_part, axis=0).astype(jnp.bfloat16)
    grads = window_grads(across, south, o_win, probs)
    grid = grads.reshape(3, 2, 6, PAD, 768)[:, :, :, :12]
    southern = from_behind(grid[:, :, 3:], "lat", 1)
    fixed = jnp.concatenate([southern, grid[:, :, :3]], axis=2)

    table_part = share(table_part, NZ // 2, "lon", far_groups)
    table_part, fixed = lax.optimization_barrier((table_part, fixed))
    western = from_behind(fixed[:, :, :, 6:], "lon", 1)
    finished = jnp.concatenate([western, fixed[:, :, :, :6]], axis=3)

    table_part = jnp.sum(table_part.astype(jnp.float32), axis=0).astype(jnp.bfloat16)
    table_grad = close_table(share(table_part, 16, "lon", near_groups), close)
    return (finished[0], finished[1], finished[2], table_grad)


def solution(mesh):
    placed = (
        P(None, "lat", "lon", None),
        P(),
        P("lon", None),
        P(None, "lat", "lon", None),
        P(None, "lat", "lon", None),
        P(None, "lat", "lon", None),
        P(None, "lat", "lon", None),
        P("lat", None, None),
    )
    return jax.shard_map(
        on_device,
        mesh=mesh,
        in_specs=placed,
        out_specs=(
            P(None, "lat", "lon", None),
            P(None, "lat", "lon", None),
            P(None, "lat", "lon", None),
            P("lat", None, None),
        ),
        check_vma=False,
    )
```

```python
import jax
import jax.numpy as jnp
import numpy as np
from jax import lax
from jax.experimental import pallas as pl
from jax.experimental.pallas import tpu as pltpu
from jax.sharding import PartitionSpec as P

NX, NY, NZ = 2, 4, 16
LAT = 4
HEADS = 24
ROWS = 12
PAD = 16
TOK = ROWS * PAD
SEG = 32
WIDE = ROWS * SEG
GROUPS = 6
PER = 3
STEPS = GROUPS // PER
SHARE = 7
LOW = -1e30
SMALL = 12 * 1024 * 1024
LARGE = 56 * 1024 * 1024
score_factor = 32 ** (-0.5)

z_groups = [[a * NZ + z for z in range(NZ)] for a in range(NX * NY)]
y_groups = [[(x * NY + y) * NZ + z for y in range(NY)] for x in range(NX) for z in range(NZ)]
near_groups = [
    [a * NZ + 2 * pair + e for a in range(NX * NY) for e in range(2)] for pair in range(NZ // 2)
]
far_groups = [
    [a * NZ + 2 * pair + e for pair in range(NZ // 2)] for a in range(NX * NY) for e in range(2)
]
x_lat_groups = [
    [(x * NY * NZ + b) * LAT + l for x in range(NX) for l in range(LAT)] for b in range(NY * NZ)
]


def layout_constants():
    tokens = np.arange(TOK)
    row, col = tokens // PAD, tokens % PAD
    real = col < 12
    sums = np.zeros((TOK, WIDE), np.float32)
    sums[tokens[real], (row * SEG + 11 - col)[real]] = 1
    spread = np.zeros((WIDE, TOK), np.float32)
    spread[(row * SEG + 11 + col)[real], tokens[real]] = 1
    quarter = np.zeros((256, 256), np.float32)
    back = np.zeros((TOK, 256), np.float32)
    for level in range(2):
        for pr in range(4):
            for pc in range(6):
                for di in range(2):
                    for dj in range(2):
                        spot = (di + 2 * dj) * 64 + (level * 4 + pr) * 8 + pc
                        fine_row, fine_col = 2 * pr + di, 2 * pc + dj
                        quarter[spot, (level * 8 + fine_row) * PAD + fine_col] = 1
                        if 1 <= fine_row <= 6:
                            back[(level * 6 + fine_row - 1) * PAD + fine_col, spot] = 1
    shuffle = np.zeros((512, 384), np.float32)
    order = np.zeros((512, 384), np.float32)
    for l in range(4):
        for z in range(NZ):
            for i in range(6):
                shuffle[l * 128 + z * 6 + i, z * 24 + l * 6 + i] = 1
                order[l * 128 + z * 6 + i, z * 24 + l * 6 + i] = 1
    open_up = np.zeros((2, 138, WIDE), np.float32)
    for half in range(2):
        for r in range(6):
            for d in range(23):
                open_up[half, r * 23 + d, half * 192 + r * SEG + 22 - d] = 1
    close = np.zeros((WIDE, 512), np.float32)
    for b in range(ROWS):
        for d in range(23):
            close[b * SEG + d, b // 6 * 256 + b % 6 * 23 + d] = 1
    all_of = (sums, spread, quarter, back, order, shuffle, open_up, close)
    return [jnp.asarray(a, jnp.bfloat16) for a in all_of]


def dot(a, b, dims=((1,), (0,))):
    return lax.dot_general(a, b, (dims, ((), ())), preferred_element_type=jnp.float32)


def head_mask(h):
    lanes = lax.broadcasted_iota(jnp.int32, (1, 128), 1)
    return (lanes // 32) == h


def by_head(block):
    return jnp.concatenate(
        [jnp.where(head_mask(h), block, jnp.zeros_like(block)) for h in range(4)], axis=0
    )


def split_dot(values, matrix):
    high = values.astype(jnp.bfloat16)
    low = (values - high.astype(jnp.float32)).astype(jnp.bfloat16)
    return dot(high, matrix) + dot(low, matrix)


def window(north_ref, south_ref, which, group):
    lanes = slice(group * 128, (group + 1) * 128)
    pieces = []
    for level in range(2):
        pieces.append(north_ref[which, level, :, :, lanes].reshape(48, 128))
        pieces.append(south_ref[which, level, 0:3, :, lanes].reshape(48, 128))
    return jnp.concatenate(pieces, axis=0)


def pack_kernel(lat_ref, w_ref, out_ref):
    first = lat_ref[0] * 6
    to = lax.broadcasted_iota(jnp.int32, (24, 24), 0)
    source = lax.broadcasted_iota(jnp.int32, (24, 24), 1)
    total = jnp.zeros((24, 384), jnp.float32)
    for part in range(4):
        pick = jnp.logical_and(to // 6 == part, source == first + to - part * 6)
        pick = jnp.where(pick, 1.0, 0.0).astype(jnp.bfloat16)
        total += dot(pick, w_ref[:, part * 384 : (part + 1) * 384])
    packed = total.astype(jnp.bfloat16)
    for z in range(NZ):
        out_ref[z] = packed


def open_kernel(table_ref, open_ref, out_ref, wide_ref):
    halves = []
    for half in range(2):
        pieces = []
        for a in range(ROWS):
            first = (a // 6 * 2 + half) * 828 + a % 6 * 138
            pieces.append(table_ref[0, :, first : first + 138])
        halves.append(split_dot(jnp.concatenate(pieces, axis=0), open_ref[half]))
    whole = halves[0] + halves[1]
    for s in range(3):
        wide_ref[s] = whole[:, s * 128 : (s + 1) * 128]
    for head in range(HEADS):
        row = head % 4 * ROWS
        for s in range(3):
            out_ref[head // 4, row : row + ROWS, s * 128 : (s + 1) * 128] = wide_ref[
                s, pl.ds(head, ROWS, stride=HEADS), :
            ]


def probs_kernel(north_ref, south_ref, table_ref, spread_ref, mask_ref, p_ref):
    for group in range(PER):
        pieces = []
        for s in range(3):
            table = table_ref[group, :, s * 128 : (s + 1) * 128]
            table = jnp.broadcast_to(table[:, None, :], (4 * ROWS, PAD, 128))
            pieces.append(pltpu.roll(table, 0, 2, stride=1, stride_axis=1))
        wide = jnp.concatenate(pieces, axis=2).reshape(4 * TOK, WIDE)
        q_win = window(north_ref, south_ref, 0, group)
        k_win = window(north_ref, south_ref, 1, group)
        scores = dot(by_head(q_win), k_win, ((1,), (1,))) * score_factor
        scores = scores + split_dot(wide, spread_ref[...])
        scores = (scores.reshape(4, TOK, TOK) + mask_ref[...][None]).reshape(4 * TOK, TOK)
        expon = jnp.exp(scores - jnp.max(scores, axis=-1, keepdims=True))
        probs = expon * (1.0 / jnp.sum(expon, axis=-1, keepdims=True))
        p_ref[group] = probs.astype(jnp.bfloat16)


def norm_kernel(a_ref, b_ref, south_ref, quarter_ref, normed_ref, inverse_ref):
    pieces = []
    for level in range(2):
        pieces.append(a_ref[0, level].reshape(32, 768))
        pieces.append(b_ref[0, level].reshape(32, 768))
        pieces.append(south_ref[0, level].reshape(64, 768))
    fields = dot(quarter_ref[...], jnp.concatenate(pieces, axis=0))
    parts = [fields[q * 64 : (q + 1) * 64] for q in range(4)]
    mean = jnp.sum(parts[0] + parts[1] + parts[2] + parts[3], axis=-1, keepdims=True) / 3072
    parts = [part - mean for part in parts]
    squares = [part * part for part in parts]
    variance = (
        jnp.sum(squares[0] + squares[1] + squares[2] + squares[3], axis=-1, keepdims=True) / 3072
    )
    inverse = lax.rsqrt(variance + 1e-05)
    for q in range(4):
        normed_ref[q] = parts[q] * inverse
    inverse_ref[...] = jnp.broadcast_to(inverse, (64, 128))


def merge_kernel(spot_ref, near_ref, far_ref, w_ref, shuffle_ref, out_ref, acc_ref):
    weights = [dot(shuffle_ref[...], w_ref[y]).astype(jnp.bfloat16) for y in range(NY)]
    near, far = None, None
    for part in range(4):
        rows, columns = slice(part * 128, part * 128 + 128), slice(part * 384, part * 384 + 384)
        weight = jnp.concatenate([weights[y][rows] for y in range(NY)], axis=0)
        near_part = dot(near_ref[:, columns], weight, ((1,), (1,)))
        far_part = dot(far_ref[:, columns], weight, ((1,), (1,)))
        near = near_part if part == 0 else near + near_part
        far = far_part if part == 0 else far + far_part
    acc_ref[:192] = near
    acc_ref[192:] = far
    for x in range(NX):
        for l in range(LAT):
            for level in range(2):
                own = pl.multiple_of(spot_ref[x * LAT + l] + level * 24 + 8, 8)
                below = pl.multiple_of(spot_ref[x * LAT + (l + 1) % LAT] + level * 24, 8)
                out_ref[x * LAT + l, level * 32 : level * 32 + 16] = acc_ref[
                    pl.ds(own, 16)
                ].astype(jnp.bfloat16)
                out_ref[x * LAT + l, level * 32 + 16 : level * 32 + 32] = acc_ref[
                    pl.ds(below, 16)
                ].astype(jnp.bfloat16)


def score_grad(probs, o_win, v_win):
    d_probs = dot(by_head(o_win), v_win, ((1,), (1,)))
    probs = probs.astype(jnp.float32)
    delta = jnp.sum(probs * d_probs, axis=-1, keepdims=True)
    return (probs * (d_probs - delta)).astype(jnp.bfloat16)


def scores_kernel(
    recv_ref,
    order_ref,
    normed_ref,
    inverse_ref,
    gain_ref,
    back_ref,
    sums_ref,
    north_ref,
    south_ref,
    p_ref,
    o_out_ref,
    table_ref,
    o_ref,
    sum_ref,
):
    g = pl.program_id(0)

    @pl.when(g == 0)
    def _():
        pieces = [
            jnp.concatenate(
                [recv_ref[x * LAT + l, :, y * 128 : (y + 1) * 128] for l in range(LAT)], axis=1
            )
            for x in range(NX)
            for y in range(NY)
        ]
        d_norm = dot(jnp.concatenate(pieces, axis=0), order_ref[...])
        hats = []
        for q in range(4):
            left = d_norm[(2 * q) * 64 : (2 * q + 1) * 64]
            right = d_norm[(2 * q + 1) * 64 : (2 * q + 2) * 64]
            hats.append(jnp.concatenate([left, right], axis=1) * gain_ref[q])
        mean = jnp.sum(hats[0] + hats[1] + hats[2] + hats[3], axis=-1, keepdims=True) / 3072
        cross = [hats[q] * normed_ref[q] for q in range(4)]
        along = jnp.sum(cross[0] + cross[1] + cross[2] + cross[3], axis=-1, keepdims=True) / 3072
        inverse = inverse_ref[:, 0:1]
        stack = [(hats[q] - mean - normed_ref[q] * along) * inverse for q in range(4)]
        d_out = dot(back_ref[...], jnp.concatenate(stack, axis=0).astype(jnp.bfloat16))
        d_out = d_out.astype(jnp.bfloat16)
        for s in range(GROUPS):
            o_ref[s] = d_out[:, s * 128 : (s + 1) * 128]

    for group in range(PER):
        o_win = o_ref[g * PER + group]
        o_out_ref[group] = o_win
        d_low = score_grad(p_ref[group], o_win, window(north_ref, south_ref, 0, group))
        spread = dot(d_low, sums_ref[...]).reshape(4 * ROWS, PAD, WIDE)
        for s in range(3):
            lanes = slice(s * 128, (s + 1) * 128)
            turned = pltpu.roll(spread[:, :, lanes], 0, 2, stride=1, stride_axis=1)
            sum_ref[g * PER + group, :, lanes] = jnp.sum(turned, axis=1)

    @pl.when(g == STEPS - 1)
    def _():
        whole = jnp.concatenate([sum_ref[s] for s in range(GROUPS)], axis=0)
        tiles = [
            whole[r * 8 : (r + 1) * 8, s * 128 : (s + 1) * 128] for s in range(3) for r in range(36)
        ]
        tiles += [jnp.zeros((8, 128), jnp.float32)] * (16 * SHARE - len(tiles))
        for part in range(16):
            chunk = jnp.concatenate(tiles[part * SHARE : (part + 1) * SHARE], axis=0)
            table_ref[part] = chunk.astype(jnp.bfloat16)


def close_kernel(parts_ref, close_ref, out_ref, wide_ref):
    for part in range(16):
        chunk = parts_ref[part].astype(jnp.float32)
        for k in range(SHARE):
            s, r = divmod(part * SHARE + k, 36)
            if s < 3:
                wide_ref[s, r * 8 : (r + 1) * 8] = chunk[k * 8 : (k + 1) * 8]
    rows = []
    for a in range(ROWS):
        lanes = [wide_ref[s, pl.ds(a, HEADS, stride=ROWS), :] for s in range(3)]
        rows.append(jnp.concatenate(lanes, axis=1))
    dense = dot(jnp.concatenate(rows, axis=0).astype(jnp.bfloat16), close_ref[...])
    for a in range(ROWS):
        for half in range(2):
            first = (a // 6 * 2 + half) * 828 + a % 6 * 138
            out_ref[0, :, first : first + 138] = dense[
                a * HEADS : (a + 1) * HEADS, half * 256 : half * 256 + 138
            ]


def grads_kernel(north_ref, south_ref, o_ref, p_ref, grads_ref):
    for group in range(PER):
        lanes = slice(group * 128, (group + 1) * 128)
        q_win = window(north_ref, south_ref, 0, group)
        k_win = window(north_ref, south_ref, 1, group)
        o_win, p_low = o_ref[group], p_ref[group]
        d_low = score_grad(p_low, o_win, window(north_ref, south_ref, 2, group))
        q_all = dot(d_low, k_win)
        q_grad = jnp.zeros((TOK, 128), jnp.float32)
        for h in range(4):
            q_grad = jnp.where(head_mask(h), q_all[h * TOK : (h + 1) * TOK], q_grad)
        grads_ref[0, :, lanes] = (q_grad * score_factor).astype(jnp.bfloat16)

        q_turn = q_win.astype(jnp.float32).T.astype(jnp.bfloat16)
        o_turn = o_win.astype(jnp.float32).T.astype(jnp.bfloat16)
        k_parts, v_parts = [], []
        for h in range(4):
            rows = slice(h * 32, (h + 1) * 32)
            k_parts.append(dot(q_turn[rows], d_low[h * TOK : (h + 1) * TOK]))
            v_parts.append(dot(o_turn[rows], p_low[h * TOK : (h + 1) * TOK]))
        k_grad = jnp.concatenate(k_parts, axis=0).T
        v_grad = jnp.concatenate(v_parts, axis=0).T
        grads_ref[1, :, lanes] = (k_grad * score_factor).astype(jnp.bfloat16)
        grads_ref[2, :, lanes] = v_grad.astype(jnp.bfloat16)


def whole_spec(shape):
    return pl.BlockSpec(shape, lambda *_: (0,) * len(shape))


def north_spec(first, count):
    return pl.BlockSpec((count, 2, 3, PAD, PER * 128), lambda g: (first // count, 0, 1, 0, g))


def south_spec(first, count):
    return pl.BlockSpec((count, 2, 4, PAD, PER * 128), lambda g: (first // count, 0, 0, 0, g))


def group_spec(rows, columns):
    return pl.BlockSpec((PER, rows, columns), lambda g: (g, 0, 0))


params = pltpu.CompilerParams(vmem_limit_bytes=SMALL)
large = pltpu.CompilerParams(vmem_limit_bytes=LARGE)
smem = pl.BlockSpec(memory_space=pltpu.SMEM)
vmem = pl.BlockSpec(memory_space=pltpu.VMEM)


def pack_weight(lat, weight):
    return pl.pallas_call(
        pack_kernel,
        in_specs=[smem, vmem],
        out_specs=vmem,
        out_shape=jax.ShapeDtypeStruct((NZ, 24, 384), jnp.bfloat16),
        compiler_params=params,
        name="pack_weight",
    )(lat, weight)


def open_table(table, open_up):
    return pl.pallas_call(
        open_kernel,
        in_specs=[vmem, vmem],
        out_specs=vmem,
        out_shape=jax.ShapeDtypeStruct((GROUPS, 4 * ROWS, WIDE), jnp.float32),
        scratch_shapes=[pltpu.VMEM((3, ROWS * HEADS, 128), jnp.float32)],
        compiler_params=params,
        name="open_table",
    )(table, open_up)


def window_probs(across, south, table, spread, mask):
    return pl.pallas_call(
        probs_kernel,
        grid=(STEPS,),
        in_specs=[
            north_spec(0, 2),
            south_spec(0, 2),
            group_spec(4 * ROWS, WIDE),
            whole_spec((WIDE, TOK)),
            whole_spec((TOK, TOK)),
        ],
        out_specs=group_spec(4 * TOK, TOK),
        out_shape=jax.ShapeDtypeStruct((GROUPS, 4 * TOK, TOK), jnp.bfloat16),
        compiler_params=large,
        name="window_probs",
    )(across, south, table, spread, mask)


def normalise(across, south, quarter):
    return pl.pallas_call(
        norm_kernel,
        grid=(1,),
        in_specs=[
            pl.BlockSpec((1, 2, 2, PAD, 768), lambda g: (3, 0, 1, 0, 0)),
            pl.BlockSpec((1, 2, 2, PAD, 768), lambda g: (3, 0, 2, 0, 0)),
            pl.BlockSpec((1, 2, 4, PAD, 768), lambda g: (3, 0, 0, 0, 0)),
            whole_spec((256, 256)),
        ],
        out_specs=(whole_spec((4, 64, 768)), whole_spec((64, 128))),
        out_shape=(
            jax.ShapeDtypeStruct((4, 64, 768), jnp.float32),
            jax.ShapeDtypeStruct((64, 128), jnp.float32),
        ),
        compiler_params=params,
        name="normalise",
    )(across, across, south, quarter)


def merge_product(spots, near, far, weight, shuffle):
    return pl.pallas_call(
        merge_kernel,
        in_specs=[smem, vmem, vmem, vmem, vmem],
        out_specs=vmem,
        out_shape=jax.ShapeDtypeStruct((8, 64, 512), jnp.bfloat16),
        scratch_shapes=[pltpu.VMEM((384, 512), jnp.float32)],
        compiler_params=params,
        name="merge_product",
    )(spots, near, far, weight, shuffle)


def score_grads(recv, order, normed, inverse, gain, back, sums, across, south, probs):
    return pl.pallas_call(
        scores_kernel,
        grid=(STEPS,),
        in_specs=[
            whole_spec((8, 64, 512)),
            whole_spec((512, 384)),
            whole_spec((4, 64, 768)),
            whole_spec((64, 128)),
            whole_spec((4, 1, 768)),
            whole_spec((TOK, 256)),
            whole_spec((TOK, WIDE)),
            north_spec(2, 1),
            south_spec(2, 1),
            group_spec(4 * TOK, TOK),
        ],
        out_specs=(
            group_spec(TOK, 128),
            whole_spec((16, 8 * SHARE, 128)),
        ),
        out_shape=(
            jax.ShapeDtypeStruct((GROUPS, TOK, 128), jnp.bfloat16),
            jax.ShapeDtypeStruct((16, 8 * SHARE, 128), jnp.bfloat16),
        ),
        scratch_shapes=[
            pltpu.VMEM((GROUPS, TOK, 128), jnp.bfloat16),
            pltpu.VMEM((GROUPS, 4 * ROWS, WIDE), jnp.float32),
        ],
        compiler_params=large,
        name="score_grads",
    )(recv, order, normed, inverse, gain, back, sums, across, south, probs)


def close_table(parts, close):
    return pl.pallas_call(
        close_kernel,
        in_specs=[vmem, vmem],
        out_specs=vmem,
        out_shape=jax.ShapeDtypeStruct((1, HEADS, 3312), jnp.float32),
        scratch_shapes=[pltpu.VMEM((3, ROWS * HEADS, 128), jnp.float32)],
        compiler_params=params,
        name="close_table",
    )(parts, close)


def window_grads(across, south, o_win, probs):
    return pl.pallas_call(
        grads_kernel,
        grid=(STEPS,),
        in_specs=[
            north_spec(0, 3),
            south_spec(0, 3),
            group_spec(TOK, 128),
            group_spec(4 * TOK, TOK),
        ],
        out_specs=pl.BlockSpec((3, TOK, PER * 128), lambda g: (0, 0, g)),
        out_shape=jax.ShapeDtypeStruct((3, TOK, 768), jnp.bfloat16),
        compiler_params=large,
        name="window_grads",
    )(across, south, o_win, probs)


def from_behind(shard, axis, by):
    size = lax.axis_size(axis)
    return lax.ppermute(shard, axis, [(i, (i + by) % size) for i in range(size)])


def partner(shard, axis, bit):
    return lax.ppermute(shard, axis, [(i, i ^ bit) for i in range(lax.axis_size(axis))])


def swap(shard, axis, groups):
    return lax.all_to_all(shard, axis, 0, 0, tiled=True, axis_index_groups=groups)


def share(shard, count, axis, groups):
    return swap(jnp.broadcast_to(shard[None], (count,) + shard.shape), axis, groups)


def on_device(y_block, merge_gain, merge_weight, d_merged, q_proj, k_proj, v_proj, bias_table):
    sums, spread, quarter, back, order, shuffle, open_up, close = layout_constants()
    lat = lax.axis_index("lat")

    packed = pack_weight(lat.reshape(1), merge_weight)

    tokens = jnp.arange(TOK, dtype=jnp.int32)
    upper = tokens // PAD % 6 >= 3
    allowed = jnp.logical_or(upper[:, None] == upper[None, :], lat != LAT - 1)
    allowed = jnp.logical_and(allowed, (tokens % PAD < 12)[None, :])
    mask = jnp.where(allowed, 0.0, LOW)

    packed, d_merged = lax.optimization_barrier((packed, d_merged))
    weight_z = swap(packed, "lon", z_groups).reshape(NZ * 24, 384)
    eastern_d = from_behind(d_merged[:, :, :3], "lon", -1)
    d_rows = jnp.concatenate(
        [d_merged[:, :, 3:], eastern_d, jnp.zeros_like(d_merged[:, :, :2])], axis=2
    ).reshape(48, -1)
    d_rows = jnp.concatenate([d_rows, partner(d_rows, "lat", 2)], axis=0)
    near = jnp.concatenate([d_rows, partner(d_rows, "lon", NY * NZ)], axis=0)
    far = partner(near, "lat", 1)
    me = (lax.axis_index("lon") // (NY * NZ)) * LAT + lat
    rel = jnp.bitwise_xor(jnp.arange(8, dtype=jnp.int32), me)
    spots = (rel % 2 * 4 + rel // 4 * 2 + rel // 2 % 2) * 48

    weight = share(weight_z, NY, "lon", y_groups)
    table = open_table(bias_table, open_up)

    eastern = from_behind(
        jnp.stack([q_proj[:, :, :6], k_proj[:, :, :6], v_proj[:, :, :6], y_block[:, :, :6]]),
        "lon",
        -1,
    )
    across = jnp.concatenate(
        [
            jnp.stack([q_proj[:, :, 6:], k_proj[:, :, 6:], v_proj[:, :, 6:], y_block[:, :, 6:]]),
            eastern,
            jnp.zeros_like(eastern[:, :, :, :4]),
        ],
        axis=3,
    )
    south = from_behind(across[:, :, :4], "lat", -1)

    weight, table, mask = lax.optimization_barrier((weight, table, mask))
    parts = merge_product(spots, near, far, weight, shuffle)
    recv = swap(parts, ("lon", "lat"), x_lat_groups)

    south, _ = lax.optimization_barrier((south, parts))
    probs = window_probs(across, south, table, spread, mask)
    normed, inverse = normalise(across, south, quarter)

    o_win, table_part = score_grads(
        recv, order, normed, inverse, merge_gain.reshape(4, 1, 768), back, sums, across, south, probs
    )

    table_part = swap(table_part, "lon", near_groups).astype(jnp.float32)
    table_part = jnp.sum(table_part, axis=0).astype(jnp.bfloat16)
    grads = window_grads(across, south, o_win, probs)
    grid = grads.reshape(3, 2, 6, PAD, 768)[:, :, :, :12]
    western = from_behind(grid[:, :, :, 6:], "lon", 1)
    fixed = jnp.concatenate([western, grid[:, :, :, :6]], axis=3)
    southern = from_behind(fixed[:, :, 3:], "lat", 1)
    finished = jnp.concatenate([southern, fixed[:, :, :3]], axis=2)

    table_part = share(table_part, NZ // 2, "lon", far_groups)
    table_part = jnp.sum(table_part.astype(jnp.float32), axis=0).astype(jnp.bfloat16)
    table_grad = close_table(share(table_part, 16, "lon", near_groups), close)
    return (finished[0], finished[1], finished[2], table_grad)


def solution(mesh):
    placed = (
        P(None, "lat", "lon", None),
        P(),
        P("lon", None),
        P(None, "lat", "lon", None),
        P(None, "lat", "lon", None),
        P(None, "lat", "lon", None),
        P(None, "lat", "lon", None),
        P("lat", None, None),
    )
    return jax.shard_map(
        on_device,
        mesh=mesh,
        in_specs=placed,
        out_specs=(
            P(None, "lat", "lon", None),
            P(None, "lat", "lon", None),
            P(None, "lat", "lon", None),
            P("lat", None, None),
        ),
        check_vma=False,
    )
```

```python
import jax
import jax.numpy as jnp
import numpy as np
from jax import lax
from jax.experimental import pallas as pl
from jax.experimental.pallas import tpu as pltpu
from jax.sharding import PartitionSpec as P

NX, NY, NZ = 2, 4, 16
LAT = 4
HEADS = 24
ROWS = 12
PAD = 16
TOK = ROWS * PAD
SEG = 32
WIDE = ROWS * SEG
GROUPS = 6
PER = 3
STEPS = GROUPS // PER
SHARE = 7
LOW = -1e30
SMALL = 12 * 1024 * 1024
LARGE = 56 * 1024 * 1024
score_factor = 32 ** (-0.5)

z_groups = [[a * NZ + z for z in range(NZ)] for a in range(NX * NY)]
y_groups = [[(x * NY + y) * NZ + z for y in range(NY)] for x in range(NX) for z in range(NZ)]
near_groups = [
    [a * NZ + 2 * pair + e for a in range(NX * NY) for e in range(2)] for pair in range(NZ // 2)
]
far_groups = [
    [a * NZ + 2 * pair + e for pair in range(NZ // 2)] for a in range(NX * NY) for e in range(2)
]
x_lat_groups = [
    [(x * NY * NZ + b) * LAT + l for x in range(NX) for l in range(LAT)] for b in range(NY * NZ)
]


def layout_constants():
    tokens = np.arange(TOK)
    row, col = tokens // PAD, tokens % PAD
    real = col < 12
    sums = np.zeros((TOK, WIDE), np.float32)
    sums[tokens[real], (row * SEG + 11 - col)[real]] = 1
    spread = np.zeros((WIDE, TOK), np.float32)
    spread[(row * SEG + 11 + col)[real], tokens[real]] = 1
    quarter = np.zeros((256, 256), np.float32)
    back = np.zeros((TOK, 256), np.float32)
    for level in range(2):
        for pr in range(4):
            for pc in range(6):
                for di in range(2):
                    for dj in range(2):
                        spot = (di + 2 * dj) * 64 + (level * 4 + pr) * 8 + pc
                        fine_row, fine_col = 2 * pr + di, 2 * pc + dj
                        quarter[spot, (level * 8 + fine_row) * PAD + fine_col] = 1
                        if 1 <= fine_row <= 6:
                            back[(level * 6 + fine_row - 1) * PAD + fine_col, spot] = 1
    shuffle = np.zeros((512, 384), np.float32)
    order = np.zeros((512, 384), np.float32)
    for l in range(4):
        for z in range(NZ):
            for i in range(6):
                shuffle[l * 128 + z * 6 + i, z * 24 + l * 6 + i] = 1
                order[l * 128 + z * 6 + i, z * 24 + l * 6 + i] = 1
    open_up = np.zeros((2, 138, WIDE), np.float32)
    for half in range(2):
        for r in range(6):
            for d in range(23):
                open_up[half, r * 23 + d, half * 192 + r * SEG + 22 - d] = 1
    close = np.zeros((WIDE, 512), np.float32)
    for b in range(ROWS):
        for d in range(23):
            close[b * SEG + d, b // 6 * 256 + b % 6 * 23 + d] = 1
    all_of = (sums, spread, quarter, back, order, shuffle, open_up, close)
    return [jnp.asarray(a, jnp.bfloat16) for a in all_of]


def dot(a, b, dims=((1,), (0,))):
    return lax.dot_general(a, b, (dims, ((), ())), preferred_element_type=jnp.float32)


def head_mask(h):
    lanes = lax.broadcasted_iota(jnp.int32, (1, 128), 1)
    return (lanes // 32) == h


def by_head(block):
    return jnp.concatenate(
        [jnp.where(head_mask(h), block, jnp.zeros_like(block)) for h in range(4)], axis=0
    )


def split_dot(values, matrix):
    high = values.astype(jnp.bfloat16)
    low = (values - high.astype(jnp.float32)).astype(jnp.bfloat16)
    return dot(high, matrix) + dot(low, matrix)


def window(north_ref, south_ref, which, group):
    lanes = slice(group * 128, (group + 1) * 128)
    pieces = []
    for level in range(2):
        pieces.append(north_ref[which, level, :, :, lanes].reshape(48, 128))
        pieces.append(south_ref[which, level, 0:3, :, lanes].reshape(48, 128))
    return jnp.concatenate(pieces, axis=0)


def pack_kernel(lat_ref, w_ref, out_ref):
    first = lat_ref[0] * 6
    to = lax.broadcasted_iota(jnp.int32, (24, 24), 0)
    source = lax.broadcasted_iota(jnp.int32, (24, 24), 1)
    total = jnp.zeros((24, 384), jnp.float32)
    for part in range(4):
        pick = jnp.logical_and(to // 6 == part, source == first + to - part * 6)
        pick = jnp.where(pick, 1.0, 0.0).astype(jnp.bfloat16)
        total += dot(pick, w_ref[:, part * 384 : (part + 1) * 384])
    packed = total.astype(jnp.bfloat16)
    for z in range(NZ):
        out_ref[z] = packed


def open_kernel(table_ref, open_ref, out_ref, wide_ref):
    halves = []
    for half in range(2):
        pieces = []
        for a in range(ROWS):
            first = (a // 6 * 2 + half) * 828 + a % 6 * 138
            pieces.append(table_ref[0, :, first : first + 138])
        halves.append(split_dot(jnp.concatenate(pieces, axis=0), open_ref[half]))
    whole = halves[0] + halves[1]
    for s in range(3):
        wide_ref[s] = whole[:, s * 128 : (s + 1) * 128]
    for head in range(HEADS):
        row = head % 4 * ROWS
        for s in range(3):
            out_ref[head // 4, row : row + ROWS, s * 128 : (s + 1) * 128] = wide_ref[
                s, pl.ds(head, ROWS, stride=HEADS), :
            ]


def probs_kernel(north_ref, south_ref, table_ref, spread_ref, mask_ref, p_ref):
    for group in range(PER):
        pieces = []
        for s in range(3):
            table = table_ref[group, :, s * 128 : (s + 1) * 128]
            table = jnp.broadcast_to(table[:, None, :], (4 * ROWS, PAD, 128))
            pieces.append(pltpu.roll(table, 0, 2, stride=1, stride_axis=1))
        wide = jnp.concatenate(pieces, axis=2).reshape(4 * TOK, WIDE)
        q_win = window(north_ref, south_ref, 0, group)
        k_win = window(north_ref, south_ref, 1, group)
        scores = dot(by_head(q_win), k_win, ((1,), (1,))) * score_factor
        scores = scores + split_dot(wide, spread_ref[...])
        scores = (scores.reshape(4, TOK, TOK) + mask_ref[...][None]).reshape(4 * TOK, TOK)
        expon = jnp.exp(scores - jnp.max(scores, axis=-1, keepdims=True))
        probs = expon * (1.0 / jnp.sum(expon, axis=-1, keepdims=True))
        p_ref[group] = probs.astype(jnp.bfloat16)


def normalise(a_ref, b_ref, south_ref, quarter_ref):
    pieces = []
    for level in range(2):
        pieces.append(a_ref[0, level].reshape(32, 768))
        pieces.append(b_ref[0, level].reshape(32, 768))
        pieces.append(south_ref[0, level].reshape(64, 768))
    fields = dot(quarter_ref[...], jnp.concatenate(pieces, axis=0))
    parts = [fields[q * 64 : (q + 1) * 64] for q in range(4)]
    mean = jnp.sum(parts[0] + parts[1] + parts[2] + parts[3], axis=-1, keepdims=True) / 3072
    parts = [part - mean for part in parts]
    squares = [part * part for part in parts]
    variance = (
        jnp.sum(squares[0] + squares[1] + squares[2] + squares[3], axis=-1, keepdims=True) / 3072
    )
    inverse = lax.rsqrt(variance + 1e-05)
    return [part * inverse for part in parts], inverse


def merge_kernel(spot_ref, near_ref, far_ref, w_ref, shuffle_ref, out_ref, acc_ref):
    weights = [dot(shuffle_ref[...], w_ref[y]).astype(jnp.bfloat16) for y in range(NY)]
    near, far = None, None
    for part in range(4):
        rows, columns = slice(part * 128, part * 128 + 128), slice(part * 384, part * 384 + 384)
        weight = jnp.concatenate([weights[y][rows] for y in range(NY)], axis=0)
        near_part = dot(near_ref[:, columns], weight, ((1,), (1,)))
        far_part = dot(far_ref[:, columns], weight, ((1,), (1,)))
        near = near_part if part == 0 else near + near_part
        far = far_part if part == 0 else far + far_part
    acc_ref[:192] = near
    acc_ref[192:] = far
    for x in range(NX):
        for l in range(LAT):
            for level in range(2):
                own = pl.multiple_of(spot_ref[x * LAT + l] + level * 24 + 8, 8)
                below = pl.multiple_of(spot_ref[x * LAT + (l + 1) % LAT] + level * 24, 8)
                out_ref[x * LAT + l, level * 32 : level * 32 + 16] = acc_ref[
                    pl.ds(own, 16)
                ].astype(jnp.bfloat16)
                out_ref[x * LAT + l, level * 32 + 16 : level * 32 + 32] = acc_ref[
                    pl.ds(below, 16)
                ].astype(jnp.bfloat16)


def score_grad(probs, o_win, v_win):
    d_probs = dot(by_head(o_win), v_win, ((1,), (1,)))
    probs = probs.astype(jnp.float32)
    delta = jnp.sum(probs * d_probs, axis=-1, keepdims=True)
    return (probs * (d_probs - delta)).astype(jnp.bfloat16)


def scores_kernel(
    recv_ref,
    order_ref,
    y_a_ref,
    y_b_ref,
    y_south_ref,
    quarter_ref,
    gain_ref,
    back_ref,
    sums_ref,
    north_ref,
    south_ref,
    p_ref,
    o_out_ref,
    table_ref,
):
    pieces = [
        jnp.concatenate(
            [recv_ref[x * LAT + l, :, y * 128 : (y + 1) * 128] for l in range(LAT)], axis=1
        )
        for x in range(NX)
        for y in range(NY)
    ]
    d_norm = dot(jnp.concatenate(pieces, axis=0), order_ref[...])
    hats = []
    for q in range(4):
        left = d_norm[(2 * q) * 64 : (2 * q + 1) * 64]
        right = d_norm[(2 * q + 1) * 64 : (2 * q + 2) * 64]
        hats.append(jnp.concatenate([left, right], axis=1) * gain_ref[q])
    mean = jnp.sum(hats[0] + hats[1] + hats[2] + hats[3], axis=-1, keepdims=True) / 3072
    normed, inverse = normalise(y_a_ref, y_b_ref, y_south_ref, quarter_ref)
    cross = [hats[q] * normed[q] for q in range(4)]
    along = jnp.sum(cross[0] + cross[1] + cross[2] + cross[3], axis=-1, keepdims=True) / 3072
    stack = [(hats[q] - mean - normed[q] * along) * inverse for q in range(4)]
    d_out = dot(back_ref[...], jnp.concatenate(stack, axis=0).astype(jnp.bfloat16))
    d_out = d_out.astype(jnp.bfloat16)

    sums = [[], [], []]
    for group in range(GROUPS):
        o_win = d_out[:, group * 128 : (group + 1) * 128]
        o_out_ref[group] = o_win
        d_low = score_grad(p_ref[group], o_win, window(north_ref, south_ref, 0, group))
        spread = dot(d_low, sums_ref[...]).reshape(4 * ROWS, PAD, WIDE)
        for s in range(3):
            part = spread[:, :, s * 128 : (s + 1) * 128]
            turned = pltpu.roll(part, 0, 2, stride=1, stride_axis=1)
            sums[s].append(jnp.sum(turned, axis=1))

    tiles = []
    for s in range(3):
        whole = jnp.concatenate(sums[s], axis=0)
        tiles += [whole[r * 8 : (r + 1) * 8] for r in range(36)]
    tiles += [jnp.zeros((8, 128), jnp.float32)] * (16 * SHARE - len(tiles))
    for part in range(16):
        chunk = jnp.concatenate(tiles[part * SHARE : (part + 1) * SHARE], axis=0)
        table_ref[part] = chunk.astype(jnp.bfloat16)


def close_kernel(parts_ref, close_ref, out_ref, wide_ref):
    for part in range(16):
        chunk = parts_ref[part].astype(jnp.float32)
        for k in range(SHARE):
            s, r = divmod(part * SHARE + k, 36)
            if s < 3:
                wide_ref[s, r * 8 : (r + 1) * 8] = chunk[k * 8 : (k + 1) * 8]
    rows = []
    for a in range(ROWS):
        lanes = [wide_ref[s, pl.ds(a, HEADS, stride=ROWS), :] for s in range(3)]
        rows.append(jnp.concatenate(lanes, axis=1))
    dense = dot(jnp.concatenate(rows, axis=0).astype(jnp.bfloat16), close_ref[...])
    for a in range(ROWS):
        for half in range(2):
            first = (a // 6 * 2 + half) * 828 + a % 6 * 138
            out_ref[0, :, first : first + 138] = dense[
                a * HEADS : (a + 1) * HEADS, half * 256 : half * 256 + 138
            ]


def grads_kernel(north_ref, south_ref, o_ref, p_ref, grads_ref):
    for group in range(PER):
        lanes = slice(group * 128, (group + 1) * 128)
        q_win = window(north_ref, south_ref, 0, group)
        k_win = window(north_ref, south_ref, 1, group)
        o_win, p_low = o_ref[group], p_ref[group]
        d_low = score_grad(p_low, o_win, window(north_ref, south_ref, 2, group))
        q_all = dot(d_low, k_win)
        q_grad = jnp.zeros((TOK, 128), jnp.float32)
        for h in range(4):
            q_grad = jnp.where(head_mask(h), q_all[h * TOK : (h + 1) * TOK], q_grad)
        grads_ref[0, :, lanes] = (q_grad * score_factor).astype(jnp.bfloat16)

        q_turn = q_win.astype(jnp.float32).T.astype(jnp.bfloat16)
        o_turn = o_win.astype(jnp.float32).T.astype(jnp.bfloat16)
        k_parts, v_parts = [], []
        for h in range(4):
            rows = slice(h * 32, (h + 1) * 32)
            k_parts.append(dot(q_turn[rows], d_low[h * TOK : (h + 1) * TOK]))
            v_parts.append(dot(o_turn[rows], p_low[h * TOK : (h + 1) * TOK]))
        k_grad = jnp.concatenate(k_parts, axis=0).T
        v_grad = jnp.concatenate(v_parts, axis=0).T
        grads_ref[1, :, lanes] = (k_grad * score_factor).astype(jnp.bfloat16)
        grads_ref[2, :, lanes] = v_grad.astype(jnp.bfloat16)


def whole_spec(shape):
    return pl.BlockSpec(shape, lambda *_: (0,) * len(shape))


def north_spec(first, count):
    return pl.BlockSpec((count, 2, 3, PAD, PER * 128), lambda g: (first // count, 0, 1, 0, g))


def south_spec(first, count):
    return pl.BlockSpec((count, 2, 4, PAD, PER * 128), lambda g: (first // count, 0, 0, 0, g))


def group_spec(rows, columns):
    return pl.BlockSpec((PER, rows, columns), lambda g: (g, 0, 0))


params = pltpu.CompilerParams(vmem_limit_bytes=SMALL)
large = pltpu.CompilerParams(vmem_limit_bytes=LARGE)
smem = pl.BlockSpec(memory_space=pltpu.SMEM)
vmem = pl.BlockSpec(memory_space=pltpu.VMEM)


def pack_weight(lat, weight):
    return pl.pallas_call(
        pack_kernel,
        in_specs=[smem, vmem],
        out_specs=vmem,
        out_shape=jax.ShapeDtypeStruct((NZ, 24, 384), jnp.bfloat16),
        compiler_params=params,
        name="pack_weight",
    )(lat, weight)


def open_table(table, open_up):
    return pl.pallas_call(
        open_kernel,
        in_specs=[vmem, vmem],
        out_specs=vmem,
        out_shape=jax.ShapeDtypeStruct((GROUPS, 4 * ROWS, WIDE), jnp.float32),
        scratch_shapes=[pltpu.VMEM((3, ROWS * HEADS, 128), jnp.float32)],
        compiler_params=params,
        name="open_table",
    )(table, open_up)


def window_probs(across, south, table, spread, mask):
    return pl.pallas_call(
        probs_kernel,
        grid=(STEPS,),
        in_specs=[
            north_spec(0, 2),
            south_spec(0, 2),
            group_spec(4 * ROWS, WIDE),
            whole_spec((WIDE, TOK)),
            whole_spec((TOK, TOK)),
        ],
        out_specs=group_spec(4 * TOK, TOK),
        out_shape=jax.ShapeDtypeStruct((GROUPS, 4 * TOK, TOK), jnp.bfloat16),
        compiler_params=large,
        name="window_probs",
    )(across, south, table, spread, mask)


def merge_product(spots, near, far, weight, shuffle):
    return pl.pallas_call(
        merge_kernel,
        in_specs=[smem, vmem, vmem, vmem, vmem],
        out_specs=vmem,
        out_shape=jax.ShapeDtypeStruct((8, 64, 512), jnp.bfloat16),
        scratch_shapes=[pltpu.VMEM((384, 512), jnp.float32)],
        compiler_params=params,
        name="merge_product",
    )(spots, near, far, weight, shuffle)


def score_grads(recv, order, quarter, gain, back, sums, across, south, probs):
    return pl.pallas_call(
        scores_kernel,
        grid=(1,),
        in_specs=[
            whole_spec((8, 64, 512)),
            whole_spec((512, 384)),
            pl.BlockSpec((1, 2, 2, PAD, 768), lambda g: (3, 0, 1, 0, 0)),
            pl.BlockSpec((1, 2, 2, PAD, 768), lambda g: (3, 0, 2, 0, 0)),
            pl.BlockSpec((1, 2, 4, PAD, 768), lambda g: (3, 0, 0, 0, 0)),
            whole_spec((256, 256)),
            whole_spec((4, 1, 768)),
            whole_spec((TOK, 256)),
            whole_spec((TOK, WIDE)),
            pl.BlockSpec((1, 2, 3, PAD, 768), lambda g: (2, 0, 1, 0, 0)),
            pl.BlockSpec((1, 2, 4, PAD, 768), lambda g: (2, 0, 0, 0, 0)),
            whole_spec((GROUPS, 4 * TOK, TOK)),
        ],
        out_specs=(
            whole_spec((GROUPS, TOK, 128)),
            whole_spec((16, 8 * SHARE, 128)),
        ),
        out_shape=(
            jax.ShapeDtypeStruct((GROUPS, TOK, 128), jnp.bfloat16),
            jax.ShapeDtypeStruct((16, 8 * SHARE, 128), jnp.bfloat16),
        ),
        compiler_params=large,
        name="score_grads",
    )(recv, order, across, across, south, quarter, gain, back, sums, across, south, probs)


def close_table(parts, close):
    return pl.pallas_call(
        close_kernel,
        in_specs=[vmem, vmem],
        out_specs=vmem,
        out_shape=jax.ShapeDtypeStruct((1, HEADS, 3312), jnp.float32),
        scratch_shapes=[pltpu.VMEM((3, ROWS * HEADS, 128), jnp.float32)],
        compiler_params=params,
        name="close_table",
    )(parts, close)


def window_grads(across, south, o_win, probs):
    return pl.pallas_call(
        grads_kernel,
        grid=(STEPS,),
        in_specs=[
            north_spec(0, 3),
            south_spec(0, 3),
            group_spec(TOK, 128),
            group_spec(4 * TOK, TOK),
        ],
        out_specs=pl.BlockSpec((3, TOK, PER * 128), lambda g: (0, 0, g)),
        out_shape=jax.ShapeDtypeStruct((3, TOK, 768), jnp.bfloat16),
        compiler_params=large,
        name="window_grads",
    )(across, south, o_win, probs)


def from_behind(shard, axis, by):
    size = lax.axis_size(axis)
    return lax.ppermute(shard, axis, [(i, (i + by) % size) for i in range(size)])


def partner(shard, axis, bit):
    return lax.ppermute(shard, axis, [(i, i ^ bit) for i in range(lax.axis_size(axis))])


def swap(shard, axis, groups):
    return lax.all_to_all(shard, axis, 0, 0, tiled=True, axis_index_groups=groups)


def share(shard, count, axis, groups):
    return swap(jnp.broadcast_to(shard[None], (count,) + shard.shape), axis, groups)


def on_device(y_block, merge_gain, merge_weight, d_merged, q_proj, k_proj, v_proj, bias_table):
    sums, spread, quarter, back, order, shuffle, open_up, close = layout_constants()
    lat = lax.axis_index("lat")

    packed = pack_weight(lat.reshape(1), merge_weight)

    tokens = jnp.arange(TOK, dtype=jnp.int32)
    upper = tokens // PAD % 6 >= 3
    allowed = jnp.logical_or(upper[:, None] == upper[None, :], lat != LAT - 1)
    allowed = jnp.logical_and(allowed, (tokens % PAD < 12)[None, :])
    mask = jnp.where(allowed, 0.0, LOW)

    packed, d_merged = lax.optimization_barrier((packed, d_merged))
    weight_z = swap(packed, "lon", z_groups).reshape(NZ * 24, 384)
    eastern_d = from_behind(d_merged[:, :, :3], "lon", -1)
    d_rows = jnp.concatenate(
        [d_merged[:, :, 3:], eastern_d, jnp.zeros_like(d_merged[:, :, :2])], axis=2
    ).reshape(48, -1)
    d_rows = jnp.concatenate([d_rows, partner(d_rows, "lat", 2)], axis=0)
    near = jnp.concatenate([d_rows, partner(d_rows, "lon", NY * NZ)], axis=0)
    far = partner(near, "lat", 1)
    me = (lax.axis_index("lon") // (NY * NZ)) * LAT + lat
    rel = jnp.bitwise_xor(jnp.arange(8, dtype=jnp.int32), me)
    spots = (rel % 2 * 4 + rel // 4 * 2 + rel // 2 % 2) * 48

    weight = share(weight_z, NY, "lon", y_groups)
    table = open_table(bias_table, open_up)

    eastern = from_behind(
        jnp.stack([q_proj[:, :, :6], k_proj[:, :, :6], v_proj[:, :, :6], y_block[:, :, :6]]),
        "lon",
        -1,
    )
    across = jnp.concatenate(
        [
            jnp.stack([q_proj[:, :, 6:], k_proj[:, :, 6:], v_proj[:, :, 6:], y_block[:, :, 6:]]),
            eastern,
            jnp.zeros_like(eastern[:, :, :, :4]),
        ],
        axis=3,
    )
    south = from_behind(across[:, :, :4], "lat", -1)

    weight, table, mask = lax.optimization_barrier((weight, table, mask))
    parts = merge_product(spots, near, far, weight, shuffle)
    recv = swap(parts, ("lon", "lat"), x_lat_groups)

    south, _ = lax.optimization_barrier((south, parts))
    probs = window_probs(across, south, table, spread, mask)

    gain = merge_gain.reshape(4, 1, 768)
    o_win, table_part = score_grads(
        recv, order, quarter, gain, back, sums, across, south, probs
    )

    table_part = swap(table_part, "lon", near_groups).astype(jnp.float32)
    table_part = jnp.sum(table_part, axis=0).astype(jnp.bfloat16)
    grads = window_grads(across, south, o_win, probs)
    grid = grads.reshape(3, 2, 6, PAD, 768)[:, :, :, :12]
    western = from_behind(grid[:, :, :, 6:], "lon", 1)
    fixed = jnp.concatenate([western, grid[:, :, :, :6]], axis=3)

    table_part = share(table_part, NZ // 2, "lon", far_groups)
    table_part, fixed = lax.optimization_barrier((table_part, fixed))
    southern = from_behind(fixed[:, :, 3:], "lat", 1)
    table_part = jnp.sum(table_part.astype(jnp.float32), axis=0).astype(jnp.bfloat16)
    finished = jnp.concatenate([southern, fixed[:, :, :3]], axis=2)
    table_grad = close_table(share(table_part, 16, "lon", near_groups), close)
    return (finished[0], finished[1], finished[2], table_grad)


def solution(mesh):
    placed = (
        P(None, "lat", "lon", None),
        P(),
        P("lon", None),
        P(None, "lat", "lon", None),
        P(None, "lat", "lon", None),
        P(None, "lat", "lon", None),
        P(None, "lat", "lon", None),
        P("lat", None, None),
    )
    return jax.shard_map(
        on_device,
        mesh=mesh,
        in_specs=placed,
        out_specs=(
            P(None, "lat", "lon", None),
            P(None, "lat", "lon", None),
            P(None, "lat", "lon", None),
            P("lat", None, None),
        ),
        check_vma=False,
    )
```

```python
import jax
import jax.numpy as jnp
import numpy as np
from jax import lax
from jax.experimental import pallas as pl
from jax.experimental.pallas import tpu as pltpu
from jax.sharding import PartitionSpec as P

NX, NY, NZ = 2, 4, 16
LAT = 4
HEADS = 24
ROWS = 12
PAD = 16
TOK = ROWS * PAD
SEG = 32
WIDE = ROWS * SEG
GROUPS = 6
PER = 3
STEPS = GROUPS // PER
SHARE = 7
LOW = -1e30
SMALL = 12 * 1024 * 1024
LARGE = 56 * 1024 * 1024
score_factor = 32 ** (-0.5)

z_groups = [[a * NZ + z for z in range(NZ)] for a in range(NX * NY)]
y_groups = [[(x * NY + y) * NZ + z for y in range(NY)] for x in range(NX) for z in range(NZ)]
near_groups = [
    [a * NZ + 2 * pair + e for a in range(NX * NY) for e in range(2)] for pair in range(NZ // 2)
]
far_groups = [
    [a * NZ + 2 * pair + e for pair in range(NZ // 2)] for a in range(NX * NY) for e in range(2)
]
x_lat_groups = [
    [(x * NY * NZ + b) * LAT + l for x in range(NX) for l in range(LAT)] for b in range(NY * NZ)
]


def layout_constants():
    tokens = np.arange(TOK)
    row, col = tokens // PAD, tokens % PAD
    real = col < 12
    sums = np.zeros((2, TOK, WIDE), np.float32)
    spread = np.zeros((2, WIDE, TOK), np.float32)
    for half in range(2):
        sums[half, tokens[real], (row * SEG + 11 - col + 8 * half)[real]] = 1
        spread[half, (row * SEG + 11 + col - 8 * half)[real], tokens[real]] = 1
    quarter = np.zeros((256, 256), np.float32)
    back = np.zeros((TOK, 256), np.float32)
    for level in range(2):
        for pr in range(4):
            for pc in range(6):
                for di in range(2):
                    for dj in range(2):
                        spot = (di + 2 * dj) * 64 + (level * 4 + pr) * 8 + pc
                        fine_row, fine_col = 2 * pr + di, 2 * pc + dj
                        quarter[spot, (level * 8 + fine_row) * PAD + fine_col] = 1
                        if 1 <= fine_row <= 6:
                            back[(level * 6 + fine_row - 1) * PAD + fine_col, spot] = 1
    shuffle = np.zeros((512, 384), np.float32)
    order = np.zeros((512, 384), np.float32)
    for l in range(4):
        for z in range(NZ):
            for i in range(6):
                shuffle[l * 128 + z * 6 + i, z * 24 + l * 6 + i] = 1
                order[l * 128 + z * 6 + i, z * 24 + l * 6 + i] = 1
    open_up = np.zeros((2, 138, WIDE), np.float32)
    for half in range(2):
        for r in range(6):
            for d in range(23):
                open_up[half, r * 23 + d, half * 192 + r * SEG + 22 - d] = 1
    close = np.zeros((WIDE, 512), np.float32)
    for b in range(ROWS):
        for d in range(23):
            close[b * SEG + d, b // 6 * 256 + b % 6 * 23 + d] = 1
    all_of = (sums, spread, quarter, back, order, shuffle, open_up, close)
    return [jnp.asarray(a, jnp.bfloat16) for a in all_of]


def dot(a, b, dims=((1,), (0,))):
    return lax.dot_general(a, b, (dims, ((), ())), preferred_element_type=jnp.float32)


def head_mask(h):
    lanes = lax.broadcasted_iota(jnp.int32, (1, 128), 1)
    return (lanes // 32) == h


def by_head(block):
    return jnp.concatenate(
        [jnp.where(head_mask(h), block, jnp.zeros_like(block)) for h in range(4)], axis=0
    )


def split_dot(values, matrix):
    high = values.astype(jnp.bfloat16)
    low = (values - high.astype(jnp.float32)).astype(jnp.bfloat16)
    return dot(high, matrix) + dot(low, matrix)


def window(north_ref, south_ref, which, group):
    lanes = slice(group * 128, (group + 1) * 128)
    pieces = []
    for level in range(2):
        pieces.append(north_ref[which, level, :, :, lanes].reshape(48, 128))
        pieces.append(south_ref[which, level, 0:3, :, lanes].reshape(48, 128))
    return jnp.concatenate(pieces, axis=0)


def pack_kernel(lat_ref, w_ref, out_ref):
    first = lat_ref[0] * 6
    to = lax.broadcasted_iota(jnp.int32, (24, 24), 0)
    source = lax.broadcasted_iota(jnp.int32, (24, 24), 1)
    total = jnp.zeros((24, 384), jnp.float32)
    for part in range(4):
        pick = jnp.logical_and(to // 6 == part, source == first + to - part * 6)
        pick = jnp.where(pick, 1.0, 0.0).astype(jnp.bfloat16)
        total += dot(pick, w_ref[:, part * 384 : (part + 1) * 384])
    packed = total.astype(jnp.bfloat16)
    for z in range(NZ):
        out_ref[z] = packed


def open_kernel(table_ref, open_ref, out_ref, wide_ref):
    halves = []
    for half in range(2):
        pieces = []
        for a in range(ROWS):
            first = (a // 6 * 2 + half) * 828 + a % 6 * 138
            pieces.append(table_ref[0, :, first : first + 138])
        halves.append(split_dot(jnp.concatenate(pieces, axis=0), open_ref[half]))
    whole = halves[0] + halves[1]
    for s in range(3):
        wide_ref[s] = whole[:, s * 128 : (s + 1) * 128]
    for head in range(HEADS):
        row = head % 4 * ROWS
        for s in range(3):
            out_ref[head // 4, row : row + ROWS, s * 128 : (s + 1) * 128] = wide_ref[
                s, pl.ds(head, ROWS, stride=HEADS), :
            ]


def probs_kernel(north_ref, south_ref, table_ref, spread_ref, mask_ref, p_ref):
    for group in range(PER):
        pieces = []
        for s in range(3):
            table = table_ref[group, :, s * 128 : (s + 1) * 128]
            table = jnp.broadcast_to(table[:, None, :], (4 * ROWS, 8, 128))
            pieces.append(pltpu.roll(table, 0, 2, stride=1, stride_axis=1))
        wide = jnp.concatenate(pieces, axis=2).reshape(2 * TOK, WIDE)
        q_win = window(north_ref, south_ref, 0, group)
        k_win = window(north_ref, south_ref, 1, group)
        scores = dot(by_head(q_win), k_win, ((1,), (1,))) * score_factor
        bias = [split_dot(wide, spread_ref[half]).reshape(-1, 1, 8, TOK) for half in range(2)]
        scores = scores + jnp.concatenate(bias, axis=1).reshape(4 * TOK, TOK)
        scores = (scores.reshape(4, TOK, TOK) + mask_ref[...][None]).reshape(4 * TOK, TOK)
        expon = jnp.exp(scores - jnp.max(scores, axis=-1, keepdims=True))
        probs = expon * (1.0 / jnp.sum(expon, axis=-1, keepdims=True))
        p_ref[group] = probs.astype(jnp.bfloat16)


def normalise(a_ref, b_ref, south_ref, quarter_ref):
    pieces = []
    for level in range(2):
        pieces.append(a_ref[0, level].reshape(32, 768))
        pieces.append(b_ref[0, level].reshape(32, 768))
        pieces.append(south_ref[0, level].reshape(64, 768))
    fields = dot(quarter_ref[...], jnp.concatenate(pieces, axis=0))
    parts = [fields[q * 64 : (q + 1) * 64] for q in range(4)]
    mean = jnp.sum(parts[0] + parts[1] + parts[2] + parts[3], axis=-1, keepdims=True) / 3072
    parts = [part - mean for part in parts]
    squares = [part * part for part in parts]
    variance = (
        jnp.sum(squares[0] + squares[1] + squares[2] + squares[3], axis=-1, keepdims=True) / 3072
    )
    inverse = lax.rsqrt(variance + 1e-05)
    return [part * inverse for part in parts], inverse


def merge_kernel(spot_ref, near_ref, far_ref, w_ref, shuffle_ref, out_ref, acc_ref):
    weights = [dot(shuffle_ref[...], w_ref[y]).astype(jnp.bfloat16) for y in range(NY)]
    near, far = None, None
    for part in range(4):
        rows, columns = slice(part * 128, part * 128 + 128), slice(part * 384, part * 384 + 384)
        weight = jnp.concatenate([weights[y][rows] for y in range(NY)], axis=0)
        near_part = dot(near_ref[:, columns], weight, ((1,), (1,)))
        far_part = dot(far_ref[:, columns], weight, ((1,), (1,)))
        near = near_part if part == 0 else near + near_part
        far = far_part if part == 0 else far + far_part
    acc_ref[:192] = near
    acc_ref[192:] = far
    for x in range(NX):
        for l in range(LAT):
            for level in range(2):
                own = pl.multiple_of(spot_ref[x * LAT + l] + level * 24 + 8, 8)
                below = pl.multiple_of(spot_ref[x * LAT + (l + 1) % LAT] + level * 24, 8)
                out_ref[x * LAT + l, level * 32 : level * 32 + 16] = acc_ref[
                    pl.ds(own, 16)
                ].astype(jnp.bfloat16)
                out_ref[x * LAT + l, level * 32 + 16 : level * 32 + 32] = acc_ref[
                    pl.ds(below, 16)
                ].astype(jnp.bfloat16)


def score_grad(probs, o_win, v_win):
    d_probs = dot(by_head(o_win), v_win, ((1,), (1,)))
    probs = probs.astype(jnp.float32)
    delta = jnp.sum(probs * d_probs, axis=-1, keepdims=True)
    return probs * (d_probs - delta)


def scores_kernel(
    recv_ref,
    order_ref,
    y_a_ref,
    y_b_ref,
    y_south_ref,
    quarter_ref,
    gain_ref,
    back_ref,
    sums_ref,
    north_ref,
    south_ref,
    p_ref,
    o_out_ref,
    table_ref,
    p_buf,
    p_sem,
):
    copy = pltpu.make_async_copy(p_ref, p_buf, p_sem)
    copy.start()
    pieces = [
        jnp.concatenate(
            [recv_ref[x * LAT + l, :, y * 128 : (y + 1) * 128] for l in range(LAT)], axis=1
        )
        for x in range(NX)
        for y in range(NY)
    ]
    d_norm = dot(jnp.concatenate(pieces, axis=0), order_ref[...])
    hats = []
    for q in range(4):
        left = d_norm[(2 * q) * 64 : (2 * q + 1) * 64]
        right = d_norm[(2 * q + 1) * 64 : (2 * q + 2) * 64]
        hats.append(jnp.concatenate([left, right], axis=1) * gain_ref[q])
    mean = jnp.sum(hats[0] + hats[1] + hats[2] + hats[3], axis=-1, keepdims=True) / 3072
    normed, inverse = normalise(y_a_ref, y_b_ref, y_south_ref, quarter_ref)
    cross = [hats[q] * normed[q] for q in range(4)]
    along = jnp.sum(cross[0] + cross[1] + cross[2] + cross[3], axis=-1, keepdims=True) / 3072
    stack = [(hats[q] - mean - normed[q] * along) * inverse for q in range(4)]
    d_out = dot(back_ref[...], jnp.concatenate(stack, axis=0).astype(jnp.bfloat16))
    d_out = d_out.astype(jnp.bfloat16)

    copy.wait()
    sums = [[], [], []]
    for group in range(GROUPS):
        o_win = d_out[:, group * 128 : (group + 1) * 128]
        o_out_ref[group] = o_win
        d_scores = score_grad(p_buf[group], o_win, window(north_ref, south_ref, 0, group))
        halves = d_scores.reshape(4 * ROWS, 2, 8, TOK)
        spread = sum(
            dot(halves[:, half].reshape(2 * TOK, TOK).astype(jnp.bfloat16), sums_ref[half])
            for half in range(2)
        ).reshape(4 * ROWS, 8, WIDE)
        for s in range(3):
            part = spread[:, :, s * 128 : (s + 1) * 128]
            turned = pltpu.roll(part, 0, 2, stride=1, stride_axis=1)
            sums[s].append(jnp.sum(turned, axis=1))

    tiles = []
    for s in range(3):
        whole = jnp.concatenate(sums[s], axis=0)
        tiles += [whole[r * 8 : (r + 1) * 8] for r in range(36)]
    tiles += [jnp.zeros((8, 128), jnp.float32)] * (16 * SHARE - len(tiles))
    for part in range(16):
        chunk = jnp.concatenate(tiles[part * SHARE : (part + 1) * SHARE], axis=0)
        table_ref[part] = chunk.astype(jnp.bfloat16)


def close_kernel(parts_ref, close_ref, out_ref, wide_ref):
    for part in range(16):
        chunk = parts_ref[part].astype(jnp.float32)
        for k in range(SHARE):
            s, r = divmod(part * SHARE + k, 36)
            if s < 3:
                wide_ref[s, r * 8 : (r + 1) * 8] = chunk[k * 8 : (k + 1) * 8]
    rows = []
    for a in range(ROWS):
        lanes = [wide_ref[s, pl.ds(a, HEADS, stride=ROWS), :] for s in range(3)]
        rows.append(jnp.concatenate(lanes, axis=1))
    dense = dot(jnp.concatenate(rows, axis=0).astype(jnp.bfloat16), close_ref[...])
    for a in range(ROWS):
        for half in range(2):
            first = (a // 6 * 2 + half) * 828 + a % 6 * 138
            out_ref[0, :, first : first + 138] = dense[
                a * HEADS : (a + 1) * HEADS, half * 256 : half * 256 + 138
            ]


def grads_kernel(north_ref, south_ref, o_ref, p_ref, grads_ref):
    for group in range(PER):
        lanes = slice(group * 128, (group + 1) * 128)
        q_win = window(north_ref, south_ref, 0, group)
        k_win = window(north_ref, south_ref, 1, group)
        o_win, p_low = o_ref[group], p_ref[group]
        d_low = score_grad(p_low, o_win, window(north_ref, south_ref, 2, group))
        d_low = d_low.astype(jnp.bfloat16)
        q_all = dot(d_low, k_win)
        q_grad = jnp.zeros((TOK, 128), jnp.float32)
        for h in range(4):
            q_grad = jnp.where(head_mask(h), q_all[h * TOK : (h + 1) * TOK], q_grad)
        grads_ref[0, :, lanes] = (q_grad * score_factor).astype(jnp.bfloat16)

        q_turn = q_win.astype(jnp.float32).T.astype(jnp.bfloat16)
        o_turn = o_win.astype(jnp.float32).T.astype(jnp.bfloat16)
        k_parts, v_parts = [], []
        for h in range(4):
            rows = slice(h * 32, (h + 1) * 32)
            k_parts.append(dot(q_turn[rows], d_low[h * TOK : (h + 1) * TOK]))
            v_parts.append(dot(o_turn[rows], p_low[h * TOK : (h + 1) * TOK]))
        k_grad = jnp.concatenate(k_parts, axis=0).T
        v_grad = jnp.concatenate(v_parts, axis=0).T
        grads_ref[1, :, lanes] = (k_grad * score_factor).astype(jnp.bfloat16)
        grads_ref[2, :, lanes] = v_grad.astype(jnp.bfloat16)


def whole_spec(shape):
    return pl.BlockSpec(shape, lambda *_: (0,) * len(shape))


def north_spec(first, count):
    return pl.BlockSpec((count, 2, 3, PAD, PER * 128), lambda g: (first // count, 0, 1, 0, g))


def south_spec(first, count):
    return pl.BlockSpec((count, 2, 4, PAD, PER * 128), lambda g: (first // count, 0, 0, 0, g))


def group_spec(rows, columns):
    return pl.BlockSpec((PER, rows, columns), lambda g: (g, 0, 0))


params = pltpu.CompilerParams(vmem_limit_bytes=SMALL)
large = pltpu.CompilerParams(vmem_limit_bytes=LARGE)
smem = pl.BlockSpec(memory_space=pltpu.SMEM)
vmem = pl.BlockSpec(memory_space=pltpu.VMEM)


def pack_weight(lat, weight):
    return pl.pallas_call(
        pack_kernel,
        in_specs=[smem, vmem],
        out_specs=vmem,
        out_shape=jax.ShapeDtypeStruct((NZ, 24, 384), jnp.bfloat16),
        compiler_params=params,
        name="pack_weight",
    )(lat, weight)


def open_table(table, open_up):
    return pl.pallas_call(
        open_kernel,
        in_specs=[vmem, vmem],
        out_specs=vmem,
        out_shape=jax.ShapeDtypeStruct((GROUPS, 4 * ROWS, WIDE), jnp.float32),
        scratch_shapes=[pltpu.VMEM((3, ROWS * HEADS, 128), jnp.float32)],
        compiler_params=params,
        name="open_table",
    )(table, open_up)


def window_probs(across, south, table, spread, mask):
    return pl.pallas_call(
        probs_kernel,
        grid=(STEPS,),
        in_specs=[
            north_spec(0, 2),
            south_spec(0, 2),
            group_spec(4 * ROWS, WIDE),
            whole_spec((2, WIDE, TOK)),
            whole_spec((TOK, TOK)),
        ],
        out_specs=group_spec(4 * TOK, TOK),
        out_shape=jax.ShapeDtypeStruct((GROUPS, 4 * TOK, TOK), jnp.bfloat16),
        compiler_params=large,
        name="window_probs",
    )(across, south, table, spread, mask)


def merge_product(spots, near, far, weight, shuffle):
    return pl.pallas_call(
        merge_kernel,
        in_specs=[smem, vmem, vmem, vmem, vmem],
        out_specs=vmem,
        out_shape=jax.ShapeDtypeStruct((8, 64, 512), jnp.bfloat16),
        scratch_shapes=[pltpu.VMEM((384, 512), jnp.float32)],
        compiler_params=params,
        name="merge_product",
    )(spots, near, far, weight, shuffle)


def score_grads(recv, order, quarter, gain, back, sums, across, south, probs):
    return pl.pallas_call(
        scores_kernel,
        grid=(1,),
        in_specs=[
            whole_spec((8, 64, 512)),
            whole_spec((512, 384)),
            pl.BlockSpec((1, 2, 2, PAD, 768), lambda g: (3, 0, 1, 0, 0)),
            pl.BlockSpec((1, 2, 2, PAD, 768), lambda g: (3, 0, 2, 0, 0)),
            pl.BlockSpec((1, 2, 4, PAD, 768), lambda g: (3, 0, 0, 0, 0)),
            whole_spec((256, 256)),
            whole_spec((4, 1, 768)),
            whole_spec((TOK, 256)),
            whole_spec((2, TOK, WIDE)),
            pl.BlockSpec((1, 2, 3, PAD, 768), lambda g: (2, 0, 1, 0, 0)),
            pl.BlockSpec((1, 2, 4, PAD, 768), lambda g: (2, 0, 0, 0, 0)),
            pl.BlockSpec(memory_space=pl.ANY),
        ],
        out_specs=(
            whole_spec((GROUPS, TOK, 128)),
            whole_spec((16, 8 * SHARE, 128)),
        ),
        out_shape=(
            jax.ShapeDtypeStruct((GROUPS, TOK, 128), jnp.bfloat16),
            jax.ShapeDtypeStruct((16, 8 * SHARE, 128), jnp.bfloat16),
        ),
        scratch_shapes=[
            pltpu.VMEM((GROUPS, 4 * TOK, TOK), jnp.bfloat16),
            pltpu.SemaphoreType.DMA,
        ],
        compiler_params=large,
        name="score_grads",
    )(recv, order, across, across, south, quarter, gain, back, sums, across, south, probs)


def close_table(parts, close):
    return pl.pallas_call(
        close_kernel,
        in_specs=[vmem, vmem],
        out_specs=vmem,
        out_shape=jax.ShapeDtypeStruct((1, HEADS, 3312), jnp.float32),
        scratch_shapes=[pltpu.VMEM((3, ROWS * HEADS, 128), jnp.float32)],
        compiler_params=params,
        name="close_table",
    )(parts, close)


def window_grads(across, south, o_win, probs):
    return pl.pallas_call(
        grads_kernel,
        grid=(STEPS,),
        in_specs=[
            north_spec(0, 3),
            south_spec(0, 3),
            group_spec(TOK, 128),
            group_spec(4 * TOK, TOK),
        ],
        out_specs=pl.BlockSpec((3, TOK, PER * 128), lambda g: (0, 0, g)),
        out_shape=jax.ShapeDtypeStruct((3, TOK, 768), jnp.bfloat16),
        compiler_params=large,
        name="window_grads",
    )(across, south, o_win, probs)


def from_behind(shard, axis, by):
    size = lax.axis_size(axis)
    return lax.ppermute(shard, axis, [(i, (i + by) % size) for i in range(size)])


def partner(shard, axis, bit):
    return lax.ppermute(shard, axis, [(i, i ^ bit) for i in range(lax.axis_size(axis))])


def swap(shard, axis, groups):
    return lax.all_to_all(shard, axis, 0, 0, tiled=True, axis_index_groups=groups)


def share(shard, count, axis, groups):
    return swap(jnp.broadcast_to(shard[None], (count,) + shard.shape), axis, groups)


def on_device(y_block, merge_gain, merge_weight, d_merged, q_proj, k_proj, v_proj, bias_table):
    sums, spread, quarter, back, order, shuffle, open_up, close = layout_constants()
    lat = lax.axis_index("lat")

    packed = pack_weight(lat.reshape(1), merge_weight)

    tokens = jnp.arange(TOK, dtype=jnp.int32)
    upper = tokens // PAD % 6 >= 3
    allowed = jnp.logical_or(upper[:, None] == upper[None, :], lat != LAT - 1)
    allowed = jnp.logical_and(allowed, (tokens % PAD < 12)[None, :])
    mask = jnp.where(allowed, 0.0, LOW)

    packed, d_merged = lax.optimization_barrier((packed, d_merged))
    weight_z = swap(packed, "lon", z_groups).reshape(NZ * 24, 384)
    eastern_d = from_behind(d_merged[:, :, :3], "lon", -1)
    d_rows = jnp.concatenate(
        [d_merged[:, :, 3:], eastern_d, jnp.zeros_like(d_merged[:, :, :2])], axis=2
    ).reshape(48, -1)
    d_rows = jnp.concatenate([d_rows, partner(d_rows, "lat", 2)], axis=0)
    near = jnp.concatenate([d_rows, partner(d_rows, "lon", NY * NZ)], axis=0)
    far = partner(near, "lat", 1)
    me = (lax.axis_index("lon") // (NY * NZ)) * LAT + lat
    rel = jnp.bitwise_xor(jnp.arange(8, dtype=jnp.int32), me)
    spots = (rel % 2 * 4 + rel // 4 * 2 + rel // 2 % 2) * 48

    weight = share(weight_z, NY, "lon", y_groups)
    table = open_table(bias_table, open_up)

    eastern = from_behind(
        jnp.stack([q_proj[:, :, :6], k_proj[:, :, :6], v_proj[:, :, :6], y_block[:, :, :6]]),
        "lon",
        -1,
    )
    across = jnp.concatenate(
        [
            jnp.stack([q_proj[:, :, 6:], k_proj[:, :, 6:], v_proj[:, :, 6:], y_block[:, :, 6:]]),
            eastern,
            jnp.zeros_like(eastern[:, :, :, :4]),
        ],
        axis=3,
    )
    south = from_behind(across[:, :, :4], "lat", -1)

    weight, table, mask = lax.optimization_barrier((weight, table, mask))
    parts = merge_product(spots, near, far, weight, shuffle)
    recv = swap(parts, ("lon", "lat"), x_lat_groups)

    south, _ = lax.optimization_barrier((south, parts))
    probs = window_probs(across, south, table, spread, mask)

    gain = merge_gain.reshape(4, 1, 768)
    o_win, table_part = score_grads(
        recv, order, quarter, gain, back, sums, across, south, probs
    )

    table_part = swap(table_part, "lon", near_groups).astype(jnp.float32)
    table_part = jnp.sum(table_part, axis=0).astype(jnp.bfloat16)
    grads = window_grads(across, south, o_win, probs)
    grid = grads.reshape(3, 2, 6, PAD, 768)[:, :, :, :12]
    western = from_behind(grid[:, :, :, 6:], "lon", 1)
    fixed = jnp.concatenate([western, grid[:, :, :, :6]], axis=3)

    table_part = share(table_part, NZ // 2, "lon", far_groups)
    table_part, fixed = lax.optimization_barrier((table_part, fixed))
    southern = from_behind(fixed[:, :, 3:], "lat", 1)
    table_part = jnp.sum(table_part.astype(jnp.float32), axis=0).astype(jnp.bfloat16)
    finished = jnp.concatenate([southern, fixed[:, :, :3]], axis=2)
    table_grad = close_table(share(table_part, 16, "lon", near_groups), close)
    return (finished[0], finished[1], finished[2], table_grad)


def solution(mesh):
    placed = (
        P(None, "lat", "lon", None),
        P(),
        P("lon", None),
        P(None, "lat", "lon", None),
        P(None, "lat", "lon", None),
        P(None, "lat", "lon", None),
        P(None, "lat", "lon", None),
        P("lat", None, None),
    )
    return jax.shard_map(
        on_device,
        mesh=mesh,
        in_specs=placed,
        out_specs=(
            P(None, "lat", "lon", None),
            P(None, "lat", "lon", None),
            P(None, "lat", "lon", None),
            P("lat", None, None),
        ),
        check_vma=False,
    )
```

```python
import jax
import jax.numpy as jnp
import numpy as np
from jax import lax
from jax.experimental import pallas as pl
from jax.experimental.pallas import tpu as pltpu
from jax.sharding import PartitionSpec as P

NX, NY, NZ = 2, 4, 16
LAT = 4
HEADS = 24
ROWS = 12
PAD = 16
TOK = ROWS * PAD
SEG = 32
WIDE = ROWS * SEG
GROUPS = 6
PER = 3
STEPS = GROUPS // PER
SHARE = 7
LOW = -1e30
SMALL = 12 * 1024 * 1024
LARGE = 56 * 1024 * 1024
score_factor = 32 ** (-0.5)

z_groups = [[a * NZ + z for z in range(NZ)] for a in range(NX * NY)]
y_groups = [[(x * NY + y) * NZ + z for y in range(NY)] for x in range(NX) for z in range(NZ)]
near_groups = [
    [a * NZ + 2 * pair + e for a in range(NX * NY) for e in range(2)] for pair in range(NZ // 2)
]
far_groups = [
    [a * NZ + 2 * pair + e for pair in range(NZ // 2)] for a in range(NX * NY) for e in range(2)
]
x_lat_groups = [
    [(x * NY * NZ + b) * LAT + l for x in range(NX) for l in range(LAT)] for b in range(NY * NZ)
]


def layout_constants():
    tokens = np.arange(TOK)
    row, col = tokens // PAD, tokens % PAD
    real = col < 12
    sums = np.zeros((2, TOK, WIDE), np.float32)
    spread = np.zeros((2, WIDE, TOK), np.float32)
    for half in range(2):
        sums[half, tokens[real], (row * SEG + 11 - col + 8 * half)[real]] = 1
        spread[half, (row * SEG + 11 + col - 8 * half)[real], tokens[real]] = 1
    quarter = np.zeros((256, 256), np.float32)
    back = np.zeros((TOK, 256), np.float32)
    for level in range(2):
        for pr in range(4):
            for pc in range(6):
                for di in range(2):
                    for dj in range(2):
                        spot = (di + 2 * dj) * 64 + (level * 4 + pr) * 8 + pc
                        fine_row, fine_col = 2 * pr + di, 2 * pc + dj
                        quarter[spot, (level * 8 + fine_row) * PAD + fine_col] = 1
                        if 1 <= fine_row <= 6:
                            back[(level * 6 + fine_row - 1) * PAD + fine_col, spot] = 1
    shuffle = np.zeros((512, 384), np.float32)
    order = np.zeros((512, 384), np.float32)
    for l in range(4):
        for z in range(NZ):
            for i in range(6):
                shuffle[l * 128 + z * 6 + i, z * 24 + l * 6 + i] = 1
                order[l * 128 + z * 6 + i, z * 24 + l * 6 + i] = 1
    open_up = np.zeros((2, 138, WIDE), np.float32)
    for half in range(2):
        for r in range(6):
            for d in range(23):
                open_up[half, r * 23 + d, half * 192 + r * SEG + 22 - d] = 1
    close = np.zeros((WIDE, 512), np.float32)
    for b in range(ROWS):
        for d in range(23):
            close[b * SEG + d, b // 6 * 256 + b % 6 * 23 + d] = 1
    all_of = (sums, spread, quarter, back, order, shuffle, open_up, close)
    return [jnp.asarray(a, jnp.bfloat16) for a in all_of]


def dot(a, b, dims=((1,), (0,))):
    return lax.dot_general(a, b, (dims, ((), ())), preferred_element_type=jnp.float32)


def head_mask(h):
    lanes = lax.broadcasted_iota(jnp.int32, (1, 128), 1)
    return (lanes // 32) == h


def by_head(block):
    return jnp.concatenate(
        [jnp.where(head_mask(h), block, jnp.zeros_like(block)) for h in range(4)], axis=0
    )


def split_dot(values, matrix):
    high = values.astype(jnp.bfloat16)
    low = (values - high.astype(jnp.float32)).astype(jnp.bfloat16)
    return dot(high, matrix) + dot(low, matrix)


def window(north_ref, south_ref, which, group):
    lanes = slice(group * 128, (group + 1) * 128)
    pieces = []
    for level in range(2):
        pieces.append(north_ref[which, level, :, :, lanes].reshape(48, 128))
        pieces.append(south_ref[which, level, 0:3, :, lanes].reshape(48, 128))
    return jnp.concatenate(pieces, axis=0)


def pack_kernel(lat_ref, w_ref, out_ref):
    first = lat_ref[0] * 6
    to = lax.broadcasted_iota(jnp.int32, (24, 24), 0)
    source = lax.broadcasted_iota(jnp.int32, (24, 24), 1)
    total = jnp.zeros((24, 384), jnp.float32)
    for part in range(4):
        pick = jnp.logical_and(to // 6 == part, source == first + to - part * 6)
        pick = jnp.where(pick, 1.0, 0.0).astype(jnp.bfloat16)
        total += dot(pick, w_ref[:, part * 384 : (part + 1) * 384])
    packed = total.astype(jnp.bfloat16)
    for z in range(NZ):
        out_ref[z] = packed


def open_kernel(table_ref, open_ref, out_ref, wide_ref):
    halves = []
    for half in range(2):
        pieces = []
        for a in range(ROWS):
            first = (a // 6 * 2 + half) * 828 + a % 6 * 138
            pieces.append(table_ref[0, :, first : first + 138])
        halves.append(split_dot(jnp.concatenate(pieces, axis=0), open_ref[half]))
    whole = halves[0] + halves[1]
    for s in range(3):
        wide_ref[s] = whole[:, s * 128 : (s + 1) * 128]
    for head in range(HEADS):
        row = head % 4 * ROWS
        for s in range(3):
            out_ref[head // 4, row : row + ROWS, s * 128 : (s + 1) * 128] = wide_ref[
                s, pl.ds(head, ROWS, stride=HEADS), :
            ]


def probs_kernel(north_ref, south_ref, table_ref, spread_ref, mask_ref, p_ref):
    for group in range(PER):
        pieces = []
        for s in range(3):
            table = table_ref[group, :, s * 128 : (s + 1) * 128]
            table = jnp.broadcast_to(table[:, None, :], (4 * ROWS, 8, 128))
            pieces.append(pltpu.roll(table, 0, 2, stride=1, stride_axis=1))
        wide = jnp.concatenate(pieces, axis=2).reshape(2 * TOK, WIDE)
        q_win = window(north_ref, south_ref, 0, group)
        k_win = window(north_ref, south_ref, 1, group)
        scores = dot(by_head(q_win), k_win, ((1,), (1,))) * score_factor
        bias = [split_dot(wide, spread_ref[half]).reshape(-1, 1, 8, TOK) for half in range(2)]
        scores = scores + jnp.concatenate(bias, axis=1).reshape(4 * TOK, TOK)
        scores = (scores.reshape(4, TOK, TOK) + mask_ref[...][None]).reshape(4 * TOK, TOK)
        expon = jnp.exp(scores - jnp.max(scores, axis=-1, keepdims=True))
        probs = expon * (1.0 / jnp.sum(expon, axis=-1, keepdims=True))
        p_ref[group] = probs.astype(jnp.bfloat16)


def normalise(a_ref, b_ref, south_ref, quarter_ref):
    pieces = []
    for level in range(2):
        pieces.append(a_ref[0, level].reshape(32, 768))
        pieces.append(b_ref[0, level].reshape(32, 768))
        pieces.append(south_ref[0, level].reshape(64, 768))
    fields = dot(quarter_ref[...], jnp.concatenate(pieces, axis=0))
    parts = [fields[q * 64 : (q + 1) * 64] for q in range(4)]
    mean = jnp.sum(parts[0] + parts[1] + parts[2] + parts[3], axis=-1, keepdims=True) / 3072
    parts = [part - mean for part in parts]
    squares = [part * part for part in parts]
    variance = (
        jnp.sum(squares[0] + squares[1] + squares[2] + squares[3], axis=-1, keepdims=True) / 3072
    )
    inverse = lax.rsqrt(variance + 1e-05)
    return [part * inverse for part in parts], inverse


def merge_kernel(spot_ref, near_ref, far_ref, w_ref, shuffle_ref, out_ref, acc_ref):
    weights = [dot(shuffle_ref[...], w_ref[y]).astype(jnp.bfloat16) for y in range(NY)]
    near, far = None, None
    for part in range(4):
        rows, columns = slice(part * 128, part * 128 + 128), slice(part * 384, part * 384 + 384)
        weight = jnp.concatenate([weights[y][rows] for y in range(NY)], axis=0)
        near_part = dot(near_ref[:, columns], weight, ((1,), (1,)))
        far_part = dot(far_ref[:, columns], weight, ((1,), (1,)))
        near = near_part if part == 0 else near + near_part
        far = far_part if part == 0 else far + far_part
    acc_ref[:192] = near
    acc_ref[192:] = far
    for x in range(NX):
        for l in range(LAT):
            for level in range(2):
                own = pl.multiple_of(spot_ref[x * LAT + l] + level * 24 + 8, 8)
                below = pl.multiple_of(spot_ref[x * LAT + (l + 1) % LAT] + level * 24, 8)
                out_ref[x * LAT + l, level * 32 : level * 32 + 16] = acc_ref[
                    pl.ds(own, 16)
                ].astype(jnp.bfloat16)
                out_ref[x * LAT + l, level * 32 + 16 : level * 32 + 32] = acc_ref[
                    pl.ds(below, 16)
                ].astype(jnp.bfloat16)


def score_grad(probs, o_win, v_win):
    d_probs = dot(by_head(o_win), v_win, ((1,), (1,)))
    probs = probs.astype(jnp.float32)
    delta = jnp.sum(probs * d_probs, axis=-1, keepdims=True)
    return probs * (d_probs - delta)


def scores_kernel(
    recv_ref,
    order_ref,
    y_a_ref,
    y_b_ref,
    y_south_ref,
    quarter_ref,
    gain_ref,
    back_ref,
    sums_ref,
    north_ref,
    south_ref,
    p_ref,
    o_out_ref,
    table_ref,
    p_buf,
    p_sem,
):
    copy = pltpu.make_async_copy(p_ref, p_buf, p_sem)
    copy.start()
    pieces = [
        jnp.concatenate(
            [recv_ref[x * LAT + l, :, y * 128 : (y + 1) * 128] for l in range(LAT)], axis=1
        )
        for x in range(NX)
        for y in range(NY)
    ]
    d_norm = dot(jnp.concatenate(pieces, axis=0), order_ref[...])
    hats = []
    for q in range(4):
        left = d_norm[(2 * q) * 64 : (2 * q + 1) * 64]
        right = d_norm[(2 * q + 1) * 64 : (2 * q + 2) * 64]
        hats.append(jnp.concatenate([left, right], axis=1) * gain_ref[q])
    mean = jnp.sum(hats[0] + hats[1] + hats[2] + hats[3], axis=-1, keepdims=True) / 3072
    normed, inverse = normalise(y_a_ref, y_b_ref, y_south_ref, quarter_ref)
    cross = [hats[q] * normed[q] for q in range(4)]
    along = jnp.sum(cross[0] + cross[1] + cross[2] + cross[3], axis=-1, keepdims=True) / 3072
    stack = [(hats[q] - mean - normed[q] * along) * inverse for q in range(4)]
    d_out = dot(back_ref[...], jnp.concatenate(stack, axis=0).astype(jnp.bfloat16))
    d_out = d_out.astype(jnp.bfloat16)

    copy.wait()
    sums = [[], [], []]
    for group in range(GROUPS):
        o_win = d_out[:, group * 128 : (group + 1) * 128]
        o_out_ref[group] = o_win
        d_scores = score_grad(p_buf[group], o_win, window(north_ref, south_ref, 0, group))
        halves = d_scores.reshape(4 * ROWS, 2, 8, TOK)
        spread = sum(
            dot(halves[:, half].reshape(2 * TOK, TOK).astype(jnp.bfloat16), sums_ref[half])
            for half in range(2)
        ).reshape(4 * ROWS, 8, WIDE)
        for s in range(3):
            part = spread[:, :, s * 128 : (s + 1) * 128]
            turned = pltpu.roll(part, 0, 2, stride=1, stride_axis=1)
            sums[s].append(jnp.sum(turned, axis=1))

    tiles = []
    for s in range(3):
        whole = jnp.concatenate(sums[s], axis=0)
        tiles += [whole[r * 8 : (r + 1) * 8] for r in range(36)]
    tiles += [jnp.zeros((8, 128), jnp.float32)] * (16 * SHARE - len(tiles))
    for part in range(16):
        chunk = jnp.concatenate(tiles[part * SHARE : (part + 1) * SHARE], axis=0)
        table_ref[part] = chunk.astype(jnp.bfloat16)


def close_kernel(parts_ref, close_ref, out_ref, wide_ref):
    for part in range(16):
        chunk = parts_ref[part].astype(jnp.float32)
        for k in range(SHARE):
            s, r = divmod(part * SHARE + k, 36)
            if s < 3:
                wide_ref[s, r * 8 : (r + 1) * 8] = chunk[k * 8 : (k + 1) * 8]
    rows = []
    for a in range(ROWS):
        lanes = [wide_ref[s, pl.ds(a, HEADS, stride=ROWS), :] for s in range(3)]
        rows.append(jnp.concatenate(lanes, axis=1))
    dense = dot(jnp.concatenate(rows, axis=0).astype(jnp.bfloat16), close_ref[...])
    for a in range(ROWS):
        for half in range(2):
            first = (a // 6 * 2 + half) * 828 + a % 6 * 138
            out_ref[0, :, first : first + 138] = dense[
                a * HEADS : (a + 1) * HEADS, half * 256 : half * 256 + 138
            ]


def grads_kernel(north_ref, south_ref, o_ref, p_ref, grads_ref):
    for group in range(PER):
        lanes = slice(group * 128, (group + 1) * 128)
        q_win = window(north_ref, south_ref, 0, group)
        k_win = window(north_ref, south_ref, 1, group)
        o_win, p_low = o_ref[group], p_ref[group]
        d_low = score_grad(p_low, o_win, window(north_ref, south_ref, 2, group))
        d_low = d_low.astype(jnp.bfloat16)
        q_all = dot(d_low, k_win)
        q_grad = jnp.zeros((TOK, 128), jnp.float32)
        for h in range(4):
            q_grad = jnp.where(head_mask(h), q_all[h * TOK : (h + 1) * TOK], q_grad)
        grads_ref[0, :, lanes] = (q_grad * score_factor).astype(jnp.bfloat16)

        q_turn = q_win.astype(jnp.float32).T.astype(jnp.bfloat16)
        o_turn = o_win.astype(jnp.float32).T.astype(jnp.bfloat16)
        k_parts, v_parts = [], []
        for h in range(4):
            rows = slice(h * 32, (h + 1) * 32)
            k_parts.append(dot(q_turn[rows], d_low[h * TOK : (h + 1) * TOK]))
            v_parts.append(dot(o_turn[rows], p_low[h * TOK : (h + 1) * TOK]))
        k_grad = jnp.concatenate(k_parts, axis=0).T
        v_grad = jnp.concatenate(v_parts, axis=0).T
        grads_ref[1, :, lanes] = (k_grad * score_factor).astype(jnp.bfloat16)
        grads_ref[2, :, lanes] = v_grad.astype(jnp.bfloat16)


def whole_spec(shape):
    return pl.BlockSpec(shape, lambda *_: (0,) * len(shape))


def north_spec(first, count):
    return pl.BlockSpec((count, 2, 3, PAD, PER * 128), lambda g: (first // count, 0, 1, 0, g))


def south_spec(first, count):
    return pl.BlockSpec((count, 2, 4, PAD, PER * 128), lambda g: (first // count, 0, 0, 0, g))


def group_spec(rows, columns):
    return pl.BlockSpec((PER, rows, columns), lambda g: (g, 0, 0))


params = pltpu.CompilerParams(vmem_limit_bytes=SMALL)
large = pltpu.CompilerParams(vmem_limit_bytes=LARGE)
smem = pl.BlockSpec(memory_space=pltpu.SMEM)
vmem = pl.BlockSpec(memory_space=pltpu.VMEM)


def pack_weight(lat, weight):
    return pl.pallas_call(
        pack_kernel,
        in_specs=[smem, vmem],
        out_specs=vmem,
        out_shape=jax.ShapeDtypeStruct((NZ, 24, 384), jnp.bfloat16),
        compiler_params=params,
        name="pack_weight",
    )(lat, weight)


def open_table(table, open_up):
    return pl.pallas_call(
        open_kernel,
        in_specs=[vmem, vmem],
        out_specs=vmem,
        out_shape=jax.ShapeDtypeStruct((GROUPS, 4 * ROWS, WIDE), jnp.float32),
        scratch_shapes=[pltpu.VMEM((3, ROWS * HEADS, 128), jnp.float32)],
        compiler_params=params,
        name="open_table",
    )(table, open_up)


def window_probs(across, south, table, spread, mask):
    return pl.pallas_call(
        probs_kernel,
        grid=(STEPS,),
        in_specs=[
            north_spec(0, 2),
            south_spec(0, 2),
            group_spec(4 * ROWS, WIDE),
            whole_spec((2, WIDE, TOK)),
            whole_spec((TOK, TOK)),
        ],
        out_specs=group_spec(4 * TOK, TOK),
        out_shape=jax.ShapeDtypeStruct((GROUPS, 4 * TOK, TOK), jnp.bfloat16),
        compiler_params=large,
        name="window_probs",
    )(across, south, table, spread, mask)


def merge_product(spots, near, far, weight, shuffle):
    return pl.pallas_call(
        merge_kernel,
        in_specs=[smem, vmem, vmem, vmem, vmem],
        out_specs=vmem,
        out_shape=jax.ShapeDtypeStruct((8, 64, 512), jnp.bfloat16),
        scratch_shapes=[pltpu.VMEM((384, 512), jnp.float32)],
        compiler_params=params,
        name="merge_product",
    )(spots, near, far, weight, shuffle)


def score_grads(recv, order, quarter, gain, back, sums, across, south, probs):
    return pl.pallas_call(
        scores_kernel,
        grid=(1,),
        in_specs=[
            whole_spec((8, 64, 512)),
            whole_spec((512, 384)),
            pl.BlockSpec((1, 2, 2, PAD, 768), lambda g: (3, 0, 1, 0, 0)),
            pl.BlockSpec((1, 2, 2, PAD, 768), lambda g: (3, 0, 2, 0, 0)),
            pl.BlockSpec((1, 2, 4, PAD, 768), lambda g: (3, 0, 0, 0, 0)),
            whole_spec((256, 256)),
            whole_spec((4, 1, 768)),
            whole_spec((TOK, 256)),
            whole_spec((2, TOK, WIDE)),
            pl.BlockSpec((1, 2, 3, PAD, 768), lambda g: (2, 0, 1, 0, 0)),
            pl.BlockSpec((1, 2, 4, PAD, 768), lambda g: (2, 0, 0, 0, 0)),
            pl.BlockSpec(memory_space=pl.ANY),
        ],
        out_specs=(
            whole_spec((GROUPS, TOK, 128)),
            whole_spec((16, 8 * SHARE, 128)),
        ),
        out_shape=(
            jax.ShapeDtypeStruct((GROUPS, TOK, 128), jnp.bfloat16),
            jax.ShapeDtypeStruct((16, 8 * SHARE, 128), jnp.bfloat16),
        ),
        scratch_shapes=[
            pltpu.VMEM((GROUPS, 4 * TOK, TOK), jnp.bfloat16),
            pltpu.SemaphoreType.DMA,
        ],
        compiler_params=large,
        name="score_grads",
    )(recv, order, across, across, south, quarter, gain, back, sums, across, south, probs)


def close_table(parts, close):
    return pl.pallas_call(
        close_kernel,
        in_specs=[vmem, vmem],
        out_specs=vmem,
        out_shape=jax.ShapeDtypeStruct((1, HEADS, 3312), jnp.float32),
        scratch_shapes=[pltpu.VMEM((3, ROWS * HEADS, 128), jnp.float32)],
        compiler_params=params,
        name="close_table",
    )(parts, close)


def window_grads(across, south, o_win, probs):
    return pl.pallas_call(
        grads_kernel,
        grid=(STEPS,),
        in_specs=[
            north_spec(0, 3),
            south_spec(0, 3),
            group_spec(TOK, 128),
            group_spec(4 * TOK, TOK),
        ],
        out_specs=pl.BlockSpec((3, TOK, PER * 128), lambda g: (0, 0, g)),
        out_shape=jax.ShapeDtypeStruct((3, TOK, 768), jnp.bfloat16),
        compiler_params=large,
        name="window_grads",
    )(across, south, o_win, probs)


def from_behind(shard, axis, by):
    size = lax.axis_size(axis)
    return lax.ppermute(shard, axis, [(i, (i + by) % size) for i in range(size)])


def partner(shard, axis, bit):
    return lax.ppermute(shard, axis, [(i, i ^ bit) for i in range(lax.axis_size(axis))])


def swap(shard, axis, groups):
    return lax.all_to_all(shard, axis, 0, 0, tiled=True, axis_index_groups=groups)


def share(shard, count, axis, groups):
    return swap(jnp.broadcast_to(shard[None], (count,) + shard.shape), axis, groups)


def on_device(y_block, merge_gain, merge_weight, d_merged, q_proj, k_proj, v_proj, bias_table):
    sums, spread, quarter, back, order, shuffle, open_up, close = layout_constants()
    lat = lax.axis_index("lat")

    packed = pack_weight(lat.reshape(1), merge_weight)

    tokens = jnp.arange(TOK, dtype=jnp.int32)
    upper = tokens // PAD % 6 >= 3
    allowed = jnp.logical_or(upper[:, None] == upper[None, :], lat != LAT - 1)
    allowed = jnp.logical_and(allowed, (tokens % PAD < 12)[None, :])
    mask = jnp.where(allowed, 0.0, LOW)

    packed, d_merged = lax.optimization_barrier((packed, d_merged))
    weight_z = swap(packed, "lon", z_groups).reshape(NZ * 24, 384)
    eastern_d = from_behind(d_merged[:, :, :3], "lon", -1)
    d_rows = jnp.concatenate(
        [d_merged[:, :, 3:], eastern_d, jnp.zeros_like(d_merged[:, :, :2])], axis=2
    ).reshape(48, -1)
    d_rows = jnp.concatenate([d_rows, partner(d_rows, "lat", 2)], axis=0)
    near = jnp.concatenate([d_rows, partner(d_rows, "lon", NY * NZ)], axis=0)
    far = partner(near, "lat", 1)
    me = (lax.axis_index("lon") // (NY * NZ)) * LAT + lat
    rel = jnp.bitwise_xor(jnp.arange(8, dtype=jnp.int32), me)
    spots = (rel % 2 * 4 + rel // 4 * 2 + rel // 2 % 2) * 48

    weight = share(weight_z, NY, "lon", y_groups)
    table = open_table(bias_table, open_up)

    eastern = from_behind(
        jnp.stack([q_proj[:, :, :6], k_proj[:, :, :6], v_proj[:, :, :6], y_block[:, :, :6]]),
        "lon",
        -1,
    )
    across = jnp.concatenate(
        [
            jnp.stack([q_proj[:, :, 6:], k_proj[:, :, 6:], v_proj[:, :, 6:], y_block[:, :, 6:]]),
            eastern,
            jnp.zeros_like(eastern[:, :, :, :4]),
        ],
        axis=3,
    )
    south = from_behind(across[:, :, :4], "lat", -1)

    weight, table, mask = lax.optimization_barrier((weight, table, mask))
    parts = merge_product(spots, near, far, weight, shuffle)
    recv = swap(parts, ("lon", "lat"), x_lat_groups)

    south, _ = lax.optimization_barrier((south, parts))
    probs = window_probs(across, south, table, spread, mask)

    gain = merge_gain.reshape(4, 1, 768)
    o_win, table_part = score_grads(
        recv, order, quarter, gain, back, sums, across, south, probs
    )

    table_part = swap(table_part, "lon", near_groups).astype(jnp.float32)
    table_part = jnp.sum(table_part, axis=0).astype(jnp.bfloat16)
    grads = window_grads(across, south, o_win, probs)
    grid = grads.reshape(3, 2, 6, PAD, 768)[:, :, :, :12]
    own, other = grid[:, :, :, :6], grid[:, :, :, 6:]
    table_part, own, other = lax.optimization_barrier((table_part, own, other))
    western = from_behind(other, "lon", 1)
    fixed = jnp.concatenate([western, own], axis=3)
    southern = from_behind(fixed[:, :, 3:], "lat", 1)

    table_part = share(table_part, NZ // 2, "lon", far_groups)
    table_part, southern = lax.optimization_barrier((table_part, southern))
    finished = jnp.concatenate([southern, fixed[:, :, :3]], axis=2)
    table_part = jnp.sum(table_part.astype(jnp.float32), axis=0).astype(jnp.bfloat16)
    table_grad = close_table(share(table_part, 16, "lon", near_groups), close)
    return (finished[0], finished[1], finished[2], table_grad)


def solution(mesh):
    placed = (
        P(None, "lat", "lon", None),
        P(),
        P("lon", None),
        P(None, "lat", "lon", None),
        P(None, "lat", "lon", None),
        P(None, "lat", "lon", None),
        P(None, "lat", "lon", None),
        P("lat", None, None),
    )
    return jax.shard_map(
        on_device,
        mesh=mesh,
        in_specs=placed,
        out_specs=(
            P(None, "lat", "lon", None),
            P(None, "lat", "lon", None),
            P(None, "lat", "lon", None),
            P("lat", None, None),
        ),
        check_vma=False,
    )
```

```python
import jax
import jax.numpy as jnp
import numpy as np
from jax import lax
from jax.experimental import pallas as pl
from jax.experimental.pallas import tpu as pltpu
from jax.sharding import PartitionSpec as P

NX, NY, NZ = 2, 4, 16
LAT = 4
HEADS = 24
ROWS = 12
PAD = 16
TOK = ROWS * PAD
SEG = 32
WIDE = ROWS * SEG
GROUPS = 6
PER = 3
STEPS = GROUPS // PER
SHARE = 7
LOW = -1e30
SMALL = 12 * 1024 * 1024
LARGE = 56 * 1024 * 1024
score_factor = 32 ** (-0.5)

z_groups = [[a * NZ + z for z in range(NZ)] for a in range(NX * NY)]
y_groups = [[(x * NY + y) * NZ + z for y in range(NY)] for x in range(NX) for z in range(NZ)]
near_groups = [
    [a * NZ + 2 * pair + e for a in range(NX * NY) for e in range(2)] for pair in range(NZ // 2)
]
far_groups = [
    [a * NZ + 2 * pair + e for pair in range(NZ // 2)] for a in range(NX * NY) for e in range(2)
]
x_lat_groups = [
    [(x * NY * NZ + b) * LAT + l for x in range(NX) for l in range(LAT)] for b in range(NY * NZ)
]


def layout_constants():
    tokens = np.arange(TOK)
    row, col = tokens // PAD, tokens % PAD
    real = col < 12
    sums = np.zeros((2, TOK, WIDE), np.float32)
    spread = np.zeros((2, WIDE, TOK), np.float32)
    for half in range(2):
        sums[half, tokens[real], (row * SEG + 11 - col + 8 * half)[real]] = 1
        spread[half, (row * SEG + 11 + col - 8 * half)[real], tokens[real]] = 1
    quarter = np.zeros((256, 256), np.float32)
    back = np.zeros((TOK, 256), np.float32)
    for level in range(2):
        for pr in range(4):
            for pc in range(6):
                for di in range(2):
                    for dj in range(2):
                        spot = (di + 2 * dj) * 64 + (level * 4 + pr) * 8 + pc
                        fine_row, fine_col = 2 * pr + di, 2 * pc + dj
                        quarter[spot, (level * 8 + fine_row) * PAD + fine_col] = 1
                        if 1 <= fine_row <= 6:
                            back[(level * 6 + fine_row - 1) * PAD + fine_col, spot] = 1
    shuffle = np.zeros((512, 384), np.float32)
    order = np.zeros((512, 384), np.float32)
    for l in range(4):
        for z in range(NZ):
            for i in range(6):
                shuffle[l * 128 + z * 6 + i, z * 24 + l * 6 + i] = 1
                order[l * 128 + z * 6 + i, z * 24 + l * 6 + i] = 1
    open_up = np.zeros((2, 138, WIDE), np.float32)
    for half in range(2):
        for r in range(6):
            for d in range(23):
                open_up[half, r * 23 + d, half * 192 + r * SEG + 22 - d] = 1
    close = np.zeros((WIDE, 512), np.float32)
    for b in range(ROWS):
        for d in range(23):
            close[b * SEG + d, b // 6 * 256 + b % 6 * 23 + d] = 1
    all_of = (sums, spread, quarter, back, order, shuffle, open_up, close)
    return [jnp.asarray(a, jnp.bfloat16) for a in all_of]


def dot(a, b, dims=((1,), (0,))):
    return lax.dot_general(a, b, (dims, ((), ())), preferred_element_type=jnp.float32)


def head_mask(h):
    lanes = lax.broadcasted_iota(jnp.int32, (1, 128), 1)
    return (lanes // 32) == h


def by_head(block):
    return jnp.concatenate(
        [jnp.where(head_mask(h), block, jnp.zeros_like(block)) for h in range(4)], axis=0
    )


def split_dot(values, matrix):
    high = values.astype(jnp.bfloat16)
    low = (values - high.astype(jnp.float32)).astype(jnp.bfloat16)
    return dot(high, matrix) + dot(low, matrix)


def window(north_ref, south_ref, which, group):
    lanes = slice(group * 128, (group + 1) * 128)
    pieces = []
    for level in range(2):
        pieces.append(north_ref[which, level, :, :, lanes].reshape(48, 128))
        pieces.append(south_ref[which, level, 0:3, :, lanes].reshape(48, 128))
    return jnp.concatenate(pieces, axis=0)


def pack_kernel(lat_ref, w_ref, out_ref):
    first = lat_ref[0] * 6
    to = lax.broadcasted_iota(jnp.int32, (24, 24), 0)
    source = lax.broadcasted_iota(jnp.int32, (24, 24), 1)
    total = jnp.zeros((24, 384), jnp.float32)
    for part in range(4):
        pick = jnp.logical_and(to // 6 == part, source == first + to - part * 6)
        pick = jnp.where(pick, 1.0, 0.0).astype(jnp.bfloat16)
        total += dot(pick, w_ref[:, part * 384 : (part + 1) * 384])
    packed = total.astype(jnp.bfloat16)
    for z in range(NZ):
        out_ref[z] = packed


def open_kernel(table_ref, open_ref, out_ref, wide_ref):
    halves = []
    for half in range(2):
        pieces = []
        for a in range(ROWS):
            first = (a // 6 * 2 + half) * 828 + a % 6 * 138
            pieces.append(table_ref[0, :, first : first + 138])
        halves.append(split_dot(jnp.concatenate(pieces, axis=0), open_ref[half]))
    whole = halves[0] + halves[1]
    for s in range(3):
        wide_ref[s] = whole[:, s * 128 : (s + 1) * 128]
    for head in range(HEADS):
        row = head % 4 * ROWS
        for s in range(3):
            out_ref[head // 4, row : row + ROWS, s * 128 : (s + 1) * 128] = wide_ref[
                s, pl.ds(head, ROWS, stride=HEADS), :
            ]


def probs_kernel(north_ref, south_ref, table_ref, spread_ref, mask_ref, p_ref):
    for group in range(PER):
        pieces = []
        for s in range(3):
            table = table_ref[group, :, s * 128 : (s + 1) * 128]
            table = jnp.broadcast_to(table[:, None, :], (4 * ROWS, 8, 128))
            pieces.append(pltpu.roll(table, 0, 2, stride=1, stride_axis=1))
        wide = jnp.concatenate(pieces, axis=2).reshape(2 * TOK, WIDE)
        q_win = window(north_ref, south_ref, 0, group)
        k_win = window(north_ref, south_ref, 1, group)
        scores = dot(by_head(q_win), k_win, ((1,), (1,))) * score_factor
        bias = [split_dot(wide, spread_ref[half]).reshape(-1, 1, 8, TOK) for half in range(2)]
        scores = scores + jnp.concatenate(bias, axis=1).reshape(4 * TOK, TOK)
        scores = (scores.reshape(4, TOK, TOK) + mask_ref[...][None]).reshape(4 * TOK, TOK)
        expon = jnp.exp(scores - jnp.max(scores, axis=-1, keepdims=True))
        probs = expon * (1.0 / jnp.sum(expon, axis=-1, keepdims=True))
        p_ref[group] = probs.astype(jnp.bfloat16)


def normalise(a_ref, b_ref, south_ref, quarter_ref):
    pieces = []
    for level in range(2):
        pieces.append(a_ref[0, level].reshape(32, 768))
        pieces.append(b_ref[0, level].reshape(32, 768))
        pieces.append(south_ref[0, level].reshape(64, 768))
    fields = dot(quarter_ref[...], jnp.concatenate(pieces, axis=0))
    parts = [fields[q * 64 : (q + 1) * 64] for q in range(4)]
    mean = jnp.sum(parts[0] + parts[1] + parts[2] + parts[3], axis=-1, keepdims=True) / 3072
    parts = [part - mean for part in parts]
    squares = [part * part for part in parts]
    variance = (
        jnp.sum(squares[0] + squares[1] + squares[2] + squares[3], axis=-1, keepdims=True) / 3072
    )
    inverse = lax.rsqrt(variance + 1e-05)
    return [part * inverse for part in parts], inverse


def merge_kernel(spot_ref, near_ref, far_ref, w_ref, shuffle_ref, out_ref, acc_ref):
    weights = [dot(shuffle_ref[...], w_ref[y]).astype(jnp.bfloat16) for y in range(NY)]
    near, far = None, None
    for part in range(4):
        rows, columns = slice(part * 128, part * 128 + 128), slice(part * 384, part * 384 + 384)
        weight = jnp.concatenate([weights[y][rows] for y in range(NY)], axis=0)
        near_part = dot(near_ref[:, columns], weight, ((1,), (1,)))
        far_part = dot(far_ref[:, columns], weight, ((1,), (1,)))
        near = near_part if part == 0 else near + near_part
        far = far_part if part == 0 else far + far_part
    acc_ref[:192] = near
    acc_ref[192:] = far
    for x in range(NX):
        for l in range(LAT):
            for level in range(2):
                own = pl.multiple_of(spot_ref[x * LAT + l] + level * 24 + 8, 8)
                below = pl.multiple_of(spot_ref[x * LAT + (l + 1) % LAT] + level * 24, 8)
                out_ref[x * LAT + l, level * 32 : level * 32 + 16] = acc_ref[
                    pl.ds(own, 16)
                ].astype(jnp.bfloat16)
                out_ref[x * LAT + l, level * 32 + 16 : level * 32 + 32] = acc_ref[
                    pl.ds(below, 16)
                ].astype(jnp.bfloat16)


def score_grad(probs, o_win, v_win):
    d_probs = dot(by_head(o_win), v_win, ((1,), (1,)))
    probs = probs.astype(jnp.float32)
    total = jnp.sum(probs, axis=-1, keepdims=True)
    delta = jnp.sum(probs * d_probs, axis=-1, keepdims=True) / total
    return probs * (d_probs - delta)


def scores_kernel(
    recv_ref,
    order_ref,
    y_a_ref,
    y_b_ref,
    y_south_ref,
    quarter_ref,
    gain_ref,
    back_ref,
    sums_ref,
    north_ref,
    south_ref,
    p_ref,
    o_out_ref,
    table_ref,
    p_buf,
    p_sem,
):
    copy = pltpu.make_async_copy(p_ref, p_buf, p_sem)
    copy.start()
    pieces = [
        jnp.concatenate(
            [recv_ref[x * LAT + l, :, y * 128 : (y + 1) * 128] for l in range(LAT)], axis=1
        )
        for x in range(NX)
        for y in range(NY)
    ]
    d_norm = dot(jnp.concatenate(pieces, axis=0), order_ref[...])
    hats = []
    for q in range(4):
        left = d_norm[(2 * q) * 64 : (2 * q + 1) * 64]
        right = d_norm[(2 * q + 1) * 64 : (2 * q + 2) * 64]
        hats.append(jnp.concatenate([left, right], axis=1) * gain_ref[q])
    mean = jnp.sum(hats[0] + hats[1] + hats[2] + hats[3], axis=-1, keepdims=True) / 3072
    normed, inverse = normalise(y_a_ref, y_b_ref, y_south_ref, quarter_ref)
    cross = [hats[q] * normed[q] for q in range(4)]
    along = jnp.sum(cross[0] + cross[1] + cross[2] + cross[3], axis=-1, keepdims=True) / 3072
    stack = [(hats[q] - mean - normed[q] * along) * inverse for q in range(4)]
    d_out = dot(back_ref[...], jnp.concatenate(stack, axis=0).astype(jnp.bfloat16))
    d_out = d_out.astype(jnp.bfloat16)

    copy.wait()
    sums = [[], [], []]
    for group in range(GROUPS):
        o_win = d_out[:, group * 128 : (group + 1) * 128]
        o_out_ref[group] = o_win
        d_scores = score_grad(p_buf[group], o_win, window(north_ref, south_ref, 0, group))
        halves = d_scores.reshape(4 * ROWS, 2, 8, TOK)
        spread = sum(
            dot(halves[:, half].reshape(2 * TOK, TOK).astype(jnp.bfloat16), sums_ref[half])
            for half in range(2)
        ).reshape(4 * ROWS, 8, WIDE)
        for s in range(3):
            part = spread[:, :, s * 128 : (s + 1) * 128]
            turned = pltpu.roll(part, 0, 2, stride=1, stride_axis=1)
            sums[s].append(jnp.sum(turned, axis=1))

    tiles = []
    for s in range(3):
        whole = jnp.concatenate(sums[s], axis=0)
        tiles += [whole[r * 8 : (r + 1) * 8] for r in range(36)]
    tiles += [jnp.zeros((8, 128), jnp.float32)] * (16 * SHARE - len(tiles))
    for part in range(16):
        chunk = jnp.concatenate(tiles[part * SHARE : (part + 1) * SHARE], axis=0)
        table_ref[part] = chunk.astype(jnp.bfloat16)


def close_kernel(parts_ref, close_ref, out_ref, wide_ref):
    for part in range(16):
        chunk = parts_ref[part].astype(jnp.float32)
        for k in range(SHARE):
            s, r = divmod(part * SHARE + k, 36)
            if s < 3:
                wide_ref[s, r * 8 : (r + 1) * 8] = chunk[k * 8 : (k + 1) * 8]
    rows = []
    for a in range(ROWS):
        lanes = [wide_ref[s, pl.ds(a, HEADS, stride=ROWS), :] for s in range(3)]
        rows.append(jnp.concatenate(lanes, axis=1))
    dense = dot(jnp.concatenate(rows, axis=0).astype(jnp.bfloat16), close_ref[...])
    for a in range(ROWS):
        for half in range(2):
            first = (a // 6 * 2 + half) * 828 + a % 6 * 138
            out_ref[0, :, first : first + 138] = dense[
                a * HEADS : (a + 1) * HEADS, half * 256 : half * 256 + 138
            ]


def grads_kernel(north_ref, south_ref, o_ref, p_ref, grads_ref):
    for group in range(PER):
        lanes = slice(group * 128, (group + 1) * 128)
        q_win = window(north_ref, south_ref, 0, group)
        k_win = window(north_ref, south_ref, 1, group)
        o_win, p_low = o_ref[group], p_ref[group]
        d_low = score_grad(p_low, o_win, window(north_ref, south_ref, 2, group))
        d_low = d_low.astype(jnp.bfloat16)
        q_all = dot(d_low, k_win)
        q_grad = jnp.zeros((TOK, 128), jnp.float32)
        for h in range(4):
            q_grad = jnp.where(head_mask(h), q_all[h * TOK : (h + 1) * TOK], q_grad)
        grads_ref[0, :, lanes] = (q_grad * score_factor).astype(jnp.bfloat16)

        q_turn = q_win.astype(jnp.float32).T.astype(jnp.bfloat16)
        o_turn = o_win.astype(jnp.float32).T.astype(jnp.bfloat16)
        k_parts, v_parts = [], []
        for h in range(4):
            rows = slice(h * 32, (h + 1) * 32)
            k_parts.append(dot(q_turn[rows], d_low[h * TOK : (h + 1) * TOK]))
            v_parts.append(dot(o_turn[rows], p_low[h * TOK : (h + 1) * TOK]))
        k_grad = jnp.concatenate(k_parts, axis=0).T
        v_grad = jnp.concatenate(v_parts, axis=0).T
        grads_ref[1, :, lanes] = (k_grad * score_factor).astype(jnp.bfloat16)
        grads_ref[2, :, lanes] = v_grad.astype(jnp.bfloat16)


def whole_spec(shape):
    return pl.BlockSpec(shape, lambda *_: (0,) * len(shape))


def north_spec(first, count):
    return pl.BlockSpec((count, 2, 3, PAD, PER * 128), lambda g: (first // count, 0, 1, 0, g))


def south_spec(first, count):
    return pl.BlockSpec((count, 2, 4, PAD, PER * 128), lambda g: (first // count, 0, 0, 0, g))


def group_spec(rows, columns):
    return pl.BlockSpec((PER, rows, columns), lambda g: (g, 0, 0))


params = pltpu.CompilerParams(vmem_limit_bytes=SMALL)
large = pltpu.CompilerParams(vmem_limit_bytes=LARGE)
smem = pl.BlockSpec(memory_space=pltpu.SMEM)
vmem = pl.BlockSpec(memory_space=pltpu.VMEM)


def pack_weight(lat, weight):
    return pl.pallas_call(
        pack_kernel,
        in_specs=[smem, vmem],
        out_specs=vmem,
        out_shape=jax.ShapeDtypeStruct((NZ, 24, 384), jnp.bfloat16),
        compiler_params=params,
        name="pack_weight",
    )(lat, weight)


def open_table(table, open_up):
    return pl.pallas_call(
        open_kernel,
        in_specs=[vmem, vmem],
        out_specs=vmem,
        out_shape=jax.ShapeDtypeStruct((GROUPS, 4 * ROWS, WIDE), jnp.float32),
        scratch_shapes=[pltpu.VMEM((3, ROWS * HEADS, 128), jnp.float32)],
        compiler_params=params,
        name="open_table",
    )(table, open_up)


def window_probs(across, south, table, spread, mask):
    return pl.pallas_call(
        probs_kernel,
        grid=(STEPS,),
        in_specs=[
            north_spec(0, 2),
            south_spec(0, 2),
            group_spec(4 * ROWS, WIDE),
            whole_spec((2, WIDE, TOK)),
            whole_spec((TOK, TOK)),
        ],
        out_specs=group_spec(4 * TOK, TOK),
        out_shape=jax.ShapeDtypeStruct((GROUPS, 4 * TOK, TOK), jnp.bfloat16),
        compiler_params=large,
        name="window_probs",
    )(across, south, table, spread, mask)


def merge_product(spots, near, far, weight, shuffle):
    return pl.pallas_call(
        merge_kernel,
        in_specs=[smem, vmem, vmem, vmem, vmem],
        out_specs=vmem,
        out_shape=jax.ShapeDtypeStruct((8, 64, 512), jnp.bfloat16),
        scratch_shapes=[pltpu.VMEM((384, 512), jnp.float32)],
        compiler_params=params,
        name="merge_product",
    )(spots, near, far, weight, shuffle)


def score_grads(recv, order, quarter, gain, back, sums, across, south, probs):
    return pl.pallas_call(
        scores_kernel,
        grid=(1,),
        in_specs=[
            whole_spec((8, 64, 512)),
            whole_spec((512, 384)),
            pl.BlockSpec((1, 2, 2, PAD, 768), lambda g: (3, 0, 1, 0, 0)),
            pl.BlockSpec((1, 2, 2, PAD, 768), lambda g: (3, 0, 2, 0, 0)),
            pl.BlockSpec((1, 2, 4, PAD, 768), lambda g: (3, 0, 0, 0, 0)),
            whole_spec((256, 256)),
            whole_spec((4, 1, 768)),
            whole_spec((TOK, 256)),
            whole_spec((2, TOK, WIDE)),
            pl.BlockSpec((1, 2, 3, PAD, 768), lambda g: (2, 0, 1, 0, 0)),
            pl.BlockSpec((1, 2, 4, PAD, 768), lambda g: (2, 0, 0, 0, 0)),
            pl.BlockSpec(memory_space=pl.ANY),
        ],
        out_specs=(
            whole_spec((GROUPS, TOK, 128)),
            whole_spec((16, 8 * SHARE, 128)),
        ),
        out_shape=(
            jax.ShapeDtypeStruct((GROUPS, TOK, 128), jnp.bfloat16),
            jax.ShapeDtypeStruct((16, 8 * SHARE, 128), jnp.bfloat16),
        ),
        scratch_shapes=[
            pltpu.VMEM((GROUPS, 4 * TOK, TOK), jnp.bfloat16),
            pltpu.SemaphoreType.DMA,
        ],
        compiler_params=large,
        name="score_grads",
    )(recv, order, across, across, south, quarter, gain, back, sums, across, south, probs)


def close_table(parts, close):
    return pl.pallas_call(
        close_kernel,
        in_specs=[vmem, vmem],
        out_specs=vmem,
        out_shape=jax.ShapeDtypeStruct((1, HEADS, 3312), jnp.float32),
        scratch_shapes=[pltpu.VMEM((3, ROWS * HEADS, 128), jnp.float32)],
        compiler_params=params,
        name="close_table",
    )(parts, close)


def window_grads(across, south, o_win, probs):
    return pl.pallas_call(
        grads_kernel,
        grid=(STEPS,),
        in_specs=[
            north_spec(0, 3),
            south_spec(0, 3),
            group_spec(TOK, 128),
            group_spec(4 * TOK, TOK),
        ],
        out_specs=pl.BlockSpec((3, TOK, PER * 128), lambda g: (0, 0, g)),
        out_shape=jax.ShapeDtypeStruct((3, TOK, 768), jnp.bfloat16),
        compiler_params=large,
        name="window_grads",
    )(across, south, o_win, probs)


def from_behind(shard, axis, by):
    size = lax.axis_size(axis)
    return lax.ppermute(shard, axis, [(i, (i + by) % size) for i in range(size)])


def partner(shard, axis, bit):
    return lax.ppermute(shard, axis, [(i, i ^ bit) for i in range(lax.axis_size(axis))])


def swap(shard, axis, groups):
    return lax.all_to_all(shard, axis, 0, 0, tiled=True, axis_index_groups=groups)


def share(shard, count, axis, groups):
    return swap(jnp.broadcast_to(shard[None], (count,) + shard.shape), axis, groups)


def on_device(y_block, merge_gain, merge_weight, d_merged, q_proj, k_proj, v_proj, bias_table):
    sums, spread, quarter, back, order, shuffle, open_up, close = layout_constants()
    lat = lax.axis_index("lat")

    packed = pack_weight(lat.reshape(1), merge_weight)

    tokens = jnp.arange(TOK, dtype=jnp.int32)
    upper = tokens // PAD % 6 >= 3
    allowed = jnp.logical_or(upper[:, None] == upper[None, :], lat != LAT - 1)
    allowed = jnp.logical_and(allowed, (tokens % PAD < 12)[None, :])
    mask = jnp.where(allowed, 0.0, LOW)

    packed, d_merged = lax.optimization_barrier((packed, d_merged))
    weight_z = swap(packed, "lon", z_groups).reshape(NZ * 24, 384)
    eastern_d = from_behind(d_merged[:, :, :3], "lon", -1)
    d_rows = jnp.concatenate(
        [d_merged[:, :, 3:], eastern_d, jnp.zeros_like(d_merged[:, :, :2])], axis=2
    ).reshape(48, -1)
    d_rows = jnp.concatenate([d_rows, partner(d_rows, "lat", 2)], axis=0)
    near = jnp.concatenate([d_rows, partner(d_rows, "lon", NY * NZ)], axis=0)
    far = partner(near, "lat", 1)
    me = (lax.axis_index("lon") // (NY * NZ)) * LAT + lat
    rel = jnp.bitwise_xor(jnp.arange(8, dtype=jnp.int32), me)
    spots = (rel % 2 * 4 + rel // 4 * 2 + rel // 2 % 2) * 48

    weight = share(weight_z, NY, "lon", y_groups)
    table = open_table(bias_table, open_up)

    eastern = from_behind(
        jnp.stack([q_proj[:, :, :6], k_proj[:, :, :6], v_proj[:, :, :6], y_block[:, :, :6]]),
        "lon",
        -1,
    )
    across = jnp.concatenate(
        [
            jnp.stack([q_proj[:, :, 6:], k_proj[:, :, 6:], v_proj[:, :, 6:], y_block[:, :, 6:]]),
            eastern,
            jnp.zeros_like(eastern[:, :, :, :4]),
        ],
        axis=3,
    )
    south = from_behind(across[:, :, :4], "lat", -1)

    weight, table, mask = lax.optimization_barrier((weight, table, mask))
    parts = merge_product(spots, near, far, weight, shuffle)
    recv = swap(parts, ("lon", "lat"), x_lat_groups)

    south, _ = lax.optimization_barrier((south, parts))
    probs = window_probs(across, south, table, spread, mask)

    gain = merge_gain.reshape(4, 1, 768)
    o_win, table_part = score_grads(
        recv, order, quarter, gain, back, sums, across, south, probs
    )

    table_part = swap(table_part, "lon", near_groups).astype(jnp.float32)
    table_part = jnp.sum(table_part, axis=0).astype(jnp.bfloat16)
    grads = window_grads(across, south, o_win, probs)
    grid = grads.reshape(3, 2, 6, PAD, 768)[:, :, :, :12]
    own, other = grid[:, :, :, :6], grid[:, :, :, 6:]
    table_part, other = lax.optimization_barrier((table_part, other))
    western = from_behind(other, "lon", 1)
    fixed = jnp.concatenate([western, own], axis=3)
    southern = from_behind(fixed[:, :, 3:], "lat", 1)

    table_part = share(table_part, NZ // 2, "lon", far_groups)
    table_part, southern = lax.optimization_barrier((table_part, southern))
    finished = jnp.concatenate([southern, fixed[:, :, :3]], axis=2)
    table_part = jnp.sum(table_part.astype(jnp.float32), axis=0).astype(jnp.bfloat16)
    table_grad = close_table(share(table_part, 16, "lon", near_groups), close)
    return (finished[0], finished[1], finished[2], table_grad)


def solution(mesh):
    placed = (
        P(None, "lat", "lon", None),
        P(),
        P("lon", None),
        P(None, "lat", "lon", None),
        P(None, "lat", "lon", None),
        P(None, "lat", "lon", None),
        P(None, "lat", "lon", None),
        P("lat", None, None),
    )
    return jax.shard_map(
        on_device,
        mesh=mesh,
        in_specs=placed,
        out_specs=(
            P(None, "lat", "lon", None),
            P(None, "lat", "lon", None),
            P(None, "lat", "lon", None),
            P("lat", None, None),
        ),
        check_vma=False,
    )
```
